512 devices in a mesh: wall: 16 (over y, x_lo, core), stream: 32 (over z, x_hi).
Axes of the slice: x: 4 (x_hi: 2, x_lo: 2; x = x_hi * 2 + x_lo), y: 4, z: 16, core: 2. Of those that a mesh axis runs over, the one named last changes fastest.
Arguments:
- concentration: float32 [2, 256, 128, 512], P(None, 'stream', 'wall'), may hold values from 0.2 to 2
- velocity: float32 [3, 256, 128, 512], P(None, 'stream', 'wall'), may hold values from -5 to 5
- potential: float32 [256, 128, 512], P('stream', 'wall'), may hold values from -6 to 6
Outputs:
- updated: float32 [2, 256, 128, 512], P(None, 'stream', 'wall')
The draws below stay inside these ranges and needn't reach their ends.
All inputs are finite; a program needn't handle non-finite values.
Results may differ from the reference program's by a relative error of at most 0.0003.
Values sent between devices are 32-bit elements; how exact they have to be, the bound alone decides.
No kernel may reach another device: no remote copies, remote signals or barrier semaphores. Data moves between devices by JAX's collectives and lax.ppermute only.
A program may use at most 64 MiB of HBM per device.

```python
import jax
import jax.numpy as jnp
from jax import lax

CX = 8
CZ = 8
SY = 512
NX = 256
NZ = 128


def block_levels(rng, dims, shards, smallest, largest):
    loudness = 1.0
    for position, parts in shards:
        draws = jax.random.uniform(jax.random.fold_in(jax.random.fold_in(rng, 6), position), (parts,), jnp.float32, smallest / len(shards), largest / len(shards))
        loudness = loudness * jnp.repeat(jnp.exp(draws), dims[position] // parts).reshape((-1,) + (1,) * (len(dims) - 1 - position))
    return loudness


def noise(key, shape, deviation, reach, pieces=(), kind=jnp.bfloat16):
    gain = block_levels(key, shape, pieces, -0.22, 0.18) if pieces else 1.0
    result = jax.random.normal(key, shape, jnp.float32) * deviation * gain
    return jnp.minimum(jnp.maximum(result, -reach), reach).astype(kind)


def setup_inputs(seed: int = 0) -> dict:
    seeds = jax.random.split(jax.random.key(seed), 4)
    return {
        "concentration": jnp.clip(0.2 + 1.8 * jax.random.uniform(seeds[0], (2, NX, NZ, SY), jnp.float32) ** block_levels(seeds[0], (2, NX, NZ, SY), ((1, 32), (2, 16)), -0.2, 0.2), 0.2, 2.0),
        "velocity": noise(seeds[1], (3, NX, NZ, SY), 1.0, 5.0, ((1, 32), (2, 16)), jnp.float32),
        "potential": noise(seeds[2], (NX, NZ, SY), 1.0, 6.0, ((0, 32), (1, 16)), jnp.float32),
    }


ADVECT_STEP = 0.2
DRIFT_RATES = (1.0, -0.5)

def pad_axis(values_in, dimension, periodic):
    extent = values_in.shape[dimension]
    if periodic:
        below_pad = lax.slice_in_dim(values_in, extent - 1, extent, axis=dimension)
        above_pad = lax.slice_in_dim(values_in, 0, 1, axis=dimension)
    else:
        below_pad = jnp.zeros_like(lax.slice_in_dim(values_in, 0, 1, axis=dimension))
        above_pad = below_pad
    return jnp.concatenate([below_pad, values_in, above_pad], axis=dimension)

def face_divergence(conc_pad, speed_pad, volt_pad, dimension):
    face_count = speed_pad.shape[dimension] - 1
    face_speed = 0.5 * (lax.slice_in_dim(speed_pad, 0, face_count, axis=dimension) + lax.slice_in_dim(speed_pad, 1, face_count + 1, axis=dimension))
    voltage_step = lax.slice_in_dim(volt_pad, 1, face_count + 1, axis=dimension) - lax.slice_in_dim(volt_pad, 0, face_count, axis=dimension)
    drift_rate = jnp.array(DRIFT_RATES, jnp.float32).reshape((2,) + (1,) * face_speed.ndim)
    mean_conc = 0.5 * (lax.slice_in_dim(conc_pad, 0, face_count, axis=dimension + 1) + lax.slice_in_dim(conc_pad, 1, face_count + 1, axis=dimension + 1))
    face_flux = mean_conc * (face_speed[None] - drift_rate * voltage_step[None])
    return lax.slice_in_dim(face_flux, 1, face_count, axis=dimension + 1) - lax.slice_in_dim(face_flux, 0, face_count - 1, axis=dimension + 1)

def line_solve(values_in, dimension, rate, periodic):
    shifted = jnp.moveaxis(values_in, dimension, 0)
    line_length = shifted.shape[0]
    columns = shifted.reshape(line_length, -1)
    centre_value = 1.0 + 2.0 * rate
    filled = jnp.ones((line_length,), values_in.dtype)
    below_diag = (-rate * filled).at[0].set(0.0)
    above_diag = (-rate * filled).at[line_length - 1].set(0.0)
    if periodic:
        middle = (centre_value * filled).at[0].set(2.0 * centre_value)
        middle = middle.at[line_length - 1].set(centre_value + rate * rate / centre_value)
        primary = lax.linalg.tridiagonal_solve(below_diag, middle, above_diag, columns)
        correction_in = jnp.zeros((line_length, 1), values_in.dtype)
        correction_in = correction_in.at[0, 0].set(-centre_value).at[line_length - 1, 0].set(-rate)
        response = lax.linalg.tridiagonal_solve(below_diag, middle, above_diag, correction_in)
        dot_base = primary[0] + rate / centre_value * primary[line_length - 1]
        dot_corr = response[0, 0] + rate / centre_value * response[line_length - 1, 0]
        solved = primary - (dot_base / (1.0 + dot_corr))[None, :] * response
    else:
        solved = lax.linalg.tridiagonal_solve(below_diag, centre_value * filled, above_diag, columns)
    return jnp.moveaxis(solved.reshape(shifted.shape), 0, dimension)

def reference(concentration, velocity, potential):
    divergence = face_divergence(pad_axis(concentration, 1, True), pad_axis(velocity[0], 0, True), pad_axis(potential, 0, True), 0)
    divergence = divergence + face_divergence(pad_axis(concentration, 2, False), pad_axis(velocity[1], 1, False), pad_axis(potential, 1, False), 1)
    divergence = divergence + face_divergence(pad_axis(concentration, 3, True), pad_axis(velocity[2], 2, True), pad_axis(potential, 2, True), 2)
    predicted = concentration - ADVECT_STEP * divergence
    rates_stream = (4.0 * CX * CX, float(NX * NX // 25))
    rates_wall = (4.0 * CZ * CZ, float(NZ * NZ // 16))
    results = []
    for species in range(2):
        streamwise = line_solve(predicted[species], 0, rates_stream[species], True)
        results.append(line_solve(streamwise, 1, rates_wall[species], False))
    return jnp.stack(results)
```

```python
import functools

import jax
import jax.numpy as jnp
import numpy as np
from jax import lax
from jax.experimental import pallas as pl
from jax.experimental.pallas import tpu as pltpu
from jax.sharding import PartitionSpec as P

ADVECT_STEP = 0.2
DRIFT_RATES = (1.0, -0.5)
FLUX_SCALE = 0.25 * ADVECT_STEP
HIGHEST = lax.Precision.HIGHEST


def line_factors(rate):
    base = 1.0 + 2.0 * rate
    root = np.sqrt(1.0 + 4.0 * rate)
    return 2.0 * rate / (base + root), 1.0 / root


def cyclic_links(rate, width, blocks):
    decay, _ = line_factors(rate)
    step = decay**width
    table = np.zeros((blocks, 2, blocks, 2))
    for block in range(blocks):
        for other in range(blocks):
            table[block, 0, other, 0] = step ** ((block - 1 - other) % blocks)
            table[block, 1, other, 1] = step ** ((other - block - 1) % blocks)
    return table.reshape(2 * blocks, 2 * blocks) / (1.0 - step**blocks)


def bounded_links(rate, width, blocks):
    decay, _ = line_factors(rate)
    step = decay**width
    length = width * blocks
    table = np.zeros((blocks, 2, blocks, 2))
    below_wall = np.zeros((blocks, 2))
    above_wall = np.zeros((blocks, 2))
    for block in range(blocks):
        below_wall[block, 1] = decay ** (width * block + 1)
        above_wall[block, 0] = decay ** (length - width * block - width + 1)
    mirror = decay ** (length + 1)
    below_weight = -(below_wall - mirror * above_wall) / (1.0 - mirror**2)
    above_weight = -(above_wall - mirror * below_wall) / (1.0 - mirror**2)
    for block in range(blocks):
        for other in range(blocks):
            if other < block:
                table[block, 0, other, 0] = step ** (block - 1 - other)
            if other > block:
                table[block, 1, other, 1] = step ** (other - block - 1)
        table[block, 0] += decay ** (width * block) * below_weight
        table[block, 1] += decay ** (length - width * (block + 1)) * above_weight
    return table.reshape(2 * blocks, 2 * blocks)


def whole(memory=pltpu.VMEM):
    return pl.BlockSpec(memory_space=memory)


def call(kernel, outs, ins, scratch=()):
    return pl.pallas_call(
        kernel,
        out_shape=[jax.ShapeDtypeStruct(shape, jnp.float32) for shape in outs],
        in_specs=[whole()] * len(ins),
        out_specs=[whole()] * len(outs),
        scratch_shapes=list(scratch),
        compiler_params=pltpu.CompilerParams(vmem_limit_bytes=32 * 1024 * 1024),
    )(*ins)


def edge_kernel(conc, vel, volt, low_out, high_out, right_out):
    width = conc.shape[1]
    depth = conc.shape[2]
    for item in range(4):
        if item < 2:
            right_out[item] = conc[item, width - 1]
        elif item == 2:
            right_out[item] = vel[0, width - 1]
        else:
            right_out[item] = volt[width - 1]
        for x in range(width):
            if item < 2:
                layer = conc.at[item, x]
            elif item == 2:
                layer = vel.at[1, x]
            else:
                layer = volt.at[x]
            low_out[item, x : x + 1] = layer[0:1]
            high_out[item, x : x + 1] = layer[depth - 1 : depth]


def face(conc_low, conc_high, speed_low, speed_high, volt_low, volt_high, species):
    drift = speed_low + speed_high - (2.0 * DRIFT_RATES[species]) * (volt_high - volt_low)
    return (conc_low + conc_high) * drift


def predict_kernel(
    decays, conc, vel, volt, low_edge, high_edge, left_halo, below_halo, above_halo, pred, spill, ends
):
    width, depth, span = volt.shape
    row = lax.broadcasted_iota(jnp.int32, (depth, span), 0)
    bottom = [
        face(below_halo[s], low_edge[s], below_halo[2], low_edge[2], below_halo[3], low_edge[3], s)
        for s in range(2)
    ]
    top = [
        face(high_edge[s], above_halo[s], high_edge[2], above_halo[2], high_edge[3], above_halo[3], s)
        for s in range(2)
    ]
    half = span // 2
    left = [face(left_halo[s], conc[s, 0], left_halo[2], vel[0, 0], left_halo[3], volt[0], s) for s in range(2)]
    running = []
    for s in range(2):
        moved = -FLUX_SCALE * left[s]
        spill[s] = moved
        running.append(moved)
    for x in range(width):
        here = volt[x]
        volt_up = pltpu.roll(here, depth - 1, 0)
        volt_next = pltpu.roll(here, span - 1, 1)
        speed_up = pltpu.roll(vel[1, x], depth - 1, 0)
        speed_next = pltpu.roll(vel[2, x], span - 1, 1)
        for s in range(2):
            value = conc[s, x]
            wall = face(value, pltpu.roll(value, depth - 1, 0), vel[1, x], speed_up, here, volt_up, s)
            wall_low = jnp.where(row == 0, bottom[s][x : x + 1], pltpu.roll(wall, 1, 0))
            wall_high = jnp.where(row == depth - 1, top[s][x : x + 1], wall)
            side = face(value, pltpu.roll(value, span - 1, 1), vel[2, x], speed_next, here, volt_next, s)
            total = (wall_high - wall_low) + (side - pltpu.roll(side, 1, 1)) - left[s]
            if x + 1 < width:
                right = face(value, conc[s, x + 1], vel[0, x], vel[0, x + 1], here, volt[x + 1], s)
                total = total + right
                left[s] = right
            result = value - FLUX_SCALE * total
            pred[s, x] = result
            running[s] = result + decays[s] * running[s]
    for s in range(2):
        behind = pred[s, width - 1]
        for x in range(width - 2, -1, -1):
            behind = pred[s, x] + decays[s] * behind
        behind = behind + (1.0 / decays[s]) * spill[s]
        for z in range(depth):
            for part in range(2):
                peer = (s * depth + z) * 2 + part
                cut = slice(part * half, (part + 1) * half)
                ends[peer, 0:1] = running[s][z : z + 1, cut]
                ends[peer, 1:2] = behind[z : z + 1, cut]


def link_kernel(axis, share, ends, table, links, flat):
    blocks = ends.shape[0]
    for block in range(blocks):
        flat[2 * block : 2 * block + 2] = ends[block]
    species = lax.div(lax.axis_index(axis), share)
    solved = jnp.dot(table[species], flat[...], precision=HIGHEST, preferred_element_type=jnp.float32)
    for block in range(blocks):
        links[block] = solved[2 * block : 2 * block + 2]


def stream_kernel(decays, gains, wall_decays, wall_gains, pred, spill, links, base, ends, carry):
    _, width, depth, span = pred.shape
    half = span // 2
    for s in range(2):
        for z in range(depth):
            for part in range(2):
                peer = (s * depth + z) * 2 + part
                cut = slice(part * half, (part + 1) * half)
                carry[0, s, z : z + 1, cut] = links[peer, 0:1]
                carry[1, s, z : z + 1, cut] = links[peer, 1:2]
    row = lax.broadcasted_iota(jnp.int32, (depth, span), 0)
    for s in range(2):
        behind = carry[1, s]
        for x in range(width - 1, -1, -1):
            base[s, x] = decays[s] * behind
            behind = pred[s, x] + decays[s] * behind
        running = carry[0, s] + spill[s]
        for x in range(width):
            running = pred[s, x] + decays[s] * running
            value = (gains[s] * wall_gains[s]) * (running + base[s, x])
            forward = value
            back = value
            step = 1
            while step < depth:
                scale = wall_decays[s] ** step
                forward = forward + jnp.where(row >= step, scale * pltpu.roll(forward, step, 0), 0.0)
                back = back + jnp.where(row < depth - step, scale * pltpu.roll(back, depth - step, 0), 0.0)
                step *= 2
            base[s, x] = forward + back - value
            ends[s * width + x, 0:1] = forward[depth - 1 : depth]
            ends[s * width + x, 1:2] = back[0:1]


def wall_kernel(wall_decays, base, links, out):
    _, width, depth, span = base.shape
    row = lax.broadcasted_iota(jnp.int32, (depth, span), 0)
    for s in range(2):
        from_below = jnp.zeros((depth, span), jnp.float32)
        from_above = jnp.zeros((depth, span), jnp.float32)
        for z in range(depth):
            from_below = jnp.where(row == z, wall_decays[s] ** (z + 1), from_below)
            from_above = jnp.where(row == z, wall_decays[s] ** (depth - z), from_above)
        for x in range(width):
            peer = s * width + x
            out[s, x] = base[s, x] + from_below * links[peer, 0:1] + from_above * links[peer, 1:2]


def exchange(values, axis):
    return lax.all_to_all(values, axis, split_axis=0, concat_axis=0, tiled=True)


def per_device(concentration, velocity, potential):
    _, width, depth, span = concentration.shape
    stream = lax.axis_size("stream")
    wall = lax.axis_size("wall")
    stream_total = width * stream
    wall_total = depth * wall
    rates_x = (4.0 * width * width, float(stream_total * stream_total // 25))
    rates_z = (4.0 * depth * depth, float(wall_total * wall_total // 16))
    decays_x, gains_x = zip(*[tuple(float(v) for v in line_factors(rate)) for rate in rates_x])
    decays_z, gains_z = zip(*[tuple(float(v) for v in line_factors(rate)) for rate in rates_z])
    links_x = jnp.array(np.stack([cyclic_links(rate, width, stream) for rate in rates_x]), jnp.float32)
    links_z = jnp.array(np.stack([bounded_links(rate, depth, wall) for rate in rates_z]), jnp.float32)

    edges = (4, width, span)
    low_edge, high_edge, right_edge = call(
        edge_kernel, [edges, edges, (4, depth, span)], (concentration, velocity, potential)
    )
    ring = [(i, (i + 1) % stream) for i in range(stream)]
    rising = [(i, i + 1) for i in range(wall - 1)]
    falling = [(i + 1, i) for i in range(wall - 1)]
    left_halo = lax.ppermute(right_edge, "stream", ring)
    below_halo = lax.ppermute(high_edge, "wall", rising)
    above_halo = lax.ppermute(low_edge, "wall", falling)
    half = span // 2
    pred, spill, ends = call(
        functools.partial(predict_kernel, decays_x),
        [concentration.shape, (2, depth, span), (stream, 2, half)],
        (concentration, velocity, potential, low_edge, high_edge, left_halo, below_halo, above_halo),
    )
    ends = exchange(ends, "stream")
    (links,) = call(
        functools.partial(link_kernel, "stream", 2 * depth),
        [ends.shape],
        (ends, links_x),
        [pltpu.VMEM((2 * stream, half), jnp.float32)],
    )
    links = exchange(links, "stream")
    base, ends = call(
        functools.partial(stream_kernel, decays_x, gains_x, decays_z, gains_z),
        [concentration.shape, (wall, 2, span)],
        (pred, spill, links),
        [pltpu.VMEM((2, 2, depth, span), jnp.float32)],
    )
    ends = exchange(ends, "wall")
    (links,) = call(
        functools.partial(link_kernel, "wall", width),
        [ends.shape],
        (ends, links_z),
        [pltpu.VMEM((2 * wall, span), jnp.float32)],
    )
    links = exchange(links, "wall")
    (out,) = call(functools.partial(wall_kernel, decays_z), [concentration.shape], (base, links))
    return out


def solution(mesh):
    return jax.shard_map(
        per_device,
        mesh=mesh,
        in_specs=(
            P(None, "stream", "wall", None),
            P(None, "stream", "wall", None),
            P("stream", "wall", None),
        ),
        out_specs=P(None, "stream", "wall", None),
        check_vma=False,
    )
```

```python
import functools

import jax
import jax.numpy as jnp
import numpy as np
from jax import lax
from jax.experimental import pallas as pl
from jax.experimental.pallas import tpu as pltpu
from jax.sharding import PartitionSpec as P

ADVECT_STEP = 0.2
DRIFT_RATES = (1.0, -0.5)
FLUX_SCALE = 0.25 * ADVECT_STEP
TEAM = 4
HALVES = 2


def line_factors(rate):
    base = 1.0 + 2.0 * rate
    root = np.sqrt(1.0 + 4.0 * rate)
    return float(2.0 * rate / (base + root)), float(1.0 / root)


def pick(index, values):
    chosen = jnp.float32(values[0])
    for place, value in enumerate(values):
        if place:
            chosen = jnp.where(index == place, jnp.float32(value), chosen)
    return chosen


def whole(memory=pltpu.VMEM):
    return pl.BlockSpec(memory_space=memory)


def call(kernel, outs, ins, scratch=(), source=pltpu.VMEM, room=32):
    return pl.pallas_call(
        kernel,
        out_shape=[jax.ShapeDtypeStruct(shape, jnp.float32) for shape in outs],
        in_specs=[whole(source)] * len(ins),
        out_specs=[whole()] * len(outs),
        scratch_shapes=list(scratch),
        compiler_params=pltpu.CompilerParams(vmem_limit_bytes=room * 1024 * 1024),
    )(*ins)


def edge_kernel(conc_in, vel_in, volt_in, low_out, high_out, right_out, conc, speed, volt, arrived):
    width, depth, _ = volt.shape
    copies = [
        pltpu.make_async_copy(source, target, arrived.at[place])
        for place, (source, target) in enumerate(
            (
                (conc_in, conc),
                (vel_in.at[1], speed),
                (volt_in, volt),
                (vel_in.at[0, width - 1], right_out.at[2]),
            )
        )
    ]
    for copy in copies:
        copy.start()
    for copy in copies:
        copy.wait()
    for item, layers in enumerate((conc.at[0], conc.at[1], speed, volt)):
        if item != 2:
            right_out[item] = layers[width - 1]
        for x in range(width):
            low_out[item, x : x + 1] = layers[x, 0:1]
            high_out[item, x : x + 1] = layers[x, depth - 1 : depth]


def face(conc_low, conc_high, speed_low, speed_high, volt_low, volt_high, species):
    drift = speed_low + speed_high - (2.0 * DRIFT_RATES[species]) * (volt_high - volt_low)
    return (conc_low + conc_high) * drift


def predict_kernel(
    decays, conc, vel, volt, low_edge, high_edge, left_halo, below_halo, above_halo, pred, spill, ends
):
    width, depth, span = volt.shape
    row = lax.broadcasted_iota(jnp.int32, (depth, span), 0)
    bottom = [
        face(below_halo[s], low_edge[s], below_halo[2], low_edge[2], below_halo[3], low_edge[3], s)
        for s in range(2)
    ]
    top = [
        face(high_edge[s], above_halo[s], high_edge[2], above_halo[2], high_edge[3], above_halo[3], s)
        for s in range(2)
    ]
    half = span // HALVES
    left = [face(left_halo[s], conc[s, 0], left_halo[2], vel[0, 0], left_halo[3], volt[0], s) for s in range(2)]
    running = []
    for s in range(2):
        moved = -FLUX_SCALE * left[s]
        spill[s] = moved
        running.append(moved)
    for x in range(width):
        here = volt[x]
        volt_up = pltpu.roll(here, depth - 1, 0)
        volt_next = pltpu.roll(here, span - 1, 1)
        speed_up = pltpu.roll(vel[1, x], depth - 1, 0)
        speed_next = pltpu.roll(vel[2, x], span - 1, 1)
        for s in range(2):
            value = conc[s, x]
            wall = face(value, pltpu.roll(value, depth - 1, 0), vel[1, x], speed_up, here, volt_up, s)
            wall_low = jnp.where(row == 0, bottom[s][x : x + 1], pltpu.roll(wall, 1, 0))
            wall_high = jnp.where(row == depth - 1, top[s][x : x + 1], wall)
            side = face(value, pltpu.roll(value, span - 1, 1), vel[2, x], speed_next, here, volt_next, s)
            total = (wall_high - wall_low) + (side - pltpu.roll(side, 1, 1)) - left[s]
            if x + 1 < width:
                right = face(value, conc[s, x + 1], vel[0, x], vel[0, x + 1], here, volt[x + 1], s)
                total = total + right
                left[s] = right
            result = value - FLUX_SCALE * total
            pred[s, x] = result
            running[s] = result + decays[s] * running[s]
    for s in range(2):
        behind = pred[s, width - 1]
        for x in range(width - 2, -1, -1):
            behind = pred[s, x] + decays[s] * behind
        behind = behind + (1.0 / decays[s]) * spill[s]
        for part in range(HALVES):
            cut = slice(part * half, (part + 1) * half)
            ends[s * HALVES + part, 0] = running[s][:, cut]
            ends[s * HALVES + part, 1] = behind[:, cut]


def decayed(parts, step):
    total = parts[0]
    for part in parts[1:]:
        total = step * total + part
    return total


def stream_sum_kernel(steps, ends, sums):
    step = pick(lax.div(lax.rem(lax.axis_index("stream"), TEAM), HALVES), steps)
    before = decayed([ends[m, 0] for m in range(TEAM)], step)
    after = decayed([ends[m, 1] for m in range(TEAM - 1, -1, -1)], step)
    for team in range(sums.shape[0]):
        sums[team, 0] = before
        sums[team, 1] = after


def stream_link_kernel(steps, ends, sums, links):
    position = lax.axis_index("stream")
    species = lax.div(lax.rem(position, TEAM), HALVES)
    team = lax.div(position, TEAM)
    teams = sums.shape[0]
    step = pick(species, steps)
    leap = pick(species, [value**TEAM for value in steps])
    closing = pick(species, [1.0 / (1.0 - value ** (TEAM * teams)) for value in steps])
    before = decayed([sums[lax.rem(team + k, teams), 0] for k in range(teams)], leap) * closing
    after = decayed([sums[lax.rem(team + teams - k, teams), 1] for k in range(teams)], leap) * closing
    for m in range(TEAM):
        links[m, 0] = before
        before = step * before + ends[m, 0]
    for m in range(TEAM - 1, -1, -1):
        links[m, 1] = after
        after = step * after + ends[m, 1]


def stream_kernel(decays, gains, wall_decays, wall_gains, pred, spill, links, base, ends):
    _, width, depth, span = pred.shape
    row = lax.broadcasted_iota(jnp.int32, (depth, span), 0)
    for s in range(2):
        entering = [
            jnp.concatenate([links[s * HALVES + part, side] for part in range(HALVES)], axis=1) for side in range(2)
        ]
        behind = entering[1]
        for x in range(width - 1, -1, -1):
            base[s, x] = decays[s] * behind
            behind = pred[s, x] + decays[s] * behind
        running = entering[0] + spill[s]
        for x in range(width):
            running = pred[s, x] + decays[s] * running
            value = (gains[s] * wall_gains[s]) * (running + base[s, x])
            forward = value
            back = value
            step = 1
            while step < depth:
                scale = wall_decays[s] ** step
                forward = forward + jnp.where(row >= step, scale * pltpu.roll(forward, step, 0), 0.0)
                back = back + jnp.where(row < depth - step, scale * pltpu.roll(back, depth - step, 0), 0.0)
                step *= 2
            base[s, x] = forward + back - value
            for m in range(TEAM):
                ends[m, 0, s, x : x + 1] = forward[depth - 1 : depth]
                ends[m, 1, s, x : x + 1] = back[0:1]


def wall_sum_kernel(steps, ends, sums):
    for s in range(2):
        before = decayed([ends[m, 0, s] for m in range(TEAM)], steps[s])
        after = decayed([ends[m, 1, s] for m in range(TEAM - 1, -1, -1)], steps[s])
        for team in range(sums.shape[0]):
            sums[team, 0, s] = before
            sums[team, 1, s] = after


def chosen_sum(parts, index, weights):
    total = None
    for place, part in enumerate(parts):
        term = pick(index, [row[place] for row in weights]) * part
        total = term if total is None else total + term
    return total


def wall_kernel(decays, base, ends, sums, out):
    _, width, depth, span = base.shape
    teams = sums.shape[0]
    position = lax.axis_index("wall")
    member = lax.rem(position, TEAM)
    team = lax.div(position, TEAM)
    row = lax.broadcasted_iota(jnp.int32, (depth, span), 0)
    for s in range(2):
        step = decays[s] ** depth
        leap = step**TEAM
        mirror = decays[s] ** (depth * TEAM * teams + 1)
        scale = -1.0 / (1.0 - mirror * mirror)
        below = [sums[t, 0, s] for t in range(teams)]
        above = [sums[t, 1, s] for t in range(teams)]
        top = decays[s] * decayed(below, leap)
        bottom = decays[s] * decayed(above[::-1], leap)
        from_bottom = scale * (bottom - mirror * top)
        from_top = scale * (top - mirror * bottom)
        before = chosen_sum(
            below + [from_bottom],
            team,
            [[leap ** (t - 1 - k) if k < t else 0.0 for k in range(teams)] + [leap**t] for t in range(teams)],
        )
        after = chosen_sum(
            above + [from_top],
            team,
            [[leap ** (k - t - 1) if k > t else 0.0 for k in range(teams)] + [leap ** (teams - 1 - t)] for t in range(teams)],
        )
        before = chosen_sum(
            [ends[m, 0, s] for m in range(TEAM)] + [before],
            member,
            [[step ** (m - 1 - k) if k < m else 0.0 for k in range(TEAM)] + [step**m] for m in range(TEAM)],
        )
        after = chosen_sum(
            [ends[m, 1, s] for m in range(TEAM)] + [after],
            member,
            [[step ** (k - m - 1) if k > m else 0.0 for k in range(TEAM)] + [step ** (TEAM - 1 - m)] for m in range(TEAM)],
        )
        rise = jnp.zeros((depth, span), jnp.float32)
        fall = jnp.zeros((depth, span), jnp.float32)
        for z in range(depth):
            rise = jnp.where(row == z, decays[s] ** (z + 1), rise)
            fall = jnp.where(row == z, decays[s] ** (depth - z), fall)
        for x in range(width):
            out[s, x] = base[s, x] + rise * before[x : x + 1] + fall * after[x : x + 1]


def exchange(values, axis, size, stride):
    peers = values.shape[0]
    groups = [
        [start + offset + stride * k for k in range(peers)]
        for start in range(0, size, stride * peers)
        for offset in range(stride)
    ]
    return lax.all_to_all(values, axis, split_axis=0, concat_axis=0, tiled=True, axis_index_groups=groups)


def per_device(concentration, velocity, potential):
    _, width, depth, span = concentration.shape
    stream = lax.axis_size("stream")
    wall = lax.axis_size("wall")
    stream_total = width * stream
    wall_total = depth * wall
    rates_x = (4.0 * width * width, float(stream_total * stream_total // 25))
    rates_z = (4.0 * depth * depth, float(wall_total * wall_total // 16))
    decays_x, gains_x = zip(*[line_factors(rate) for rate in rates_x])
    decays_z, gains_z = zip(*[line_factors(rate) for rate in rates_z])
    steps_x = [decay**width for decay in decays_x]
    steps_z = [decay**depth for decay in decays_z]

    edges = (4, width, span)
    low_edge, high_edge, right_edge = call(
        edge_kernel,
        [edges, edges, (4, depth, span)],
        (concentration, velocity, potential),
        [
            pltpu.VMEM(concentration.shape, jnp.float32),
            pltpu.VMEM(potential.shape, jnp.float32),
            pltpu.VMEM(potential.shape, jnp.float32),
            pltpu.SemaphoreType.DMA((4,)),
        ],
        pltpu.HBM,
        62,
    )
    ring = [(i, (i + 1) % stream) for i in range(stream)]
    rising = [(i, i + 1) for i in range(wall - 1)]
    falling = [(i + 1, i) for i in range(wall - 1)]
    left_halo = lax.ppermute(right_edge, "stream", ring)
    below_halo = lax.ppermute(high_edge, "wall", rising)
    above_halo = lax.ppermute(low_edge, "wall", falling)
    share = (2, depth, span // HALVES)
    pred, spill, ends = call(
        functools.partial(predict_kernel, decays_x),
        [concentration.shape, (2, depth, span), (TEAM,) + share],
        (concentration, velocity, potential, low_edge, high_edge, left_halo, below_halo, above_halo),
    )
    ends = exchange(ends, "stream", stream, 1)
    (sums,) = call(functools.partial(stream_sum_kernel, steps_x), [(stream // TEAM,) + share], (ends,))
    sums = exchange(sums, "stream", stream, TEAM)
    (links,) = call(functools.partial(stream_link_kernel, steps_x), [(TEAM,) + share], (ends, sums))
    links = exchange(links, "stream", stream, 1)
    line_ends = (2, 2, width, span)
    base, ends = call(
        functools.partial(stream_kernel, decays_x, gains_x, decays_z, gains_z),
        [concentration.shape, (TEAM,) + line_ends],
        (pred, spill, links),
    )
    ends = exchange(ends, "wall", wall, 1)
    (sums,) = call(functools.partial(wall_sum_kernel, steps_z), [(wall // TEAM,) + line_ends], (ends,))
    sums = exchange(sums, "wall", wall, TEAM)
    (out,) = call(functools.partial(wall_kernel, decays_z), [concentration.shape], (base, ends, sums))
    return out


def solution(mesh):
    return jax.shard_map(
        per_device,
        mesh=mesh,
        in_specs=(
            P(None, "stream", "wall", None),
            P(None, "stream", "wall", None),
            P("stream", "wall", None),
        ),
        out_specs=P(None, "stream", "wall", None),
        check_vma=False,
    )
```

```python
import functools

import jax
import jax.numpy as jnp
import numpy as np
from jax import lax
from jax.experimental import pallas as pl
from jax.experimental.pallas import tpu as pltpu
from jax.sharding import PartitionSpec as P

ADVECT_STEP = 0.2
DRIFT_RATES = (1.0, -0.5)
FLUX_SCALE = 0.25 * ADVECT_STEP
HIGHEST = lax.Precision.HIGHEST
TEAM = 4
LANES = 128


def line_factors(rate):
    base = 1.0 + 2.0 * rate
    root = np.sqrt(1.0 + 4.0 * rate)
    return float(2.0 * rate / (base + root)), float(1.0 / root)


def block_tables(decay, gain, cells):
    place = np.arange(cells)
    local = gain * decay ** np.abs(place[:, None] - place[None, :])
    collect = np.stack([decay ** (cells - 1 - place), decay**place], axis=1)
    spread = gain * np.stack([decay ** (place + 1), decay ** (cells - place)])
    return local, collect, spread


def wall_tables(rates, stream_rates, width, depth):
    layers = width + 1
    size = 2 * layers * depth
    cells = 2 * width * depth
    inject = np.zeros((2, LANES, 2, layers, depth))
    into_cells = inject[0].reshape(2, width, depth, 2, layers, depth)
    top = inject[1, : 2 * width].reshape(2, width, 2, layers, depth)
    bottom = inject[1, 2 * width : 4 * width].reshape(2, width, 2, layers, depth)
    before = inject[1, LANES // 2 : LANES // 2 + 2 * depth].reshape(2, depth, 2, layers, depth)
    near = np.zeros((2, layers, depth, 2, layers, depth))
    collect = np.zeros((2, layers, depth, 2, 2, LANES // 4))
    spread = np.zeros((2, 2, LANES // 4, 2, layers, depth))
    output = np.zeros((2, layers, depth, 2, LANES))
    out_cells = output[:, :, :, 0].reshape(2, layers, depth, 2, width, depth)
    out_sums = output[:, :, :, 1, : 4 * depth].reshape(2, layers, depth, 2, 2, depth)
    out_before = output[:, :, :, 1, 4 * depth : 6 * depth].reshape(2, layers, depth, 2, depth)
    for s in range(2):
        local, gather, hand = block_tables(*line_factors(rates[s]), depth)
        decay = line_factors(stream_rates[s])[0]
        for layer in range(layers):
            x = layer - 1
            near[s, layer, :, s, layer, :] = local
            collect[s, layer, :, :, s, layer] = gather
            spread[:, s, layer, s, layer, :] = hand
            for z in range(depth):
                if layer:
                    into_cells[s, x, z, s, layer, z] = 1.0
                    out_cells[s, layer, z, s, x, z] = 1.0
                else:
                    before[s, z, s, layer, z] = 1.0
                    out_before[s, layer, z, s, z] = 1.0
                out_sums[s, layer, z, 0, s, z] = decay ** (width - 1 - x)
                out_sums[s, layer, z, 1, s, z] = decay**x
            if layer:
                top[s, x, s, layer, depth - 1] = -FLUX_SCALE
                bottom[s, x, s, layer, 0] = FLUX_SCALE
    inject = inject.reshape(2 * LANES, size)
    near = near.reshape(size, size)
    output = output.reshape(size, 2 * LANES)
    gathered = inject @ collect.reshape(size, LANES)
    solved = inject @ near @ output
    handed = spread.reshape(LANES, size) @ output
    return gathered, np.concatenate([solved[:LANES], handed, solved[LANES:]])


def stream_tables(rates, width, depth):
    near = np.zeros((2, width, depth, 2, width, depth))
    spread = np.zeros((LANES, 2, width, depth))
    entering = spread[: 4 * depth].reshape(2, 2, depth, 2, width, depth)
    before = spread[4 * depth : 6 * depth].reshape(2, depth, 2, width, depth)
    for s in range(2):
        local, _, hand = block_tables(*line_factors(rates[s]), width)
        for z in range(depth):
            near[s, :, z, s, :, z] = local
            entering[:, s, z, s, :, z] = hand
            before[s, z, s, :, z] = hand[0]
    cells = 2 * width * depth
    return np.concatenate([near.reshape(cells, cells), spread.reshape(LANES, cells)])


def whole(memory=pltpu.VMEM):
    return pl.BlockSpec(memory_space=memory)


def call(kernel, outs, ins, scratch=(), memory=pltpu.VMEM, room=32):
    return pl.pallas_call(
        kernel,
        out_shape=[jax.ShapeDtypeStruct(shape, jnp.float32) for shape in outs],
        in_specs=[whole(memory)] * len(ins),
        out_specs=[whole(memory)] * len(outs),
        scratch_shapes=list(scratch),
        compiler_params=pltpu.CompilerParams(vmem_limit_bytes=room * 1024 * 1024),
    )(*ins)


def edge_kernel(conc, vel, volt, edge, arrived):
    last = volt.shape[0] - 1
    copies = [
        pltpu.make_async_copy(source, edge.at[place], arrived.at[place])
        for place, source in enumerate((conc.at[0, last], conc.at[1, last], vel.at[0, last], volt.at[last]))
    ]
    for copy in copies:
        copy.start()
    for copy in copies:
        copy.wait()


def face(conc_low, conc_high, speed_low, speed_high, volt_low, volt_high, species):
    drift = speed_low + speed_high - (2.0 * DRIFT_RATES[species]) * (volt_high - volt_low)
    return (conc_low + conc_high) * drift


def predict_kernel(conc, vel, volt, left_halo, shares, rows):
    width, depth, span = volt.shape
    row = lax.broadcasted_iota(jnp.int32, (depth, span), 0)
    rows[LANES:] = jnp.zeros((LANES, span), jnp.float32)
    left = [face(left_halo[s], conc[s, 0], left_halo[2], vel[0, 0], left_halo[3], volt[0], s) for s in range(2)]
    for s in range(2):
        start = LANES + LANES // 2 + s * depth
        rows[start : start + depth] = -FLUX_SCALE * left[s]
    for x in range(width):
        here = volt[x]
        rise = vel[1, x]
        volt_up = pltpu.roll(here, depth - 1, 0)
        volt_next = pltpu.roll(here, span - 1, 1)
        speed_up = pltpu.roll(rise, depth - 1, 0)
        speed_next = pltpu.roll(vel[2, x], span - 1, 1)
        for s in range(2):
            value = conc[s, x]
            wall = face(value, pltpu.roll(value, depth - 1, 0), rise, speed_up, here, volt_up, s)
            wall = jnp.where(row == depth - 1, 0.0, wall)
            side = face(value, pltpu.roll(value, span - 1, 1), vel[2, x], speed_next, here, volt_next, s)
            total = (wall - pltpu.roll(wall, 1, 0)) + (side - pltpu.roll(side, 1, 1)) - left[s]
            if x + 1 < width:
                left[s] = face(value, conc[s, x + 1], vel[0, x], vel[0, x + 1], here, volt[x + 1], s)
                total = total + left[s]
            place = s * width + x
            rows[place * depth : (place + 1) * depth] = value - FLUX_SCALE * total
            drift = (2.0 * DRIFT_RATES[s]) * here
            top = slice(depth - 1, depth)
            for part, edge in enumerate(
                (value[top], rise[top] + drift[top], value[0:1], rise[0:1] - drift[0:1])
            ):
                line = LANES + part * 2 * width + place
                rows[line : line + 1] = edge
    places = shares.shape[2]
    tiles = LANES // places
    for part in range(2):
        for chunk in range(span // LANES):
            turned = rows[part * LANES : (part + 1) * LANES, chunk * LANES : (chunk + 1) * LANES].T
            shares[chunk * tiles : (chunk + 1) * tiles, part] = turned.reshape(tiles, places, LANES)


def by_lane(values, lane, unit):
    return jnp.where(lax.rem(lax.div(lane, unit), 2) == 0, values[0], values[1])


def wall_kernel(decays, stream_steps, blocks, width, depth, parts, collect, solve, solved, ends, sums, carry, fluxes):
    members, _, places, _ = parts.shape
    flat = members * places
    lane = lax.broadcasted_iota(jnp.int32, (places, LANES), 1)
    faces = 2 * width
    for m in range(TEAM):
        below = jnp.zeros((places, LANES), jnp.float32)
        for b in range(blocks):
            if b == 0:
                meet = pltpu.roll(parts[m * blocks, 1], LANES - 2 * faces, 1)
                below = meet * pltpu.roll(meet, LANES - faces, 1)
            meet = parts[m * blocks + b, 1]
            if b + 1 < blocks:
                meet = meet + pltpu.roll(parts[m * blocks + b + 1, 1], LANES - 2 * faces, 1)
            above = meet * pltpu.roll(meet, LANES - faces, 1)
            fluxes[m * blocks + b] = jnp.where(
                lane < faces, above, jnp.where(lane < 2 * faces, pltpu.roll(below, faces, 1), parts[m * blocks + b, 1])
            )
            below = above
    value = parts[:, 0].reshape(flat, LANES)
    flux = fluxes[...].reshape(flat, LANES)
    carry[...] = jnp.dot(
        jnp.concatenate([value, flux], axis=1), collect[...], precision=HIGHEST, preferred_element_type=jnp.float32
    ).reshape(members, places, LANES)
    side = LANES // 2
    unit = LANES // 4
    entering = lane < side
    step = by_lane([decay**depth for decay in decays], lane, unit)
    mirrors = [decay ** (depth * blocks + 1) for decay in decays]
    mirror = by_lane(mirrors, lane, unit)
    scale = by_lane([-d / (1.0 - m * m) for d, m in zip(decays, mirrors)], lane, unit)
    weights = [
        jnp.where(
            entering,
            by_lane([decay ** (depth * b) for decay in decays], lane, unit),
            by_lane([decay ** (depth * (blocks - 1 - b)) for decay in decays], lane, unit),
        )
        for b in range(blocks)
    ]
    for m in range(TEAM):
        before = jnp.zeros((places, LANES), jnp.float32)
        after = jnp.zeros((places, LANES), jnp.float32)
        befores = []
        afters = [None] * blocks
        for b in range(blocks):
            befores.append(before)
            before = step * before + carry[m * blocks + b]
        for b in range(blocks - 1, -1, -1):
            afters[b] = after
            after = step * after + carry[m * blocks + b]
        total = jnp.where(entering, before, after)
        mirrored = scale * (pltpu.roll(total, side, 1) - mirror * total)
        for b in range(blocks):
            carry[m * blocks + b] = jnp.where(entering, befores[b], afters[b]) + weights[b] * mirrored
    full = jnp.concatenate([value, carry[...].reshape(flat, LANES), flux], axis=1)
    result = jnp.dot(full, solve[...], precision=HIGHEST, preferred_element_type=jnp.float32)
    solved[...] = result[:, :LANES].reshape(members, places, LANES)
    ends[...] = result[:, LANES:].reshape(members, places, LANES)
    step = by_lane(stream_steps, lane, depth)
    entering = lane < 2 * depth
    pack = LANES // (4 * depth)
    for group in range(blocks // pack):
        packed = None
        for part in range(pack):
            b = group * pack + part
            before = ends[b]
            after = ends[(TEAM - 1) * blocks + b]
            for m in range(1, TEAM):
                before = step * before + ends[m * blocks + b]
                after = step * after + ends[(TEAM - 1 - m) * blocks + b]
            both = jnp.where(entering, before, jnp.where(lane < 4 * depth, after, 0.0))
            packed = packed + pltpu.roll(both, part * 4 * depth, 1) if part else both
        for team in range(sums.shape[0]):
            sums[team, group] = packed


def stream_kernel(steps, blocks, depth, cells, ends, sums, solve, solved, carry):
    places = cells.shape[1]
    flat = cells.shape[0] * places
    teams, groups = sums.shape[0], sums.shape[1]
    pack = blocks // groups
    team = lax.div(lax.axis_index("stream"), TEAM)
    lane = lax.broadcasted_iota(jnp.int32, (places, LANES), 1)
    entering = lax.rem(lane, 4 * depth) < 2 * depth
    step = by_lane(steps, lane, depth)
    leap = by_lane([value**TEAM for value in steps], lane, depth)
    closing = by_lane([1.0 / (1.0 - value ** (TEAM * teams)) for value in steps], lane, depth)
    for group in range(groups):
        before = sums[team, group]
        after = before
        for k in range(1, teams):
            before = leap * before + sums[lax.rem(team + k, teams), group]
            after = leap * after + sums[lax.rem(team + teams - k, teams), group]
        both = closing * jnp.where(entering, before, after)
        for part in range(pack):
            b = group * pack + part
            before = pltpu.roll(both, LANES - part * 4 * depth, 1) if part else both
            after = before
            afters = [None] * TEAM
            for m in range(TEAM - 1, -1, -1):
                afters[m] = after
                after = step * after + ends[m * blocks + b]
            for m in range(TEAM):
                own = ends[m * blocks + b]
                carry[m * blocks + b] = jnp.where(lane < 4 * depth, jnp.where(entering, before, afters[m]), own)
                before = step * before + own
    full = jnp.concatenate([cells[...].reshape(flat, LANES), carry[...].reshape(flat, LANES)], axis=1)
    result = jnp.dot(full, solve[...], precision=HIGHEST, preferred_element_type=jnp.float32)
    solved[...] = result.reshape(cells.shape)


def place_kernel(shares, out):
    _, width, depth, span = out.shape
    tiles = LANES // shares.shape[1]
    for chunk in range(span // LANES):
        turned = shares[chunk * tiles : (chunk + 1) * tiles].reshape(LANES, LANES).T
        for s in range(2):
            for x in range(width):
                start = (s * width + x) * depth
                out[s, x, :, chunk * LANES : (chunk + 1) * LANES] = turned[start : start + depth]


def per_device(concentration, velocity, potential):
    _, width, depth, span = concentration.shape
    stream = lax.axis_size("stream")
    wall = lax.axis_size("wall")
    stream_total = width * stream
    wall_total = depth * wall
    rates_x = (4.0 * width * width, float(stream_total * stream_total // 25))
    rates_z = (4.0 * depth * depth, float(wall_total * wall_total // 16))
    steps_x = [line_factors(rate)[0] ** width for rate in rates_x]
    decays_z = [line_factors(rate)[0] for rate in rates_z]
    collect_z, solve_z = wall_tables(rates_z, rates_x, width, depth)
    solve_x = stream_tables(rates_x, width, depth)

    (edge,) = call(
        edge_kernel,
        [(4, depth, span)],
        (concentration, velocity, potential),
        [pltpu.SemaphoreType.DMA((4,))],
        pltpu.HBM,
        62,
    )
    left_halo = lax.ppermute(edge, "stream", [(i, (i + 1) % stream) for i in range(stream)])

    members = TEAM * wall
    teams = stream // TEAM
    plane = [[b * stream + t * TEAM + m for m in range(TEAM) for b in range(wall)] for t in range(teams)]
    ranks = [[t * TEAM + m for t in range(teams)] for m in range(TEAM)]
    swap = functools.partial(lax.all_to_all, split_axis=0, concat_axis=0, tiled=True)
    table = functools.partial(jnp.array, dtype=jnp.float32)
    places = span // members
    tile = (members, places, LANES)
    (shares,) = call(
        predict_kernel,
        [(members, 2, places, LANES)],
        (concentration, velocity, potential, left_halo),
        [pltpu.VMEM((2 * LANES, span), jnp.float32)],
    )
    parts = swap(shares, ("wall", "stream"), axis_index_groups=plane)
    pack = LANES // (4 * depth)
    cells, ends, sums = call(
        functools.partial(wall_kernel, decays_z, steps_x, wall, width, depth),
        [tile, tile, (teams, wall // pack, places, LANES)],
        (parts, table(collect_z), table(solve_z)),
        [pltpu.VMEM(tile, jnp.float32), pltpu.VMEM(tile, jnp.float32)],
    )
    sums = swap(sums, "stream", axis_index_groups=ranks)
    (cells,) = call(
        functools.partial(stream_kernel, steps_x, wall, depth),
        [tile],
        (cells, ends, sums, table(solve_x)),
        [pltpu.VMEM(tile, jnp.float32)],
    )
    shares = swap(cells, ("wall", "stream"), axis_index_groups=plane)
    (out,) = call(place_kernel, [concentration.shape], (shares,))
    return out


def solution(mesh):
    return jax.shard_map(
        per_device,
        mesh=mesh,
        in_specs=(
            P(None, "stream", "wall", None),
            P(None, "stream", "wall", None),
            P("stream", "wall", None),
        ),
        out_specs=P(None, "stream", "wall", None),
        check_vma=False,
    )
```

```python
import functools

import jax
import jax.numpy as jnp
import numpy as np
from jax import lax
from jax.experimental import pallas as pl
from jax.experimental.pallas import tpu as pltpu
from jax.sharding import PartitionSpec as P

ADVECT_STEP = 0.2
DRIFT_RATES = (1.0, -0.5)
FLUX_SCALE = 0.25 * ADVECT_STEP
TEAM = 4
HALVES = 2
LANES = 128


def line_factors(rate):
    base = 1.0 + 2.0 * rate
    root = np.sqrt(1.0 + 4.0 * rate)
    return float(2.0 * rate / (base + root)), float(1.0 / root)


def block_tables(decay, gain, cells):
    place = np.arange(cells)
    local = gain * decay ** np.abs(place[:, None] - place[None, :])
    collect = np.stack([decay ** (cells - 1 - place), decay**place], axis=1)
    spread = gain * np.stack([decay ** (place + 1), decay ** (cells - place)])
    return local, collect, spread


def collect_table(rates_x, rates_z, width, depth):
    table = np.zeros((4 * depth + 4 * width, 2, width, depth))
    stream_sums = table[: 4 * depth].reshape(2, 2, depth, 2, width, depth)
    wall_sums = table[4 * depth :].reshape(2, 2, width, 2, width, depth)
    for s in range(2):
        _, gather_x, _ = block_tables(*line_factors(rates_x[s]), width)
        _, gather_z, _ = block_tables(*line_factors(rates_z[s]), depth)
        for z in range(depth):
            stream_sums[:, s, z, s, :, z] = gather_x.T
        for x in range(width):
            wall_sums[:, s, x, s, x, :] = gather_z.T
    return table.reshape(-1, 2 * width * depth)


def wall_tables(rates_x, rates_z, width, depth):
    unit = LANES // 4
    collect = np.zeros((2, LANES, 2, 2, unit))
    solve = np.zeros((3, LANES, LANES))
    sums_in = collect[0, : 4 * depth].reshape(2, 2, depth, 2, 2, unit)
    ends_in = collect[0, 4 * depth : 4 * (depth + width)].reshape(2, 2, width, 2, 2, unit)
    flux_in = collect[1, : 4 * width].reshape(2, 2, width, 2, 2, unit)
    near = solve[0, : 4 * depth, : 4 * depth].reshape(2, 2, depth, 2, 2, depth)
    spread = solve[1, :, : 4 * depth].reshape(2, 2, unit, 2, 2, depth)
    moved = solve[1, :, 4 * depth : 4 * (depth + width)].reshape(2, 2, unit, 2, 2, width)
    flux_near = solve[2, : 4 * width, : 4 * depth].reshape(2, 2, width, 2, 2, depth)
    flux_moved = solve[2, : 4 * width, 4 * depth : 4 * (depth + width)].reshape(2, 2, width, 2, 2, width)
    for s in range(2):
        _, gather_x, _ = block_tables(*line_factors(rates_x[s]), width)
        local, gather_z, hand = block_tables(*line_factors(rates_z[s]), depth)
        decay = line_factors(rates_z[s])[0]
        for side in range(2):
            sums_in[side, s, :, :, s, width + side] = gather_z
            near[side, s, :, side, s, :] = local
            spread[:, s, width + side, side, s, :] = hand
            for x in range(width):
                ends_in[side, s, x, side, s, x] = 1.0
                moved[side, s, x, side, s, x] = 1.0
        for end, cell, size in ((0, depth - 1, -FLUX_SCALE), (1, 0, FLUX_SCALE)):
            for x in range(width):
                flux_in[end, s, x, :, s, x] = size * gather_z[cell]
                flux_moved[end, s, x, 1 - end, s, x] = size / decay
                for side in range(2):
                    flux_in[end, s, x, :, s, width + side] = size * gather_x[x, side] * gather_z[cell]
                    flux_near[end, s, x, side, s, :] = size * gather_x[x, side] * local[cell]
    return collect.reshape(2 * LANES, LANES), solve.reshape(3 * LANES, LANES)


def home_table(rates_x, rates_z, width, depth):
    cells = 2 * width * depth
    near = np.zeros((2, width, depth, 2, width, depth))
    stream_spread = np.zeros((2, width, depth, 2, 2, depth))
    wall_spread = np.zeros((2, width, depth, 2, 2, width))
    for s in range(2):
        local_x, _, hand_x = block_tables(*line_factors(rates_x[s]), width)
        local_z, _, hand_z = block_tables(*line_factors(rates_z[s]), depth)
        near[s, :, :, s, :, :] = np.einsum("xa,zb->xzab", local_x, local_z)
        stream_spread[s, :, :, :, s, :] = np.einsum("ex,zb->xzeb", hand_x, np.eye(depth))
        wall_spread[s, :, :, :, s, :] = np.einsum("xa,ez->xzea", local_x, hand_z)
    return np.concatenate([part.reshape(cells, -1) for part in (near, stream_spread, wall_spread)], axis=1)


def call(kernel, outs, ins, scratch=(), aliases=None):
    return pl.pallas_call(
        kernel,
        out_shape=[jax.ShapeDtypeStruct(shape, jnp.float32) for shape in outs],
        in_specs=[pl.BlockSpec(memory_space=pltpu.VMEM)] * len(ins),
        out_specs=[pl.BlockSpec(memory_space=pltpu.VMEM)] * len(outs),
        scratch_shapes=list(scratch),
        input_output_aliases=aliases or {},
        compiler_params=pltpu.CompilerParams(vmem_limit_bytes=32 * 1024 * 1024),
    )(*ins)


def drift(volt, species):
    return (2.0 * DRIFT_RATES[species]) * volt


def face(conc_low, conc_high, speed_low, speed_high, volt_low, volt_high, species):
    return (conc_low + conc_high) * (speed_low + speed_high - drift(volt_high - volt_low, species))


def last_layers(conc, vel, volt):
    return jnp.stack([conc[0, -1], conc[1, -1], vel[0, -1] + drift(volt[-1], 0), vel[0, -1] + drift(volt[-1], 1)])


def split(values):
    high = values.astype(jnp.bfloat16)
    return high, (values - high.astype(jnp.float32)).astype(jnp.bfloat16)


def product(left, right):
    left_high, left_low = split(left)
    right_high, right_low = split(right)
    dot = functools.partial(jnp.dot, preferred_element_type=jnp.float32)
    return dot(left_high, right_high) + (dot(left_low, right_high) + dot(left_high, right_low))


def predict_kernel(conc, vel, volt, collect, cells, rows):
    width, depth, span = volt.shape
    row = lax.broadcasted_iota(jnp.int32, (depth, span), 0)
    left = [None, None]
    sums = 4 * (width + depth)
    for x in range(width):
        here = volt[x]
        rise = vel[1, x]
        volt_up = pltpu.roll(here, depth - 1, 0)
        volt_next = pltpu.roll(here, span - 1, 1)
        speed_up = pltpu.roll(rise, depth - 1, 0)
        speed_next = pltpu.roll(vel[2, x], span - 1, 1)
        for s in range(2):
            value = conc[s, x]
            wall = face(value, pltpu.roll(value, depth - 1, 0), rise, speed_up, here, volt_up, s)
            wall = jnp.where(row == depth - 1, 0.0, wall)
            side = face(value, pltpu.roll(value, span - 1, 1), vel[2, x], speed_next, here, volt_next, s)
            total = (wall - pltpu.roll(wall, 1, 0)) + (side - pltpu.roll(side, 1, 1))
            if x:
                total = total - left[s]
            if x + 1 < width:
                left[s] = face(value, conc[s, x + 1], vel[0, x], vel[0, x + 1], here, volt[x + 1], s)
                total = total + left[s]
            place = s * width + x
            cells[place * depth : (place + 1) * depth] = value - FLUX_SCALE * total
            moved = drift(here, s)
            top = slice(depth - 1, depth)
            for part, edge in enumerate(
                (value[top], rise[top] + moved[top], value[0:1], rise[0:1] - moved[0:1])
            ):
                line = sums + part * 2 * width + place
                rows[line : line + 1] = edge
    rows[:sums] = product(collect[...], cells[...])


def enter_kernel(decays_x, decays_z, cells_in, rows_in, left_halo, conc, vel, volt, shares, cells, rows):
    width, depth, span = volt.shape
    row = lax.broadcasted_iota(jnp.int32, (depth, span), 0)
    for s in range(2):
        decay = decays_x[s]
        flux = (left_halo[s] + conc[s, 0]) * (left_halo[2 + s] + (vel[0, 0] - drift(volt[0], s)))
        taken = -FLUX_SCALE * flux
        gained = (decay - 1.0) * taken
        start = s * width * depth
        cells[start : start + depth] = cells_in[start : start + depth] + gained
        for side, scale in enumerate((decay ** (width - 1) * (decay - 1.0), 1.0 / decay - 1.0)):
            start = (side * 2 + s) * depth
            rows[start : start + depth] = rows_in[start : start + depth] + scale * taken
            weight = jnp.zeros((depth, span), jnp.float32)
            for z in range(depth):
                weight = jnp.where(row == z, decays_z[s] ** (z if side else depth - 1 - z), weight)
            line = 4 * depth + (side * 2 + s) * width
            rows[line : line + 1] = rows_in[line : line + 1] + jnp.sum(weight * gained, axis=0, keepdims=True)
    part = shares.shape[1] // HALVES
    tiles = LANES // part
    for chunk in range(span // LANES):
        turned = rows[:, chunk * LANES : (chunk + 1) * LANES].T
        half, start = divmod(chunk * tiles, shares.shape[0])
        for k in range(tiles):
            shares[start + k, half * part : (half + 1) * part] = turned[k * part : (k + 1) * part]


def by_lane(values, lane, unit):
    return jnp.where(lax.rem(lax.div(lane, unit), 2) == 0, values[0], values[1])


def wall_kernel(decays, stream_steps, blocks, width, depth, parts, collect, solve, ends, sums, carry, fluxes):
    members, places, _ = parts.shape
    flat = members * places
    lane = lax.broadcasted_iota(jnp.int32, (places, LANES), 1)
    faces = 2 * width
    first = LANES // 2
    for m in range(TEAM):
        line = m * blocks
        below = pltpu.roll(parts[line], LANES - first - 2 * faces, 1)
        below = below * pltpu.roll(below, LANES - faces, 1)
        for b in range(blocks):
            meet = pltpu.roll(parts[line + b], LANES - first, 1)
            if b + 1 < blocks:
                meet = meet + pltpu.roll(parts[line + b + 1], LANES - first - 2 * faces, 1)
            above = meet * pltpu.roll(meet, LANES - faces, 1)
            both = jnp.where(lane < faces, above, pltpu.roll(below, faces, 1))
            fluxes[line + b] = jnp.where(lane < 2 * faces, both, 0.0)
            below = above
    value = parts[...].reshape(flat, LANES)
    flux = fluxes[...].reshape(flat, LANES)
    carry[...] = product(jnp.concatenate([value, flux], axis=1), collect[...]).reshape(members, places, LANES)
    side = LANES // 2
    unit = LANES // 4
    entering = lane < side
    step = by_lane([decay**depth for decay in decays], lane, unit)
    mirrors = [decay ** (depth * blocks + 1) for decay in decays]
    mirror = by_lane(mirrors, lane, unit)
    scale = by_lane([-d / (1.0 - m * m) for d, m in zip(decays, mirrors)], lane, unit)
    weights = [
        jnp.where(
            entering,
            by_lane([decay ** (depth * b) for decay in decays], lane, unit),
            by_lane([decay ** (depth * (blocks - 1 - b)) for decay in decays], lane, unit),
        )
        for b in range(blocks)
    ]
    for m in range(TEAM):
        before = jnp.zeros((places, LANES), jnp.float32)
        after = jnp.zeros((places, LANES), jnp.float32)
        befores = []
        afters = [None] * blocks
        for b in range(blocks):
            befores.append(before)
            before = step * before + carry[m * blocks + b]
        for b in range(blocks - 1, -1, -1):
            afters[b] = after
            after = step * after + carry[m * blocks + b]
        total = jnp.where(entering, before, after)
        mirrored = scale * (pltpu.roll(total, side, 1) - mirror * total)
        for b in range(blocks):
            carry[m * blocks + b] = jnp.where(entering, befores[b], afters[b]) + weights[b] * mirrored
    full = jnp.concatenate([value, carry[...].reshape(flat, LANES), flux], axis=1)
    ends[...] = product(full, solve[...]).reshape(members, places, LANES)
    step = by_lane(stream_steps, lane, depth)
    entering = lane < 2 * depth
    pack = LANES // (4 * depth)
    for group in range(blocks // pack):
        packed = None
        for part in range(pack):
            b = group * pack + part
            before = ends[b]
            after = ends[(TEAM - 1) * blocks + b]
            for m in range(1, TEAM):
                before = step * before + ends[m * blocks + b]
                after = step * after + ends[(TEAM - 1 - m) * blocks + b]
            both = jnp.where(entering, before, jnp.where(lane < 4 * depth, after, 0.0))
            packed = packed + pltpu.roll(both, part * 4 * depth, 1) if part else both
        for team in range(sums.shape[0]):
            sums[team, group] = packed


def stream_kernel(steps, blocks, depth, ends, sums, links):
    places = ends.shape[1]
    teams, groups = sums.shape[0], sums.shape[1]
    pack = blocks // groups
    part = links.shape[1]
    team = lax.div(lax.axis_index("stream"), TEAM)
    lane = lax.broadcasted_iota(jnp.int32, (places, LANES), 1)
    entering = lax.rem(lane, 4 * depth) < 2 * depth
    step = by_lane(steps, lane, depth)
    leap = by_lane([value**TEAM for value in steps], lane, depth)
    closing = by_lane([1.0 / (1.0 - value ** (TEAM * teams)) for value in steps], lane, depth)
    for group in range(groups):
        before = sums[team, group]
        after = before
        for k in range(1, teams):
            before = leap * before + sums[lax.rem(team + k, teams), group]
            after = leap * after + sums[lax.rem(team + teams - k, teams), group]
        both = closing * jnp.where(entering, before, after)
        for slot in range(pack):
            b = group * pack + slot
            before = pltpu.roll(both, LANES - slot * 4 * depth, 1) if slot else both
            after = before
            afters = [None] * TEAM
            for m in range(TEAM - 1, -1, -1):
                afters[m] = after
                after = step * after + ends[m * blocks + b]
            for m in range(TEAM):
                own = ends[m * blocks + b]
                carry = jnp.where(lane < 4 * depth, jnp.where(entering, before, afters[m]), own)
                before = step * before + own
                halved = carry + pltpu.roll(pltpu.roll(carry, LANES // HALVES, 1), part, 0)
                links[m * blocks + b] = halved[:part]


def home_kernel(cells, links, table, out, rows, carry):
    _, width, depth, span = out.shape
    part = links.shape[1]
    lanes = LANES // HALVES
    for k in range(links.shape[0]):
        rows[k * part : (k + 1) * part] = links[k]
    for chunk in range(rows.shape[0] // LANES):
        turned = rows[chunk * LANES : (chunk + 1) * LANES].T
        for half in range(HALVES):
            start = half * (span // HALVES) + chunk * LANES
            carry[:, start : start + LANES] = turned[half * lanes : (half + 1) * lanes]
    result = product(table[...], jnp.concatenate([cells[...], carry[...]], axis=0))
    for s in range(2):
        for x in range(width):
            start = (s * width + x) * depth
            out[s, x] = result[start : start + depth]


def per_device(concentration, velocity, potential):
    _, width, depth, span = concentration.shape
    stream = lax.axis_size("stream")
    wall = lax.axis_size("wall")
    stream_total = width * stream
    wall_total = depth * wall
    rates_x = (4.0 * width * width, float(stream_total * stream_total // 25))
    rates_z = (4.0 * depth * depth, float(wall_total * wall_total // 16))
    decays_x = [line_factors(rate)[0] for rate in rates_x]
    decays_z = [line_factors(rate)[0] for rate in rates_z]
    steps_x = [decay**width for decay in decays_x]
    collect_z, solve_z = wall_tables(rates_x, rates_z, width, depth)
    collect = collect_table(rates_x, rates_z, width, depth)
    home = home_table(rates_x, rates_z, width, depth)

    edge = last_layers(concentration, velocity, potential)
    left_halo = lax.ppermute(edge, "stream", [(i, (i + 1) % stream) for i in range(stream)])

    members = TEAM * wall
    teams = stream // TEAM
    plane = [[b * stream + t * TEAM + m for m in range(TEAM) for b in range(wall)] for t in range(teams)]
    ranks = [[t * TEAM + m for t in range(teams)] for m in range(TEAM)]
    swap = functools.partial(lax.all_to_all, split_axis=0, concat_axis=0, tiled=True)
    table = functools.partial(jnp.array, dtype=jnp.float32)
    places = span // members
    tile = (members, places, LANES)
    flat = (2 * width * depth, span)
    cells, rows = call(
        predict_kernel, [flat, (LANES, span)], (concentration, velocity, potential, table(collect))
    )
    shares, cells, rows = call(
        functools.partial(enter_kernel, decays_x, decays_z),
        [tile, flat, (LANES, span)],
        (cells, rows, left_halo, concentration, velocity, potential),
        aliases={0: 1, 1: 2},
    )
    parts = swap(shares, ("wall", "stream"), axis_index_groups=plane)
    pack = LANES // (4 * depth)
    ends, sums = call(
        functools.partial(wall_kernel, decays_z, steps_x, wall, width, depth),
        [tile, (teams, wall // pack, places, LANES)],
        (parts, table(collect_z), table(solve_z)),
        [pltpu.VMEM(tile, jnp.float32), pltpu.VMEM(tile, jnp.float32)],
    )
    sums = swap(sums, "stream", axis_index_groups=ranks)
    (links,) = call(
        functools.partial(stream_kernel, steps_x, wall, depth),
        [(members, places // HALVES, LANES)],
        (ends, sums),
    )
    links = swap(links, ("wall", "stream"), axis_index_groups=plane)
    (out,) = call(
        home_kernel,
        [concentration.shape],
        (cells, links, table(home)),
        [pltpu.VMEM((span // HALVES, LANES), jnp.float32), pltpu.VMEM((LANES // HALVES, span), jnp.float32)],
    )
    return out


def solution(mesh):
    return jax.shard_map(
        per_device,
        mesh=mesh,
        in_specs=(
            P(None, "stream", "wall", None),
            P(None, "stream", "wall", None),
            P("stream", "wall", None),
        ),
        out_specs=P(None, "stream", "wall", None),
        check_vma=False,
    )
```

```python
import functools

import jax
import jax.numpy as jnp
import numpy as np
from jax import lax
from jax.experimental import pallas as pl
from jax.experimental.pallas import tpu as pltpu
from jax.sharding import PartitionSpec as P

ADVECT_STEP = 0.2
DRIFT_RATES = (1.0, -0.5)
FLUX_SCALE = 0.25 * ADVECT_STEP
TEAM = 4
HALVES = 2
LANES = 128


def line_factors(rate):
    base = 1.0 + 2.0 * rate
    root = np.sqrt(1.0 + 4.0 * rate)
    return float(2.0 * rate / (base + root)), float(1.0 / root)


def block_tables(decay, gain, cells):
    place = np.arange(cells)
    local = gain * decay ** np.abs(place[:, None] - place[None, :])
    collect = np.stack([decay ** (cells - 1 - place), decay**place], axis=1)
    spread = gain * np.stack([decay ** (place + 1), decay ** (cells - place)])
    return local, collect, spread


def collect_table(rates_x, rates_z, width, depth):
    table = np.zeros((4 * depth + 4 * width, 2, width, depth))
    stream_sums = table[: 4 * depth].reshape(2, 2, depth, 2, width, depth)
    wall_sums = table[4 * depth :].reshape(2, 2, width, 2, width, depth)
    for s in range(2):
        _, gather_x, _ = block_tables(*line_factors(rates_x[s]), width)
        _, gather_z, _ = block_tables(*line_factors(rates_z[s]), depth)
        for z in range(depth):
            stream_sums[:, s, z, s, :, z] = gather_x.T
        for x in range(width):
            wall_sums[:, s, x, s, x, :] = gather_z.T
    return table.reshape(-1, 2 * width * depth)


def wall_tables(rates_x, rates_z, width, depth):
    unit = LANES // 4
    sums = 4 * (depth + width)
    collect = np.zeros((LANES, 2, 2, unit))
    solve = np.zeros((2, LANES, LANES))
    sums_in = collect[: 4 * depth].reshape(2, 2, depth, 2, 2, unit)
    ends_in = collect[4 * depth : sums].reshape(2, 2, width, 2, 2, unit)
    flux_in = collect[sums : sums + 4 * width].reshape(2, 2, width, 2, 2, unit)
    near = solve[0, : 4 * depth, : 4 * depth].reshape(2, 2, depth, 2, 2, depth)
    spread = solve[1, :, : 4 * depth].reshape(2, 2, unit, 2, 2, depth)
    moved = solve[1, :, 4 * depth : sums].reshape(2, 2, unit, 2, 2, width)
    flux_near = solve[0, sums : sums + 4 * width, : 4 * depth].reshape(2, 2, width, 2, 2, depth)
    flux_moved = solve[0, sums : sums + 4 * width, 4 * depth : sums].reshape(2, 2, width, 2, 2, width)
    for s in range(2):
        _, gather_x, _ = block_tables(*line_factors(rates_x[s]), width)
        local, gather_z, hand = block_tables(*line_factors(rates_z[s]), depth)
        decay = line_factors(rates_z[s])[0]
        for side in range(2):
            sums_in[side, s, :, :, s, width + side] = gather_z
            near[side, s, :, side, s, :] = local
            spread[:, s, width + side, side, s, :] = hand
            for x in range(width):
                ends_in[side, s, x, side, s, x] = 1.0
                moved[side, s, x, side, s, x] = 1.0
        for end, cell, size in ((0, depth - 1, -FLUX_SCALE), (1, 0, FLUX_SCALE)):
            for x in range(width):
                flux_in[end, s, x, :, s, x] = size * gather_z[cell]
                flux_moved[end, s, x, 1 - end, s, x] = size / decay
                for side in range(2):
                    flux_in[end, s, x, :, s, width + side] = size * gather_x[x, side] * gather_z[cell]
                    flux_near[end, s, x, side, s, :] = size * gather_x[x, side] * local[cell]
    return collect.reshape(LANES, LANES), solve.reshape(2 * LANES, LANES)


def home_tables(rates_x, rates_z, width, depth):
    cells = 2 * width * depth
    near = np.zeros((2, width, depth, 2, width, depth))
    stream_spread = np.zeros((2, width, depth, 2, 2, depth))
    wall_spread = np.zeros((2, width, depth, 2, 2, width))
    for s in range(2):
        local_x, _, hand_x = block_tables(*line_factors(rates_x[s]), width)
        local_z, _, hand_z = block_tables(*line_factors(rates_z[s]), depth)
        near[s, :, :, s, :, :] = np.einsum("xa,zb->xzab", local_x, local_z)
        stream_spread[s, :, :, :, s, :] = np.einsum("ex,zb->xzeb", hand_x, np.eye(depth))
        wall_spread[s, :, :, :, s, :] = np.einsum("xa,ez->xzea", local_x, hand_z)
    parts = (near[:, :, :, :, 0], stream_spread, wall_spread)
    return near.reshape(cells, cells), np.concatenate([part.reshape(cells, -1) for part in parts], axis=1)


def call(kernel, outs, ins, scratch=(), aliases=None, source=pltpu.VMEM, target=pltpu.VMEM, room=32 * 1024):
    return pl.pallas_call(
        kernel,
        out_shape=[jax.ShapeDtypeStruct(shape, jnp.float32) for shape in outs],
        in_specs=[pl.BlockSpec(memory_space=source)] * len(ins),
        out_specs=[pl.BlockSpec(memory_space=target)] * len(outs),
        scratch_shapes=list(scratch),
        input_output_aliases=aliases or {},
        compiler_params=pltpu.CompilerParams(vmem_limit_bytes=room * 1024),
    )(*ins)


def drift(volt, species):
    return (2.0 * DRIFT_RATES[species]) * volt


def face(conc_low, conc_high, speed_low, speed_high, volt_low, volt_high, species):
    return (conc_low + conc_high) * (speed_low + speed_high - drift(volt_high - volt_low, species))


def border_kernel(conc, vel, volt, edge, arrived):
    last = volt.shape[0] - 1
    copies = [
        pltpu.make_async_copy(source, edge.at[place], arrived.at[place])
        for place, source in enumerate((conc.at[0, last], conc.at[1, last], vel.at[0, last], volt.at[last]))
    ]
    for copy in copies:
        copy.start()
    for copy in copies:
        copy.wait()


def split(values):
    high = values.astype(jnp.bfloat16)
    return high, (values - high.astype(jnp.float32)).astype(jnp.bfloat16)


def product(values, table):
    high, low = split(values)
    table_high, table_low = split(table)
    dot = functools.partial(jnp.dot, preferred_element_type=jnp.float32)
    wide = table.shape[1]
    beside = jnp.concatenate([table_high, table_low], axis=1)
    if values.shape[1] <= LANES:
        under = jnp.concatenate([table_high, jnp.zeros_like(table_low)], axis=1)
        both = dot(jnp.concatenate([high, low], axis=1), jnp.concatenate([beside, under], axis=0))
        return both[:, :wide] + both[:, wide:]
    both = dot(high, beside)
    return both[:, :wide] + (both[:, wide:] + dot(low, table_high))


def left_product(table, values):
    high, low = split(values)
    table_high, table_low = split(table)
    dot = functools.partial(jnp.dot, preferred_element_type=jnp.float32)
    tall = table.shape[0]
    above = jnp.concatenate([table_high, table_low], axis=0)
    under = jnp.concatenate([table_high, jnp.zeros_like(table_low)], axis=0)
    both = dot(jnp.concatenate([above, under], axis=1), jnp.concatenate([high, low], axis=0))
    return both[:tall] + both[tall:]


def predict_kernel(conc, vel, volt, table, near, rows, cells):
    width, depth, span = volt.shape
    row = lax.broadcasted_iota(jnp.int32, (depth, span), 0)
    left = [None, None]
    sums = 4 * (width + depth)
    for x in range(width):
        here = volt[x]
        rise = vel[1, x]
        volt_up = pltpu.roll(here, depth - 1, 0)
        volt_next = pltpu.roll(here, span - 1, 1)
        speed_up = pltpu.roll(rise, depth - 1, 0)
        speed_next = pltpu.roll(vel[2, x], span - 1, 1)
        for s in range(2):
            value = conc[s, x]
            wall = face(value, pltpu.roll(value, depth - 1, 0), rise, speed_up, here, volt_up, s)
            wall = jnp.where(row == depth - 1, 0.0, wall)
            side = face(value, pltpu.roll(value, span - 1, 1), vel[2, x], speed_next, here, volt_next, s)
            total = (wall - pltpu.roll(wall, 1, 0)) + (side - pltpu.roll(side, 1, 1))
            if x:
                total = total - left[s]
            if x + 1 < width:
                left[s] = face(value, conc[s, x + 1], vel[0, x], vel[0, x + 1], here, volt[x + 1], s)
                total = total + left[s]
            place = s * width + x
            cells[place * depth : (place + 1) * depth] = value - FLUX_SCALE * total
            moved = drift(here, s)
            top = slice(depth - 1, depth)
            for part, edge in enumerate(
                (value[top], rise[top] + moved[top], value[0:1], rise[0:1] - moved[0:1])
            ):
                line = sums + part * 2 * width + place
                rows[line : line + 1] = edge
    solved = left_product(table[...], cells[...])
    near[...] = solved[: cells.shape[0]]
    rows[:sums] = solved[cells.shape[0] :]


def enter_kernel(decays_x, decays_z, rows_in, left_halo, conc, vel, volt, shares, gains, rows):
    width, depth, span = volt.shape
    row = lax.broadcasted_iota(jnp.int32, (depth, span), 0)
    for s in range(2):
        decay = decays_x[s]
        flux = face(left_halo[s], conc[s, 0], left_halo[2], vel[0, 0], left_halo[3], volt[0], s)
        taken = -FLUX_SCALE * flux
        gained = (decay - 1.0) * taken
        gains[s * depth : (s + 1) * depth] = gained
        for side, scale in enumerate((decay ** (width - 1) * (decay - 1.0), 1.0 / decay - 1.0)):
            start = (side * 2 + s) * depth
            rows[start : start + depth] = rows_in[start : start + depth] + scale * taken
            weight = jnp.zeros((depth, span), jnp.float32)
            for z in range(depth):
                weight = jnp.where(row == z, decays_z[s] ** (z if side else depth - 1 - z), weight)
            line = 4 * depth + (side * 2 + s) * width
            rows[line : line + 1] = rows_in[line : line + 1] + jnp.sum(weight * gained, axis=0, keepdims=True)
    part = shares.shape[1] // HALVES
    tiles = LANES // part
    for chunk in range(span // LANES):
        turned = rows[:, chunk * LANES : (chunk + 1) * LANES].T
        half, start = divmod(chunk * tiles, shares.shape[0])
        for k in range(tiles):
            shares[start + k, half * part : (half + 1) * part] = turned[k * part : (k + 1) * part]


def member_shift(team, teams):
    return lax.div(team, teams // 2) * (TEAM // 2)


def by_lane(values, lane, unit):
    return jnp.where(lax.bitwise_and(lane, unit) == 0, values[0], values[1])


def wall_kernel(decays, stream_steps, blocks, width, depth, parts, collect, solve, ends, sums, carry, lines):
    members, places, _ = parts.shape
    flat = members * places
    lane = lax.broadcasted_iota(jnp.int32, (places, LANES), 1)
    faces = 2 * width
    first = LANES // 2
    for m in range(TEAM):
        below = pltpu.roll(parts[m * blocks], LANES - 2 * faces, 1)
        below = below * pltpu.roll(below, LANES - faces, 1)
        for b in range(blocks):
            own = parts[m * blocks + b]
            meet = own
            if b + 1 < blocks:
                meet = meet + pltpu.roll(parts[m * blocks + b + 1], LANES - 2 * faces, 1)
            above = meet * pltpu.roll(meet, LANES - faces, 1)
            both = jnp.where(lane < first + faces, above, pltpu.roll(below, faces, 1))
            lines[m * blocks + b] = jnp.where(lane < first, own, both)
            below = above
    value = lines[...].reshape(flat, LANES)
    carry[...] = product(value, collect[...]).reshape(members, places, LANES)
    side = LANES // 2
    unit = LANES // 4
    entering = lane < side
    step = by_lane([decay**depth for decay in decays], lane, unit)
    mirrors = [decay ** (depth * blocks + 1) for decay in decays]
    mirror = by_lane(mirrors, lane, unit)
    scale = by_lane([-d / (1.0 - m * m) for d, m in zip(decays, mirrors)], lane, unit)
    weights = [
        jnp.where(
            entering,
            by_lane([decay ** (depth * b) for decay in decays], lane, unit),
            by_lane([decay ** (depth * (blocks - 1 - b)) for decay in decays], lane, unit),
        )
        for b in range(blocks)
    ]
    for m in range(TEAM):
        before = jnp.zeros((places, LANES), jnp.float32)
        after = jnp.zeros((places, LANES), jnp.float32)
        befores = []
        afters = [None] * blocks
        for b in range(blocks):
            befores.append(before)
            before = step * before + carry[m * blocks + b]
        for b in range(blocks - 1, -1, -1):
            afters[b] = after
            after = step * after + carry[m * blocks + b]
        total = jnp.where(entering, before, after)
        mirrored = scale * (pltpu.roll(total, side, 1) - mirror * total)
        for b in range(blocks):
            carry[m * blocks + b] = jnp.where(entering, befores[b], afters[b]) + weights[b] * mirrored
    full = jnp.concatenate([value, carry[...].reshape(flat, LANES)], axis=1)
    ends[...] = product(full, solve[...]).reshape(members, places, LANES)
    step = by_lane(stream_steps, lane, depth)
    entering = lane < 2 * depth
    pack = LANES // (4 * depth)
    shift = member_shift(lax.div(lax.axis_index("stream"), TEAM), sums.shape[0])
    first = [lax.rem(shift + m, TEAM) * blocks for m in range(TEAM)]
    for group in range(blocks // pack):
        packed = None
        for part in range(pack):
            b = group * pack + part
            own = [ends[first[m] + b] for m in range(TEAM)]
            before = own[0]
            after = own[-1]
            for m in range(1, TEAM):
                before = step * before + own[m]
                after = step * after + own[TEAM - 1 - m]
            both = jnp.where(entering, before, jnp.where(lane < 4 * depth, after, 0.0))
            packed = packed + pltpu.roll(both, part * 4 * depth, 1) if part else both
        for team in range(sums.shape[0]):
            sums[team, group] = packed


def stream_kernel(steps, blocks, depth, ends, sums, links):
    places = ends.shape[1]
    teams, groups = sums.shape[0], sums.shape[1]
    pack = blocks // groups
    part = links.shape[1]
    team = lax.div(lax.axis_index("stream"), TEAM)
    shift = member_shift(team, teams)
    first = [lax.rem(shift + m, TEAM) * blocks for m in range(TEAM)]
    lane = lax.broadcasted_iota(jnp.int32, (places, LANES), 1)
    entering = lax.bitwise_and(lane, 2 * depth) == 0
    step = by_lane(steps, lane, depth)
    leap = by_lane([value**TEAM for value in steps], lane, depth)
    closing = by_lane([1.0 / (1.0 - value ** (TEAM * teams)) for value in steps], lane, depth)
    for group in range(groups):
        before = sums[team, group]
        after = before
        for k in range(1, teams):
            before = leap * before + sums[lax.rem(team + k, teams), group]
            after = leap * after + sums[lax.rem(team + teams - k, teams), group]
        both = closing * jnp.where(entering, before, after)
        for slot in range(pack):
            b = group * pack + slot
            before = pltpu.roll(both, LANES - slot * 4 * depth, 1) if slot else both
            after = before
            afters = [None] * TEAM
            for m in range(TEAM - 1, -1, -1):
                afters[m] = after
                after = step * after + ends[first[m] + b]
            for m in range(TEAM):
                own = ends[first[m] + b]
                carry = jnp.where(lane < 4 * depth, jnp.where(entering, before, afters[m]), own)
                before = step * before + own
                halved = carry + pltpu.roll(pltpu.roll(carry, LANES // HALVES, 1), part, 0)
                links[first[m] + b] = halved[:part]


def home_kernel(near, gains, links, table, out, rows, carry, result, sent):
    _, width, depth, span = out.shape
    part = links.shape[1]
    lanes = LANES // HALVES
    for k in range(links.shape[0]):
        rows[k * part : (k + 1) * part] = links[k]
    for chunk in range(rows.shape[0] // LANES):
        turned = rows[chunk * LANES : (chunk + 1) * LANES].T
        for half in range(HALVES):
            start = half * (span // HALVES) + chunk * LANES
            carry[:, start : start + LANES] = turned[half * lanes : (half + 1) * lanes]
    copies = []
    for half in range(HALVES):
        cut = slice(half * (span // HALVES), (half + 1) * (span // HALVES))
        added = left_product(table[...], jnp.concatenate([gains[:, cut], carry[:, cut]], axis=0))
        solved = near[:, cut] + added
        for s in range(2):
            for x in range(width):
                start = (s * width + x) * depth
                result[half, s, x] = solved[start : start + depth]
        copies.append(pltpu.make_async_copy(result.at[half], out.at[:, :, :, cut], sent.at[half]))
        copies[-1].start()
    for copy in copies:
        copy.wait()


def per_device(concentration, velocity, potential):
    _, width, depth, span = concentration.shape
    stream = lax.axis_size("stream")
    wall = lax.axis_size("wall")
    stream_total = width * stream
    wall_total = depth * wall
    rates_x = (4.0 * width * width, float(stream_total * stream_total // 25))
    rates_z = (4.0 * depth * depth, float(wall_total * wall_total // 16))
    decays_x = [line_factors(rate)[0] for rate in rates_x]
    decays_z = [line_factors(rate)[0] for rate in rates_z]
    steps_x = [decay**width for decay in decays_x]
    collect_z, solve_z = wall_tables(rates_x, rates_z, width, depth)
    collect = collect_table(rates_x, rates_z, width, depth)
    near, home = home_tables(rates_x, rates_z, width, depth)

    (edge,) = call(
        border_kernel,
        [(4, depth, span)],
        (concentration, velocity, potential),
        [pltpu.SemaphoreType.DMA((4,))],
        source=pltpu.HBM,
        room=53 * 1024 + 848,
    )
    left_halo = lax.ppermute(edge, "stream", [(i, (i + 1) % stream) for i in range(stream)])

    members = TEAM * wall
    teams = stream // TEAM
    holders = [[t * TEAM + (m + t // (teams // 2) * (TEAM // 2)) % TEAM for m in range(TEAM)] for t in range(teams)]
    plane = [[b * stream + place for place in team for b in range(wall)] for team in holders]
    ranks = [[team[m] for team in holders] for m in range(TEAM)]
    swap = functools.partial(lax.all_to_all, split_axis=0, concat_axis=0, tiled=True)
    table = functools.partial(jnp.array, dtype=jnp.float32)
    places = span // members
    tile = (members, places, LANES)
    flat = (2 * width * depth, span)
    near, rows = call(
        predict_kernel,
        [flat, (LANES, span)],
        (concentration, velocity, potential, table(np.concatenate([near, collect]))),
        [pltpu.VMEM(flat, jnp.float32)],
    )
    shares, gains, rows = call(
        functools.partial(enter_kernel, decays_x, decays_z),
        [tile, (2 * depth, span), (LANES, span)],
        (rows, left_halo, concentration, velocity, potential),
        aliases={0: 2},
    )
    parts = swap(shares, ("wall", "stream"), axis_index_groups=plane)
    pack = LANES // (4 * depth)
    ends, sums = call(
        functools.partial(wall_kernel, decays_z, steps_x, wall, width, depth),
        [tile, (teams, wall // pack, places, LANES)],
        (parts, table(collect_z), table(solve_z)),
        [pltpu.VMEM(tile, jnp.float32), pltpu.VMEM(tile, jnp.float32)],
    )
    sums = swap(sums, "stream", axis_index_groups=ranks)
    (links,) = call(
        functools.partial(stream_kernel, steps_x, wall, depth),
        [(members, places // HALVES, LANES)],
        (ends, sums),
    )
    links = swap(links, ("wall", "stream"), axis_index_groups=plane)
    (out,) = call(
        home_kernel,
        [concentration.shape],
        (near, gains, links, table(home)),
        [
            pltpu.VMEM((span // HALVES, LANES), jnp.float32),
            pltpu.VMEM((LANES // HALVES, span), jnp.float32),
            pltpu.VMEM((HALVES, 2, width, depth, span // HALVES), jnp.float32),
            pltpu.SemaphoreType.DMA((HALVES,)),
        ],
        target=pltpu.HBM,
    )
    return out


def solution(mesh):
    return jax.shard_map(
        per_device,
        mesh=mesh,
        in_specs=(
            P(None, "stream", "wall", None),
            P(None, "stream", "wall", None),
            P("stream", "wall", None),
        ),
        out_specs=P(None, "stream", "wall", None),
        check_vma=False,
    )
```

```python
import functools

import jax
import jax.numpy as jnp
import numpy as np
from jax import lax
from jax.experimental import pallas as pl
from jax.experimental.pallas import tpu as pltpu
from jax.sharding import PartitionSpec as P

ADVECT_STEP = 0.2
DRIFT_RATES = (1.0, -0.5)
FLUX_SCALE = 0.25 * ADVECT_STEP
TEAM = 4
HALVES = 2
LANES = 128
SPREAD = 39


def line_factors(rate):
    base = 1.0 + 2.0 * rate
    root = np.sqrt(1.0 + 4.0 * rate)
    return float(2.0 * rate / (base + root)), float(1.0 / root)


def block_tables(decay, gain, cells):
    place = np.arange(cells)
    local = gain * decay ** np.abs(place[:, None] - place[None, :])
    collect = np.stack([decay ** (cells - 1 - place), decay**place], axis=1)
    spread = gain * np.stack([decay ** (place + 1), decay ** (cells - place)])
    return local, collect, spread


def collect_table(rates_x, rates_z, width, depth):
    table = np.zeros((4 * depth + 4 * width, 2, width, depth))
    stream_sums = table[: 4 * depth].reshape(2, 2, depth, 2, width, depth)
    wall_sums = table[4 * depth :].reshape(2, 2, width, 2, width, depth)
    for s in range(2):
        _, gather_x, _ = block_tables(*line_factors(rates_x[s]), width)
        _, gather_z, _ = block_tables(*line_factors(rates_z[s]), depth)
        for z in range(depth):
            stream_sums[:, s, z, s, :, z] = gather_x.T
        for x in range(width):
            wall_sums[:, s, x, s, x, :] = gather_z.T
    return table.reshape(-1, 2 * width * depth)


def wall_tables(rates_x, rates_z, width, depth):
    unit = LANES // 4
    sums = 4 * (depth + width)
    collect = np.zeros((LANES, 2, 2, unit))
    solve = np.zeros((2, LANES, LANES))
    sums_in = collect[: 4 * depth].reshape(2, 2, depth, 2, 2, unit)
    ends_in = collect[4 * depth : sums].reshape(2, 2, width, 2, 2, unit)
    flux_in = collect[sums : sums + 4 * width].reshape(2, 2, width, 2, 2, unit)
    near = solve[0, : 4 * depth, : 4 * depth].reshape(2, 2, depth, 2, 2, depth)
    spread = solve[1, :, : 4 * depth].reshape(2, 2, unit, 2, 2, depth)
    moved = solve[1, :, 4 * depth : sums].reshape(2, 2, unit, 2, 2, width)
    flux_near = solve[0, sums : sums + 4 * width, : 4 * depth].reshape(2, 2, width, 2, 2, depth)
    flux_moved = solve[0, sums : sums + 4 * width, 4 * depth : sums].reshape(2, 2, width, 2, 2, width)
    for s in range(2):
        _, gather_x, _ = block_tables(*line_factors(rates_x[s]), width)
        local, gather_z, hand = block_tables(*line_factors(rates_z[s]), depth)
        decay = line_factors(rates_z[s])[0]
        for side in range(2):
            sums_in[side, s, :, :, s, width + side] = gather_z
            near[side, s, :, side, s, :] = local
            spread[:, s, width + side, side, s, :] = hand
            for x in range(width):
                ends_in[side, s, x, side, s, x] = 1.0
                moved[side, s, x, side, s, x] = 1.0
        for end, cell, size in ((0, depth - 1, -FLUX_SCALE), (1, 0, FLUX_SCALE)):
            for x in range(width):
                flux_in[end, s, x, :, s, x] = size * gather_z[cell]
                flux_moved[end, s, x, 1 - end, s, x] = size / decay
                for side in range(2):
                    flux_in[end, s, x, :, s, width + side] = size * gather_x[x, side] * gather_z[cell]
                    flux_near[end, s, x, side, s, :] = size * gather_x[x, side] * local[cell]
    return collect.reshape(LANES, LANES), solve.reshape(2 * LANES, LANES)


def home_tables(rates_x, rates_z, width, depth):
    cells = 2 * width * depth
    near = np.zeros((2, width, depth, 2, width, depth))
    stream_spread = np.zeros((2, width, depth, 2, 2, depth))
    wall_spread = np.zeros((2, width, depth, 2, 2, width))
    for s in range(2):
        local_x, _, hand_x = block_tables(*line_factors(rates_x[s]), width)
        local_z, _, hand_z = block_tables(*line_factors(rates_z[s]), depth)
        near[s, :, :, s, :, :] = np.einsum("xa,zb->xzab", local_x, local_z)
        stream_spread[s, :, :, :, s, :] = np.einsum("ex,zb->xzeb", hand_x, np.eye(depth))
        wall_spread[s, :, :, :, s, :] = np.einsum("xa,ez->xzea", local_x, hand_z)
    parts = (near[:, :, :, :, 0], stream_spread, wall_spread)
    return near.reshape(cells, cells), np.concatenate([part.reshape(cells, -1) for part in parts], axis=1)


def call(kernel, outs, ins, scratch=(), aliases=None, source=pltpu.VMEM, target=pltpu.VMEM, room=32 * 1024):
    return pl.pallas_call(
        kernel,
        out_shape=[jax.ShapeDtypeStruct(shape, jnp.float32) for shape in outs],
        in_specs=[pl.BlockSpec(memory_space=source)] * len(ins),
        out_specs=[pl.BlockSpec(memory_space=target)] * len(outs),
        scratch_shapes=list(scratch),
        input_output_aliases=aliases or {},
        compiler_params=pltpu.CompilerParams(vmem_limit_bytes=room * 1024),
    )(*ins)


def drift(volt, species):
    return (2.0 * DRIFT_RATES[species]) * volt


def face(conc_low, conc_high, speed_low, speed_high, volt_low, volt_high, species):
    return (conc_low + conc_high) * (speed_low + speed_high - drift(volt_high - volt_low, species))


def border_kernel(conc, vel, volt, edge, arrived):
    last = volt.shape[0] - 1
    copies = [
        pltpu.make_async_copy(source, edge.at[place], arrived.at[place])
        for place, source in enumerate((conc.at[0, last], conc.at[1, last], vel.at[0, last], volt.at[last]))
    ]
    for copy in copies:
        copy.start()
    for copy in copies:
        copy.wait()


def split(values):
    high = values.astype(jnp.bfloat16)
    return high, (values - high.astype(jnp.float32)).astype(jnp.bfloat16)


def product(values, table):
    high, low = split(values)
    table_high, table_low = split(table)
    dot = functools.partial(jnp.dot, preferred_element_type=jnp.float32)
    wide = table.shape[1]
    beside = jnp.concatenate([table_high, table_low], axis=1)
    if values.shape[1] <= LANES:
        under = jnp.concatenate([table_high, jnp.zeros_like(table_low)], axis=1)
        both = dot(jnp.concatenate([high, low], axis=1), jnp.concatenate([beside, under], axis=0))
        return both[:, :wide] + both[:, wide:]
    both = dot(high, beside)
    return both[:, :wide] + (both[:, wide:] + dot(low, table_high))


def left_product(table, values):
    high, low = split(values)
    table_high, table_low = split(table)
    dot = functools.partial(jnp.dot, preferred_element_type=jnp.float32)
    tall = table.shape[0]
    above = jnp.concatenate([table_high, table_low], axis=0)
    under = jnp.concatenate([table_high, jnp.zeros_like(table_low)], axis=0)
    both = dot(jnp.concatenate([above, under], axis=1), jnp.concatenate([high, low], axis=0))
    return both[:tall] + both[tall:]


def predict_kernel(conc, vel, volt, table, near, rows, cells):
    width, depth, span = volt.shape
    row = lax.broadcasted_iota(jnp.int32, (depth, span), 0)
    left = [None, None]
    sums = 4 * (width + depth)
    for x in range(width):
        here = volt[x]
        rise = vel[1, x]
        volt_up = pltpu.roll(here, depth - 1, 0)
        volt_next = pltpu.roll(here, span - 1, 1)
        speed_up = pltpu.roll(rise, depth - 1, 0)
        speed_next = pltpu.roll(vel[2, x], span - 1, 1)
        for s in range(2):
            value = conc[s, x]
            wall = face(value, pltpu.roll(value, depth - 1, 0), rise, speed_up, here, volt_up, s)
            wall = jnp.where(row == depth - 1, 0.0, wall)
            side = face(value, pltpu.roll(value, span - 1, 1), vel[2, x], speed_next, here, volt_next, s)
            total = (wall - pltpu.roll(wall, 1, 0)) + (side - pltpu.roll(side, 1, 1))
            if x:
                total = total - left[s]
            if x + 1 < width:
                left[s] = face(value, conc[s, x + 1], vel[0, x], vel[0, x + 1], here, volt[x + 1], s)
                total = total + left[s]
            place = s * width + x
            cells[place * depth : (place + 1) * depth] = value - FLUX_SCALE * total
            moved = drift(here, s)
            top = slice(depth - 1, depth)
            for part, edge in enumerate(
                (value[top], rise[top] + moved[top], value[0:1], rise[0:1] - moved[0:1])
            ):
                line = sums + part * 2 * width + place
                rows[line : line + 1] = edge
    solved = left_product(table[...], cells[...])
    near[...] = solved[: cells.shape[0]]
    rows[:sums] = solved[cells.shape[0] :]


def enter_kernel(decays_x, decays_z, rows_in, left_halo, conc, vel, volt, shares, gains, rows):
    width, depth, span = volt.shape
    row = lax.broadcasted_iota(jnp.int32, (depth, span), 0)
    for s in range(2):
        decay = decays_x[s]
        flux = face(left_halo[s], conc[s, 0], left_halo[2], vel[0, 0], left_halo[3], volt[0], s)
        taken = -FLUX_SCALE * flux
        gained = (decay - 1.0) * taken
        gains[s * depth : (s + 1) * depth] = gained
        for side, scale in enumerate((decay ** (width - 1) * (decay - 1.0), 1.0 / decay - 1.0)):
            start = (side * 2 + s) * depth
            rows[start : start + depth] = rows_in[start : start + depth] + scale * taken
            weight = jnp.zeros((depth, span), jnp.float32)
            for z in range(depth):
                weight = jnp.where(row == z, decays_z[s] ** (z if side else depth - 1 - z), weight)
            line = 4 * depth + (side * 2 + s) * width
            rows[line : line + 1] = rows_in[line : line + 1] + jnp.sum(weight * gained, axis=0, keepdims=True)
    part = shares.shape[1] // HALVES
    tiles = LANES // part
    for chunk in range(span // LANES):
        turned = rows[:, chunk * LANES : (chunk + 1) * LANES].T
        half, start = divmod(chunk * tiles, shares.shape[0])
        for k in range(tiles):
            shares[start + k, half * part : (half + 1) * part] = turned[k * part : (k + 1) * part]


def member_shift(team, teams):
    return lax.div(team, teams // 2) * (TEAM // 2)


def list_place(member, block, blocks):
    total = TEAM * blocks
    return (member * blocks + block) * pow(SPREAD, -1, total) % total


def shifted_place(member, block, blocks, shift):
    return lax.rem(list_place(member, block, blocks) + shift * blocks, TEAM * blocks)


def by_lane(values, lane, unit):
    return jnp.where(lax.bitwise_and(lane, unit) == 0, values[0], values[1])


def wall_kernel(decays, stream_steps, blocks, width, depth, parts, collect, solve, ends, sums, carry, lines):
    members, places, _ = parts.shape
    flat = members * places
    lane = lax.broadcasted_iota(jnp.int32, (places, LANES), 1)
    faces = 2 * width
    first = LANES // 2
    for m in range(TEAM):
        below = pltpu.roll(parts[list_place(m, 0, blocks)], LANES - 2 * faces, 1)
        below = below * pltpu.roll(below, LANES - faces, 1)
        for b in range(blocks):
            own = parts[list_place(m, b, blocks)]
            meet = own
            if b + 1 < blocks:
                meet = meet + pltpu.roll(parts[list_place(m, b + 1, blocks)], LANES - 2 * faces, 1)
            above = meet * pltpu.roll(meet, LANES - faces, 1)
            both = jnp.where(lane < first + faces, above, pltpu.roll(below, faces, 1))
            lines[list_place(m, b, blocks)] = jnp.where(lane < first, own, both)
            below = above
    value = lines[...].reshape(flat, LANES)
    carry[...] = product(value, collect[...]).reshape(members, places, LANES)
    side = LANES // 2
    unit = LANES // 4
    entering = lane < side
    step = by_lane([decay**depth for decay in decays], lane, unit)
    mirrors = [decay ** (depth * blocks + 1) for decay in decays]
    mirror = by_lane(mirrors, lane, unit)
    scale = by_lane([-d / (1.0 - m * m) for d, m in zip(decays, mirrors)], lane, unit)
    weights = [
        jnp.where(
            entering,
            by_lane([decay ** (depth * b) for decay in decays], lane, unit),
            by_lane([decay ** (depth * (blocks - 1 - b)) for decay in decays], lane, unit),
        )
        for b in range(blocks)
    ]
    for m in range(TEAM):
        before = jnp.zeros((places, LANES), jnp.float32)
        after = jnp.zeros((places, LANES), jnp.float32)
        befores = []
        afters = [None] * blocks
        for b in range(blocks):
            befores.append(before)
            before = step * before + carry[list_place(m, b, blocks)]
        for b in range(blocks - 1, -1, -1):
            afters[b] = after
            after = step * after + carry[list_place(m, b, blocks)]
        total = jnp.where(entering, before, after)
        mirrored = scale * (pltpu.roll(total, side, 1) - mirror * total)
        for b in range(blocks):
            carry[list_place(m, b, blocks)] = jnp.where(entering, befores[b], afters[b]) + weights[b] * mirrored
    full = jnp.concatenate([value, carry[...].reshape(flat, LANES)], axis=1)
    ends[...] = product(full, solve[...]).reshape(members, places, LANES)
    step = by_lane(stream_steps, lane, depth)
    entering = lane < 2 * depth
    pack = LANES // (4 * depth)
    shift = member_shift(lax.div(lax.axis_index("stream"), TEAM), sums.shape[0])
    for group in range(blocks // pack):
        packed = None
        for part in range(pack):
            b = group * pack + part
            own = [ends[shifted_place(m, b, blocks, shift)] for m in range(TEAM)]
            before = own[0]
            after = own[-1]
            for m in range(1, TEAM):
                before = step * before + own[m]
                after = step * after + own[TEAM - 1 - m]
            both = jnp.where(entering, before, jnp.where(lane < 4 * depth, after, 0.0))
            packed = packed + pltpu.roll(both, part * 4 * depth, 1) if part else both
        for team in range(sums.shape[0]):
            sums[team, group] = packed


def stream_kernel(steps, blocks, depth, ends, sums, links):
    places = ends.shape[1]
    teams, groups = sums.shape[0], sums.shape[1]
    pack = blocks // groups
    part = links.shape[1]
    team = lax.div(lax.axis_index("stream"), TEAM)
    shift = member_shift(team, teams)
    lane = lax.broadcasted_iota(jnp.int32, (places, LANES), 1)
    entering = lax.bitwise_and(lane, 2 * depth) == 0
    step = by_lane(steps, lane, depth)
    leap = by_lane([value**TEAM for value in steps], lane, depth)
    closing = by_lane([1.0 / (1.0 - value ** (TEAM * teams)) for value in steps], lane, depth)
    for group in range(groups):
        before = sums[team, group]
        after = before
        for k in range(1, teams):
            before = leap * before + sums[lax.rem(team + k, teams), group]
            after = leap * after + sums[lax.rem(team + teams - k, teams), group]
        both = closing * jnp.where(entering, before, after)
        for slot in range(pack):
            b = group * pack + slot
            before = pltpu.roll(both, LANES - slot * 4 * depth, 1) if slot else both
            after = before
            afters = [None] * TEAM
            for m in range(TEAM - 1, -1, -1):
                afters[m] = after
                after = step * after + ends[shifted_place(m, b, blocks, shift)]
            for m in range(TEAM):
                own = ends[shifted_place(m, b, blocks, shift)]
                carry = jnp.where(lane < 4 * depth, jnp.where(entering, before, afters[m]), own)
                before = step * before + own
                halved = carry + pltpu.roll(pltpu.roll(carry, LANES // HALVES, 1), part, 0)
                links[shifted_place(m, b, blocks, shift)] = halved[:part]


def home_kernel(near, gains, links, table, out, rows, carry, result, sent):
    _, width, depth, span = out.shape
    part = links.shape[1]
    lanes = LANES // HALVES
    for k in range(links.shape[0]):
        rows[k * part : (k + 1) * part] = links[k]
    for chunk in range(rows.shape[0] // LANES):
        turned = rows[chunk * LANES : (chunk + 1) * LANES].T
        for half in range(HALVES):
            start = half * (span // HALVES) + chunk * LANES
            carry[:, start : start + LANES] = turned[half * lanes : (half + 1) * lanes]
    copies = []
    for half in range(HALVES):
        cut = slice(half * (span // HALVES), (half + 1) * (span // HALVES))
        added = left_product(table[...], jnp.concatenate([gains[:, cut], carry[:, cut]], axis=0))
        solved = near[:, cut] + added
        for s in range(2):
            for x in range(width):
                start = (s * width + x) * depth
                result[half, s, x] = solved[start : start + depth]
        copies.append(pltpu.make_async_copy(result.at[half], out.at[:, :, :, cut], sent.at[half]))
        copies[-1].start()
    for copy in copies:
        copy.wait()


def per_device(concentration, velocity, potential):
    _, width, depth, span = concentration.shape
    stream = lax.axis_size("stream")
    wall = lax.axis_size("wall")
    stream_total = width * stream
    wall_total = depth * wall
    rates_x = (4.0 * width * width, float(stream_total * stream_total // 25))
    rates_z = (4.0 * depth * depth, float(wall_total * wall_total // 16))
    decays_x = [line_factors(rate)[0] for rate in rates_x]
    decays_z = [line_factors(rate)[0] for rate in rates_z]
    steps_x = [decay**width for decay in decays_x]
    collect_z, solve_z = wall_tables(rates_x, rates_z, width, depth)
    collect = collect_table(rates_x, rates_z, width, depth)
    near, home = home_tables(rates_x, rates_z, width, depth)

    (edge,) = call(
        border_kernel,
        [(4, depth, span)],
        (concentration, velocity, potential),
        [pltpu.SemaphoreType.DMA((4,))],
        source=pltpu.HBM,
        room=53 * 1024 + 848,
    )
    left_halo = lax.ppermute(edge, "stream", [(i, (i + 1) % stream) for i in range(stream)])

    members = TEAM * wall
    teams = stream // TEAM
    holders = [[t * TEAM + (m + t // (teams // 2) * (TEAM // 2)) % TEAM for m in range(TEAM)] for t in range(teams)]
    listed = [[b * stream + place for place in team for b in range(wall)] for team in holders]
    plane = [[team[k * SPREAD % members] for k in range(members)] for team in listed]
    ranks = [[team[m] for team in holders] for m in range(TEAM)]
    swap = functools.partial(lax.all_to_all, split_axis=0, concat_axis=0, tiled=True)
    table = functools.partial(jnp.array, dtype=jnp.float32)
    places = span // members
    tile = (members, places, LANES)
    flat = (2 * width * depth, span)
    near, rows = call(
        predict_kernel,
        [flat, (LANES, span)],
        (concentration, velocity, potential, table(np.concatenate([near, collect]))),
        [pltpu.VMEM(flat, jnp.float32)],
    )
    shares, gains, rows = call(
        functools.partial(enter_kernel, decays_x, decays_z),
        [tile, (2 * depth, span), (LANES, span)],
        (rows, left_halo, concentration, velocity, potential),
        aliases={0: 2},
    )
    parts = swap(shares, ("wall", "stream"), axis_index_groups=plane)
    pack = LANES // (4 * depth)
    ends, sums = call(
        functools.partial(wall_kernel, decays_z, steps_x, wall, width, depth),
        [tile, (teams, wall // pack, places, LANES)],
        (parts, table(collect_z), table(solve_z)),
        [pltpu.VMEM(tile, jnp.float32), pltpu.VMEM(tile, jnp.float32)],
    )
    sums = swap(sums, "stream", axis_index_groups=ranks)
    (links,) = call(
        functools.partial(stream_kernel, steps_x, wall, depth),
        [(members, places // HALVES, LANES)],
        (ends, sums),
    )
    links = swap(links, ("wall", "stream"), axis_index_groups=plane)
    (out,) = call(
        home_kernel,
        [concentration.shape],
        (near, gains, links, table(home)),
        [
            pltpu.VMEM((span // HALVES, LANES), jnp.float32),
            pltpu.VMEM((LANES // HALVES, span), jnp.float32),
            pltpu.VMEM((HALVES, 2, width, depth, span // HALVES), jnp.float32),
            pltpu.SemaphoreType.DMA((HALVES,)),
        ],
        target=pltpu.HBM,
    )
    return out


def solution(mesh):
    return jax.shard_map(
        per_device,
        mesh=mesh,
        in_specs=(
            P(None, "stream", "wall", None),
            P(None, "stream", "wall", None),
            P("stream", "wall", None),
        ),
        out_specs=P(None, "stream", "wall", None),
        check_vma=False,
    )
```

```python
import functools

import jax
import jax.numpy as jnp
import numpy as np
from jax import lax
from jax.experimental import pallas as pl
from jax.experimental.pallas import tpu as pltpu
from jax.sharding import PartitionSpec as P

ADVECT_STEP = 0.2
DRIFT_RATES = (1.0, -0.5)
FLUX_SCALE = 0.25 * ADVECT_STEP
TEAM = 4
HALVES = 2
LANES = 128
SPREAD = 39


def line_factors(rate):
    base = 1.0 + 2.0 * rate
    root = np.sqrt(1.0 + 4.0 * rate)
    return float(2.0 * rate / (base + root)), float(1.0 / root)


def block_tables(decay, gain, cells):
    place = np.arange(cells)
    local = gain * decay ** np.abs(place[:, None] - place[None, :])
    collect = np.stack([decay ** (cells - 1 - place), decay**place], axis=1)
    spread = gain * np.stack([decay ** (place + 1), decay ** (cells - place)])
    return local, collect, spread


def collect_table(rates_x, rates_z, width, depth):
    table = np.zeros((4 * depth + 4 * width, 2, width, depth))
    stream_sums = table[: 4 * depth].reshape(2, 2, depth, 2, width, depth)
    wall_sums = table[4 * depth :].reshape(2, 2, width, 2, width, depth)
    for s in range(2):
        _, gather_x, _ = block_tables(*line_factors(rates_x[s]), width)
        _, gather_z, _ = block_tables(*line_factors(rates_z[s]), depth)
        for z in range(depth):
            stream_sums[:, s, z, s, :, z] = gather_x.T
        for x in range(width):
            wall_sums[:, s, x, s, x, :] = gather_z.T
    return table.reshape(-1, 2 * width * depth)


def wall_tables(rates_x, rates_z, width, depth):
    unit = LANES // 4
    sums = 4 * (depth + width)
    collect = np.zeros((LANES, 2, 2, unit))
    solve = np.zeros((2, LANES, LANES))
    sums_in = collect[: 4 * depth].reshape(2, 2, depth, 2, 2, unit)
    ends_in = collect[4 * depth : sums].reshape(2, 2, width, 2, 2, unit)
    flux_in = collect[sums : sums + 4 * width].reshape(2, 2, width, 2, 2, unit)
    near = solve[0, : 4 * depth, : 4 * depth].reshape(2, 2, depth, 2, 2, depth)
    spread = solve[1, :, : 4 * depth].reshape(2, 2, unit, 2, 2, depth)
    moved = solve[1, :, 4 * depth : sums].reshape(2, 2, unit, 2, 2, width)
    flux_near = solve[0, sums : sums + 4 * width, : 4 * depth].reshape(2, 2, width, 2, 2, depth)
    flux_moved = solve[0, sums : sums + 4 * width, 4 * depth : sums].reshape(2, 2, width, 2, 2, width)
    for s in range(2):
        _, gather_x, _ = block_tables(*line_factors(rates_x[s]), width)
        local, gather_z, hand = block_tables(*line_factors(rates_z[s]), depth)
        decay = line_factors(rates_z[s])[0]
        for side in range(2):
            sums_in[side, s, :, :, s, width + side] = gather_z
            near[side, s, :, side, s, :] = local
            spread[:, s, width + side, side, s, :] = hand
            for x in range(width):
                ends_in[side, s, x, side, s, x] = 1.0
                moved[side, s, x, side, s, x] = 1.0
        for end, cell, size in ((0, depth - 1, -FLUX_SCALE), (1, 0, FLUX_SCALE)):
            for x in range(width):
                flux_in[end, s, x, :, s, x] = size * gather_z[cell]
                flux_moved[end, s, x, 1 - end, s, x] = size / decay
                for side in range(2):
                    flux_in[end, s, x, :, s, width + side] = size * gather_x[x, side] * gather_z[cell]
                    flux_near[end, s, x, side, s, :] = size * gather_x[x, side] * local[cell]
    return collect.reshape(LANES, LANES), solve.reshape(2 * LANES, LANES)


def home_tables(rates_x, rates_z, width, depth):
    cells = 2 * width * depth
    near = np.zeros((2, width, depth, 2, width, depth))
    stream_spread = np.zeros((2, width, depth, 2, 2, depth))
    wall_spread = np.zeros((2, width, depth, 2, 2, width))
    for s in range(2):
        local_x, _, hand_x = block_tables(*line_factors(rates_x[s]), width)
        local_z, _, hand_z = block_tables(*line_factors(rates_z[s]), depth)
        near[s, :, :, s, :, :] = np.einsum("xa,zb->xzab", local_x, local_z)
        stream_spread[s, :, :, :, s, :] = np.einsum("ex,zb->xzeb", hand_x, np.eye(depth))
        wall_spread[s, :, :, :, s, :] = np.einsum("xa,ez->xzea", local_x, hand_z)
    ends = []
    for x in (0, width - 1):
        parts = (near[:, :, :, :, x], stream_spread, wall_spread)
        ends.append(np.concatenate([part.reshape(cells, -1) for part in parts], axis=1))
    return near.reshape(cells, cells), np.stack(ends)


def call(kernel, outs, ins, scratch=(), aliases=None, source=pltpu.VMEM, target=pltpu.VMEM, room=32 * 1024):
    return pl.pallas_call(
        kernel,
        out_shape=[jax.ShapeDtypeStruct(shape, jnp.float32) for shape in outs],
        in_specs=[pl.BlockSpec(memory_space=source)] * len(ins),
        out_specs=[pl.BlockSpec(memory_space=target)] * len(outs),
        scratch_shapes=list(scratch),
        input_output_aliases=aliases or {},
        compiler_params=pltpu.CompilerParams(vmem_limit_bytes=room * 1024),
    )(*ins)


def drift(volt, species):
    return (2.0 * DRIFT_RATES[species]) * volt


def face(conc_low, conc_high, speed_low, speed_high, volt_low, volt_high, species):
    return (conc_low + conc_high) * (speed_low + speed_high - drift(volt_high - volt_low, species))


def mirrored():
    return lax.rem(lax.axis_index("wall"), 2)


def border_kernel(conc, vel, volt, edge, arrived):
    last = (volt.shape[0] - 1) * (1 - mirrored())
    copies = [
        pltpu.make_async_copy(source, edge.at[place], arrived.at[place])
        for place, source in enumerate((conc.at[0, last], conc.at[1, last], vel.at[0, last], volt.at[last]))
    ]
    for copy in copies:
        copy.start()
    for copy in copies:
        copy.wait()


def split(values):
    high = values.astype(jnp.bfloat16)
    return high, (values - high.astype(jnp.float32)).astype(jnp.bfloat16)


def product(values, table):
    high, low = split(values)
    table_high, table_low = split(table)
    dot = functools.partial(jnp.dot, preferred_element_type=jnp.float32)
    wide = table.shape[1]
    beside = jnp.concatenate([table_high, table_low], axis=1)
    if values.shape[1] <= LANES:
        under = jnp.concatenate([table_high, jnp.zeros_like(table_low)], axis=1)
        both = dot(jnp.concatenate([high, low], axis=1), jnp.concatenate([beside, under], axis=0))
        return both[:, :wide] + both[:, wide:]
    both = dot(high, beside)
    return both[:, :wide] + (both[:, wide:] + dot(low, table_high))


def left_product(table, values):
    high, low = split(values)
    table_high, table_low = split(table)
    dot = functools.partial(jnp.dot, preferred_element_type=jnp.float32)
    tall = table.shape[0]
    above = jnp.concatenate([table_high, table_low], axis=0)
    under = jnp.concatenate([table_high, jnp.zeros_like(table_low)], axis=0)
    both = dot(jnp.concatenate([above, under], axis=1), jnp.concatenate([high, low], axis=0))
    return both[:tall] + both[tall:]


def predict_kernel(conc, vel, volt, table, near, rows, cells):
    width, depth, span = volt.shape
    row = lax.broadcasted_iota(jnp.int32, (depth, span), 0)
    left = [None, None]
    sums = 4 * (width + depth)
    for x in range(width):
        here = volt[x]
        rise = vel[1, x]
        volt_up = pltpu.roll(here, depth - 1, 0)
        volt_next = pltpu.roll(here, span - 1, 1)
        speed_up = pltpu.roll(rise, depth - 1, 0)
        speed_next = pltpu.roll(vel[2, x], span - 1, 1)
        for s in range(2):
            value = conc[s, x]
            wall = face(value, pltpu.roll(value, depth - 1, 0), rise, speed_up, here, volt_up, s)
            wall = jnp.where(row == depth - 1, 0.0, wall)
            side = face(value, pltpu.roll(value, span - 1, 1), vel[2, x], speed_next, here, volt_next, s)
            total = (wall - pltpu.roll(wall, 1, 0)) + (side - pltpu.roll(side, 1, 1))
            if x:
                total = total - left[s]
            if x + 1 < width:
                left[s] = face(value, conc[s, x + 1], vel[0, x], vel[0, x + 1], here, volt[x + 1], s)
                total = total + left[s]
            place = s * width + x
            cells[place * depth : (place + 1) * depth] = value - FLUX_SCALE * total
            moved = drift(here, s)
            top = slice(depth - 1, depth)
            for part, edge in enumerate(
                (value[top], rise[top] + moved[top], value[0:1], rise[0:1] - moved[0:1])
            ):
                line = sums + part * 2 * width + place
                rows[line : line + 1] = edge
    solved = left_product(table[...], cells[...])
    near[...] = solved[: cells.shape[0]]
    rows[:sums] = solved[cells.shape[0] :]


def enter_kernel(decays_x, decays_z, rows_in, halo, conc, vel, volt, shares, gains, rows):
    width, depth, span = volt.shape
    row = lax.broadcasted_iota(jnp.int32, (depth, span), 0)
    odd = mirrored()
    even = 1 - odd
    place = odd * (width - 1)
    sign = (even - odd).astype(jnp.float32)
    for s in range(2):
        decay = decays_x[s]
        fall = sign * drift(volt[place] - halo[3], s)
        flux = (conc[s, place] + halo[s]) * (vel[0, place] + halo[2] - fall)
        taken = (-FLUX_SCALE * sign) * flux
        gained = (decay - 1.0) * taken
        gains[s * depth : (s + 1) * depth] = gained
        scales = (decay ** (width - 1) * (decay - 1.0), 1.0 / decay - 1.0)
        for side in range(2):
            scale = jnp.where(odd == side, jnp.float32(scales[0]), jnp.float32(scales[1]))
            start = (side * 2 + s) * depth
            rows[start : start + depth] = rows_in[start : start + depth] + scale * taken
            weight = jnp.zeros((depth, span), jnp.float32)
            for z in range(depth):
                weight = jnp.where(row == z, decays_z[s] ** (z if side else depth - 1 - z), weight)
            total = jnp.sum(weight * gained, axis=0, keepdims=True)
            for x, here in ((0, even), (width - 1, odd)):
                line = 4 * depth + (side * 2 + s) * width + x
                rows[line : line + 1] = rows_in[line : line + 1] + here.astype(jnp.float32) * total
    part = shares.shape[1] // HALVES
    tiles = LANES // part
    for chunk in range(span // LANES):
        turned = rows[:, chunk * LANES : (chunk + 1) * LANES].T
        half, start = divmod(chunk * tiles, shares.shape[0])
        for k in range(tiles):
            shares[start + k, half * part : (half + 1) * part] = turned[k * part : (k + 1) * part]


def member_shift(team, teams):
    return lax.div(team, teams // 2) * (TEAM // 2)


def list_place(member, block, blocks):
    total = TEAM * blocks
    return (member * blocks + block) * pow(SPREAD, -1, total) % total


def shifted_place(member, block, blocks, shift):
    return lax.rem(list_place(member, block, blocks) + shift * blocks, TEAM * blocks)


def by_lane(values, lane, unit):
    return jnp.where(lax.bitwise_and(lane, unit) == 0, values[0], values[1])


def wall_kernel(decays, stream_steps, blocks, width, depth, parts, collect, solve, ends, sums, carry, lines):
    members, places, _ = parts.shape
    flat = members * places
    lane = lax.broadcasted_iota(jnp.int32, (places, LANES), 1)
    faces = 2 * width
    first = LANES // 2
    for m in range(TEAM):
        below = pltpu.roll(parts[list_place(m, 0, blocks)], LANES - 2 * faces, 1)
        below = below * pltpu.roll(below, LANES - faces, 1)
        for b in range(blocks):
            own = parts[list_place(m, b, blocks)]
            meet = own
            if b + 1 < blocks:
                meet = meet + pltpu.roll(parts[list_place(m, b + 1, blocks)], LANES - 2 * faces, 1)
            above = meet * pltpu.roll(meet, LANES - faces, 1)
            both = jnp.where(lane < first + faces, above, pltpu.roll(below, faces, 1))
            lines[list_place(m, b, blocks)] = jnp.where(lane < first, own, both)
            below = above
    value = lines[...].reshape(flat, LANES)
    carry[...] = product(value, collect[...]).reshape(members, places, LANES)
    side = LANES // 2
    unit = LANES // 4
    entering = lane < side
    step = by_lane([decay**depth for decay in decays], lane, unit)
    mirrors = [decay ** (depth * blocks + 1) for decay in decays]
    mirror = by_lane(mirrors, lane, unit)
    scale = by_lane([-d / (1.0 - m * m) for d, m in zip(decays, mirrors)], lane, unit)
    weights = [
        jnp.where(
            entering,
            by_lane([decay ** (depth * b) for decay in decays], lane, unit),
            by_lane([decay ** (depth * (blocks - 1 - b)) for decay in decays], lane, unit),
        )
        for b in range(blocks)
    ]
    for m in range(TEAM):
        before = jnp.zeros((places, LANES), jnp.float32)
        after = jnp.zeros((places, LANES), jnp.float32)
        befores = []
        afters = [None] * blocks
        for b in range(blocks):
            befores.append(before)
            before = step * before + carry[list_place(m, b, blocks)]
        for b in range(blocks - 1, -1, -1):
            afters[b] = after
            after = step * after + carry[list_place(m, b, blocks)]
        total = jnp.where(entering, before, after)
        mirrored = scale * (pltpu.roll(total, side, 1) - mirror * total)
        for b in range(blocks):
            carry[list_place(m, b, blocks)] = jnp.where(entering, befores[b], afters[b]) + weights[b] * mirrored
    full = jnp.concatenate([value, carry[...].reshape(flat, LANES)], axis=1)
    ends[...] = product(full, solve[...]).reshape(members, places, LANES)
    step = by_lane(stream_steps, lane, depth)
    entering = lane < 2 * depth
    pack = LANES // (4 * depth)
    shift = member_shift(lax.div(lax.axis_index("stream"), TEAM), sums.shape[0])
    for group in range(blocks // pack):
        packed = None
        for part in range(pack):
            b = group * pack + part
            own = [ends[shifted_place(m, b, blocks, shift)] for m in range(TEAM)]
            before = own[0]
            after = own[-1]
            for m in range(1, TEAM):
                before = step * before + own[m]
                after = step * after + own[TEAM - 1 - m]
            both = jnp.where(entering, before, jnp.where(lane < 4 * depth, after, 0.0))
            packed = packed + pltpu.roll(both, part * 4 * depth, 1) if part else both
        for team in range(sums.shape[0]):
            sums[team, group] = packed


def stream_kernel(steps, blocks, depth, ends, sums, links):
    places = ends.shape[1]
    teams, groups = sums.shape[0], sums.shape[1]
    pack = blocks // groups
    part = links.shape[1]
    team = lax.div(lax.axis_index("stream"), TEAM)
    shift = member_shift(team, teams)
    lane = lax.broadcasted_iota(jnp.int32, (places, LANES), 1)
    entering = lax.bitwise_and(lane, 2 * depth) == 0
    step = by_lane(steps, lane, depth)
    leap = by_lane([value**TEAM for value in steps], lane, depth)
    closing = by_lane([1.0 / (1.0 - value ** (TEAM * teams)) for value in steps], lane, depth)
    for group in range(groups):
        before = sums[team, group]
        after = before
        for k in range(1, teams):
            before = leap * before + sums[lax.rem(team + k, teams), group]
            after = leap * after + sums[lax.rem(team + teams - k, teams), group]
        both = closing * jnp.where(entering, before, after)
        for slot in range(pack):
            b = group * pack + slot
            before = pltpu.roll(both, LANES - slot * 4 * depth, 1) if slot else both
            after = before
            afters = [None] * TEAM
            for m in range(TEAM - 1, -1, -1):
                afters[m] = after
                after = step * after + ends[shifted_place(m, b, blocks, shift)]
            for m in range(TEAM):
                own = ends[shifted_place(m, b, blocks, shift)]
                carry = jnp.where(lane < 4 * depth, jnp.where(entering, before, afters[m]), own)
                before = step * before + own
                halved = carry + pltpu.roll(pltpu.roll(carry, LANES // HALVES, 1), part, 0)
                links[shifted_place(m, b, blocks, shift)] = halved[:part]


def home_kernel(near, gains, links, table, out, rows, carry, result, sent):
    _, width, depth, span = out.shape
    part = links.shape[1]
    lanes = LANES // HALVES
    for k in range(links.shape[0]):
        rows[k * part : (k + 1) * part] = links[k]
    for chunk in range(rows.shape[0] // LANES):
        turned = rows[chunk * LANES : (chunk + 1) * LANES].T
        for half in range(HALVES):
            start = half * (span // HALVES) + chunk * LANES
            carry[:, start : start + LANES] = turned[half * lanes : (half + 1) * lanes]
    copies = []
    for half in range(HALVES):
        cut = slice(half * (span // HALVES), (half + 1) * (span // HALVES))
        added = left_product(table[mirrored()], jnp.concatenate([gains[:, cut], carry[:, cut]], axis=0))
        solved = near[:, cut] + added
        for s in range(2):
            for x in range(width):
                start = (s * width + x) * depth
                result[half, s, x] = solved[start : start + depth]
        copies.append(pltpu.make_async_copy(result.at[half], out.at[:, :, :, cut], sent.at[half]))
        copies[-1].start()
    for copy in copies:
        copy.wait()


def per_device(concentration, velocity, potential):
    _, width, depth, span = concentration.shape
    stream = lax.axis_size("stream")
    wall = lax.axis_size("wall")
    stream_total = width * stream
    wall_total = depth * wall
    rates_x = (4.0 * width * width, float(stream_total * stream_total // 25))
    rates_z = (4.0 * depth * depth, float(wall_total * wall_total // 16))
    decays_x = [line_factors(rate)[0] for rate in rates_x]
    decays_z = [line_factors(rate)[0] for rate in rates_z]
    steps_x = [decay**width for decay in decays_x]
    collect_z, solve_z = wall_tables(rates_x, rates_z, width, depth)
    collect = collect_table(rates_x, rates_z, width, depth)
    near, home = home_tables(rates_x, rates_z, width, depth)

    (edge,) = call(
        border_kernel,
        [(4, depth, span)],
        (concentration, velocity, potential),
        [pltpu.SemaphoreType.DMA((4,))],
        source=pltpu.HBM,
        room=53 * 1024 + 848,
    )
    pairs = [
        (row * stream + i, row * stream + (i + (-1 if row % 2 else 1)) % stream) for row in range(wall) for i in range(stream)
    ]
    halo = lax.ppermute(edge, ("wall", "stream"), pairs)

    members = TEAM * wall
    teams = stream // TEAM
    holders = [[t * TEAM + (m + t // (teams // 2) * (TEAM // 2)) % TEAM for m in range(TEAM)] for t in range(teams)]
    listed = [[b * stream + place for place in team for b in range(wall)] for team in holders]
    plane = [[team[k * SPREAD % members] for k in range(members)] for team in listed]
    ranks = [[team[m] for team in holders] for m in range(TEAM)]
    swap = functools.partial(lax.all_to_all, split_axis=0, concat_axis=0, tiled=True)
    table = functools.partial(jnp.array, dtype=jnp.float32)
    places = span // members
    tile = (members, places, LANES)
    flat = (2 * width * depth, span)
    near, rows = call(
        predict_kernel,
        [flat, (LANES, span)],
        (concentration, velocity, potential, table(np.concatenate([near, collect]))),
        [pltpu.VMEM(flat, jnp.float32)],
    )
    shares, gains, rows = call(
        functools.partial(enter_kernel, decays_x, decays_z),
        [tile, (2 * depth, span), (LANES, span)],
        (rows, halo, concentration, velocity, potential),
        aliases={0: 2},
    )
    parts = swap(shares, ("wall", "stream"), axis_index_groups=plane)
    pack = LANES // (4 * depth)
    ends, sums = call(
        functools.partial(wall_kernel, decays_z, steps_x, wall, width, depth),
        [tile, (teams, wall // pack, places, LANES)],
        (parts, table(collect_z), table(solve_z)),
        [pltpu.VMEM(tile, jnp.float32), pltpu.VMEM(tile, jnp.float32)],
    )
    sums = swap(sums, "stream", axis_index_groups=ranks)
    (links,) = call(
        functools.partial(stream_kernel, steps_x, wall, depth),
        [(members, places // HALVES, LANES)],
        (ends, sums),
    )
    links = swap(links, ("wall", "stream"), axis_index_groups=plane)
    (out,) = call(
        home_kernel,
        [concentration.shape],
        (near, gains, links, table(home)),
        [
            pltpu.VMEM((span // HALVES, LANES), jnp.float32),
            pltpu.VMEM((LANES // HALVES, span), jnp.float32),
            pltpu.VMEM((HALVES, 2, width, depth, span // HALVES), jnp.float32),
            pltpu.SemaphoreType.DMA((HALVES,)),
        ],
        target=pltpu.HBM,
    )
    return out


def solution(mesh):
    return jax.shard_map(
        per_device,
        mesh=mesh,
        in_specs=(
            P(None, "stream", "wall", None),
            P(None, "stream", "wall", None),
            P("stream", "wall", None),
        ),
        out_specs=P(None, "stream", "wall", None),
        check_vma=False,
    )
```

```python
import functools

import jax
import jax.numpy as jnp
import numpy as np
from jax import lax
from jax.experimental import pallas as pl
from jax.experimental.pallas import tpu as pltpu
from jax.sharding import PartitionSpec as P

ADVECT_STEP = 0.2
DRIFT_RATES = (1.0, -0.5)
FLUX_SCALE = 0.25 * ADVECT_STEP
TEAM = 4
HALVES = 2
LANES = 128
SPREAD = 39


def line_factors(rate):
    base = 1.0 + 2.0 * rate
    root = np.sqrt(1.0 + 4.0 * rate)
    return float(2.0 * rate / (base + root)), float(1.0 / root)


def block_tables(decay, gain, cells):
    place = np.arange(cells)
    local = gain * decay ** np.abs(place[:, None] - place[None, :])
    collect = np.stack([decay ** (cells - 1 - place), decay**place], axis=1)
    spread = gain * np.stack([decay ** (place + 1), decay ** (cells - place)])
    return local, collect, spread


def collect_table(rates_x, rates_z, width, depth):
    table = np.zeros((4 * depth + 4 * width, 2, width, depth))
    stream_sums = table[: 4 * depth].reshape(2, 2, depth, 2, width, depth)
    wall_sums = table[4 * depth :].reshape(2, 2, width, 2, width, depth)
    for s in range(2):
        _, gather_x, _ = block_tables(*line_factors(rates_x[s]), width)
        _, gather_z, _ = block_tables(*line_factors(rates_z[s]), depth)
        for z in range(depth):
            stream_sums[:, s, z, s, :, z] = gather_x.T
        for x in range(width):
            wall_sums[:, s, x, s, x, :] = gather_z.T
    return table.reshape(-1, 2 * width * depth)


def wall_tables(rates_x, rates_z, width, depth):
    unit = LANES // 4
    sums = 4 * (depth + width)
    collect = np.zeros((LANES, 2, 2, unit))
    solve = np.zeros((2, LANES, LANES))
    sums_in = collect[: 4 * depth].reshape(2, 2, depth, 2, 2, unit)
    ends_in = collect[4 * depth : sums].reshape(2, 2, width, 2, 2, unit)
    flux_in = collect[sums : sums + 4 * width].reshape(2, 2, width, 2, 2, unit)
    near = solve[0, : 4 * depth, : 4 * depth].reshape(2, 2, depth, 2, 2, depth)
    spread = solve[1, :, : 4 * depth].reshape(2, 2, unit, 2, 2, depth)
    moved = solve[1, :, 4 * depth : sums].reshape(2, 2, unit, 2, 2, width)
    flux_near = solve[0, sums : sums + 4 * width, : 4 * depth].reshape(2, 2, width, 2, 2, depth)
    flux_moved = solve[0, sums : sums + 4 * width, 4 * depth : sums].reshape(2, 2, width, 2, 2, width)
    for s in range(2):
        _, gather_x, _ = block_tables(*line_factors(rates_x[s]), width)
        local, gather_z, hand = block_tables(*line_factors(rates_z[s]), depth)
        decay = line_factors(rates_z[s])[0]
        for side in range(2):
            sums_in[side, s, :, :, s, width + side] = gather_z
            near[side, s, :, side, s, :] = local
            spread[:, s, width + side, side, s, :] = hand
            for x in range(width):
                ends_in[side, s, x, side, s, x] = 1.0
                moved[side, s, x, side, s, x] = 1.0
        for end, cell, size in ((0, depth - 1, -FLUX_SCALE), (1, 0, FLUX_SCALE)):
            for x in range(width):
                flux_in[end, s, x, :, s, x] = size * gather_z[cell]
                flux_moved[end, s, x, 1 - end, s, x] = size / decay
                for side in range(2):
                    flux_in[end, s, x, :, s, width + side] = size * gather_x[x, side] * gather_z[cell]
                    flux_near[end, s, x, side, s, :] = size * gather_x[x, side] * local[cell]
    return collect.reshape(LANES, LANES), solve.reshape(2 * LANES, LANES)


def home_tables(rates_x, rates_z, width, depth):
    cells = 2 * width * depth
    near = np.zeros((2, width, depth, 2, width, depth))
    stream_spread = np.zeros((2, width, depth, 2, 2, depth))
    wall_spread = np.zeros((2, width, depth, 2, 2, width))
    for s in range(2):
        local_x, _, hand_x = block_tables(*line_factors(rates_x[s]), width)
        local_z, _, hand_z = block_tables(*line_factors(rates_z[s]), depth)
        near[s, :, :, s, :, :] = np.einsum("xa,zb->xzab", local_x, local_z)
        stream_spread[s, :, :, :, s, :] = np.einsum("ex,zb->xzeb", hand_x, np.eye(depth))
        wall_spread[s, :, :, :, s, :] = np.einsum("xa,ez->xzea", local_x, hand_z)
    parts = (near[:, :, :, :, 0], stream_spread, wall_spread)
    return near.reshape(cells, cells), np.concatenate([part.reshape(cells, -1) for part in parts], axis=1)


def call(kernel, outs, ins, scratch=(), aliases=None, source=pltpu.VMEM, target=pltpu.VMEM, room=32 * 1024):
    return pl.pallas_call(
        kernel,
        out_shape=[jax.ShapeDtypeStruct(shape, jnp.float32) for shape in outs],
        in_specs=[pl.BlockSpec(memory_space=source)] * len(ins),
        out_specs=[pl.BlockSpec(memory_space=target)] * len(outs),
        scratch_shapes=list(scratch),
        input_output_aliases=aliases or {},
        compiler_params=pltpu.CompilerParams(vmem_limit_bytes=room * 1024),
    )(*ins)


def drift(volt, species):
    return (2.0 * DRIFT_RATES[species]) * volt


def face(conc_low, conc_high, speed_low, speed_high, volt_low, volt_high, species):
    return (conc_low + conc_high) * (speed_low + speed_high - drift(volt_high - volt_low, species))


def border_kernel(conc, vel, volt, edge, arrived):
    last = volt.shape[0] - 1
    copies = [
        pltpu.make_async_copy(source, edge.at[place], arrived.at[place])
        for place, source in enumerate((conc.at[0, last], conc.at[1, last], vel.at[0, last], volt.at[last]))
    ]
    for copy in copies:
        copy.start()
    for copy in copies:
        copy.wait()


def split(values):
    high = values.astype(jnp.bfloat16)
    return high, (values - high.astype(jnp.float32)).astype(jnp.bfloat16)


def product(values, table):
    high, low = split(values)
    table_high, table_low = split(table)
    dot = functools.partial(jnp.dot, preferred_element_type=jnp.float32)
    wide = table.shape[1]
    beside = jnp.concatenate([table_high, table_low], axis=1)
    if values.shape[1] <= LANES:
        under = jnp.concatenate([table_high, jnp.zeros_like(table_low)], axis=1)
        both = dot(jnp.concatenate([high, low], axis=1), jnp.concatenate([beside, under], axis=0))
        return both[:, :wide] + both[:, wide:]
    both = dot(high, beside)
    return both[:, :wide] + (both[:, wide:] + dot(low, table_high))


def left_product(table, values):
    high, low = split(values)
    table_high, table_low = split(table)
    dot = functools.partial(jnp.dot, preferred_element_type=jnp.float32)
    tall = table.shape[0]
    above = jnp.concatenate([table_high, table_low], axis=0)
    under = jnp.concatenate([table_high, jnp.zeros_like(table_low)], axis=0)
    both = dot(jnp.concatenate([above, under], axis=1), jnp.concatenate([high, low], axis=0))
    return both[:tall] + both[tall:]


def predict_kernel(conc, vel, volt, table, near, rows, cells):
    width, depth, span = volt.shape
    row = lax.broadcasted_iota(jnp.int32, (depth, span), 0)
    left = [None, None]
    sums = 4 * (width + depth)
    for x in range(width):
        here = volt[x]
        rise = vel[1, x]
        volt_up = pltpu.roll(here, depth - 1, 0)
        volt_next = pltpu.roll(here, span - 1, 1)
        speed_up = pltpu.roll(rise, depth - 1, 0)
        speed_next = pltpu.roll(vel[2, x], span - 1, 1)
        for s in range(2):
            value = conc[s, x]
            wall = face(value, pltpu.roll(value, depth - 1, 0), rise, speed_up, here, volt_up, s)
            wall = jnp.where(row == depth - 1, 0.0, wall)
            side = face(value, pltpu.roll(value, span - 1, 1), vel[2, x], speed_next, here, volt_next, s)
            total = (wall - pltpu.roll(wall, 1, 0)) + (side - pltpu.roll(side, 1, 1))
            if x:
                total = total - left[s]
            if x + 1 < width:
                left[s] = face(value, conc[s, x + 1], vel[0, x], vel[0, x + 1], here, volt[x + 1], s)
                total = total + left[s]
            place = s * width + x
            cells[place * depth : (place + 1) * depth] = value - FLUX_SCALE * total
            moved = drift(here, s)
            top = slice(depth - 1, depth)
            for part, edge in enumerate(
                (value[top], rise[top] + moved[top], value[0:1], rise[0:1] - moved[0:1])
            ):
                line = sums + part * 2 * width + place
                rows[line : line + 1] = edge
    solved = left_product(table[...], cells[...])
    near[...] = solved[: cells.shape[0]]
    rows[:sums] = solved[cells.shape[0] :]


def enter_kernel(decays_x, decays_z, rows_in, left_halo, conc, vel, volt, shares, gains, rows):
    width, depth, span = volt.shape
    row = lax.broadcasted_iota(jnp.int32, (depth, span), 0)
    for s in range(2):
        decay = decays_x[s]
        flux = face(left_halo[s], conc[s, 0], left_halo[2], vel[0, 0], left_halo[3], volt[0], s)
        taken = -FLUX_SCALE * flux
        gained = (decay - 1.0) * taken
        gains[s * depth : (s + 1) * depth] = gained
        for side, scale in enumerate((decay ** (width - 1) * (decay - 1.0), 1.0 / decay - 1.0)):
            start = (side * 2 + s) * depth
            rows[start : start + depth] = rows_in[start : start + depth] + scale * taken
            weight = jnp.zeros((depth, span), jnp.float32)
            for z in range(depth):
                weight = jnp.where(row == z, decays_z[s] ** (z if side else depth - 1 - z), weight)
            line = 4 * depth + (side * 2 + s) * width
            rows[line : line + 1] = rows_in[line : line + 1] + jnp.sum(weight * gained, axis=0, keepdims=True)
    part = shares.shape[1] // HALVES
    tiles = LANES // part
    for chunk in range(span // LANES):
        turned = rows[:, chunk * LANES : (chunk + 1) * LANES].T
        half, start = divmod(chunk * tiles, shares.shape[0])
        for k in range(tiles):
            shares[start + k, half * part : (half + 1) * part] = turned[k * part : (k + 1) * part]


def member_shift(team, teams):
    return lax.div(team, teams // 2) * (TEAM // 2)


def list_place(member, block, blocks):
    total = TEAM * blocks
    return (member * blocks + block) * pow(SPREAD, -1, total) % total


def shifted_place(member, block, blocks, shift):
    return lax.rem(list_place(member, block, blocks) + shift * blocks, TEAM * blocks)


def by_lane(values, lane, unit):
    return jnp.where(lax.bitwise_and(lane, unit) == 0, values[0], values[1])


def wall_kernel(decays, stream_steps, blocks, width, depth, parts, collect, solve, ends, sums, carry, lines):
    members, places, _ = parts.shape
    flat = members * places
    lane = lax.broadcasted_iota(jnp.int32, (places, LANES), 1)
    faces = 2 * width
    first = LANES // 2
    for m in range(TEAM):
        below = pltpu.roll(parts[list_place(m, 0, blocks)], LANES - 2 * faces, 1)
        below = below * pltpu.roll(below, LANES - faces, 1)
        for b in range(blocks):
            own = parts[list_place(m, b, blocks)]
            meet = own
            if b + 1 < blocks:
                meet = meet + pltpu.roll(parts[list_place(m, b + 1, blocks)], LANES - 2 * faces, 1)
            above = meet * pltpu.roll(meet, LANES - faces, 1)
            both = jnp.where(lane < first + faces, above, pltpu.roll(below, faces, 1))
            lines[list_place(m, b, blocks)] = jnp.where(lane < first, own, both)
            below = above
    value = lines[...].reshape(flat, LANES)
    carry[...] = product(value, collect[...]).reshape(members, places, LANES)
    side = LANES // 2
    unit = LANES // 4
    entering = lane < side
    step = by_lane([decay**depth for decay in decays], lane, unit)
    mirrors = [decay ** (depth * blocks + 1) for decay in decays]
    mirror = by_lane(mirrors, lane, unit)
    scale = by_lane([-d / (1.0 - m * m) for d, m in zip(decays, mirrors)], lane, unit)
    weights = [
        jnp.where(
            entering,
            by_lane([decay ** (depth * b) for decay in decays], lane, unit),
            by_lane([decay ** (depth * (blocks - 1 - b)) for decay in decays], lane, unit),
        )
        for b in range(blocks)
    ]
    for m in range(TEAM):
        before = jnp.zeros((places, LANES), jnp.float32)
        after = jnp.zeros((places, LANES), jnp.float32)
        befores = []
        afters = [None] * blocks
        for b in range(blocks):
            befores.append(before)
            before = step * before + carry[list_place(m, b, blocks)]
        for b in range(blocks - 1, -1, -1):
            afters[b] = after
            after = step * after + carry[list_place(m, b, blocks)]
        total = jnp.where(entering, before, after)
        mirrored = scale * (pltpu.roll(total, side, 1) - mirror * total)
        for b in range(blocks):
            carry[list_place(m, b, blocks)] = jnp.where(entering, befores[b], afters[b]) + weights[b] * mirrored
    full = jnp.concatenate([value, carry[...].reshape(flat, LANES)], axis=1)
    result = product(full, solve[...])
    ends[...] = result.reshape(members, places, LANES)
    step = by_lane(stream_steps, lane, depth)
    entering = lane < 2 * depth
    pack = LANES // (4 * depth)
    shift = member_shift(lax.div(lax.axis_index("stream"), TEAM), sums.shape[0])
    weights = []
    for m in range(TEAM):
        options = [by_lane([value**k for value in stream_steps], lane, depth) for k in range(TEAM)]
        plain = jnp.where(entering, options[TEAM - 1 - m], options[m])
        turned = (m + TEAM // 2) % TEAM
        weights.append(jnp.where(shift == 0, plain, jnp.where(entering, options[TEAM - 1 - turned], options[turned])))
    for group in range(blocks // pack):
        packed = None
        for part in range(pack):
            b = group * pack + part
            both = None
            for m in range(TEAM):
                place = list_place(m, b, blocks) * places
                term = weights[m] * result[place : place + places]
                both = term if both is None else both + term
            both = jnp.where(lane < 4 * depth, both, 0.0)
            packed = packed + pltpu.roll(both, part * 4 * depth, 1) if part else both
        for team in range(sums.shape[0]):
            sums[team, group] = packed


def stream_kernel(steps, blocks, depth, ends, sums, links):
    places = ends.shape[1]
    teams, groups = sums.shape[0], sums.shape[1]
    pack = blocks // groups
    part = links.shape[1]
    team = lax.div(lax.axis_index("stream"), TEAM)
    shift = member_shift(team, teams)
    lane = lax.broadcasted_iota(jnp.int32, (places, LANES), 1)
    entering = lax.bitwise_and(lane, 2 * depth) == 0
    step = by_lane(steps, lane, depth)
    leap = by_lane([value**TEAM for value in steps], lane, depth)
    closing = by_lane([1.0 / (1.0 - value ** (TEAM * teams)) for value in steps], lane, depth)
    for group in range(groups):
        before = sums[team, group]
        after = before
        for k in range(1, teams):
            before = leap * before + sums[lax.rem(team + k, teams), group]
            after = leap * after + sums[lax.rem(team + teams - k, teams), group]
        both = closing * jnp.where(entering, before, after)
        for slot in range(pack):
            b = group * pack + slot
            before = pltpu.roll(both, LANES - slot * 4 * depth, 1) if slot else both
            after = before
            afters = [None] * TEAM
            for m in range(TEAM - 1, -1, -1):
                afters[m] = after
                after = step * after + ends[shifted_place(m, b, blocks, shift)]
            for m in range(TEAM):
                own = ends[shifted_place(m, b, blocks, shift)]
                carry = jnp.where(lane < 4 * depth, jnp.where(entering, before, afters[m]), own)
                before = step * before + own
                halved = carry + pltpu.roll(pltpu.roll(carry, LANES // HALVES, 1), part, 0)
                links[shifted_place(m, b, blocks, shift)] = halved[:part]


def home_kernel(near, gains, links, table, out, rows, solved, sent):
    _, width, depth, span = out.shape
    part = links.shape[1]
    lanes = LANES // HALVES
    tiles = LANES // part
    copies = []
    for chunk in range(links.shape[0] // tiles):
        for k in range(tiles):
            rows[k * part : (k + 1) * part] = links[chunk * tiles + k]
        turned = rows[...].T
        cuts = [slice(half * (span // HALVES) + chunk * LANES, half * (span // HALVES) + (chunk + 1) * LANES) for half in range(HALVES)]
        carry = jnp.concatenate([turned[half * lanes : (half + 1) * lanes] for half in range(HALVES)], axis=1)
        gained = jnp.concatenate([gains[:, cut] for cut in cuts], axis=1)
        added = left_product(table[...], jnp.concatenate([gained, carry], axis=0))
        for half, cut in enumerate(cuts):
            place = chunk * HALVES + half
            total = near[:, cut] + added[:, half * LANES : (half + 1) * LANES]
            for s in range(2):
                for x in range(width):
                    start = (s * width + x) * depth
                    solved[place, s, x] = total[start : start + depth]
            copies.append(pltpu.make_async_copy(solved.at[place], out.at[:, :, :, cut], sent.at[place]))
            copies[-1].start()
    for copy in copies:
        copy.wait()


def per_device(concentration, velocity, potential):
    _, width, depth, span = concentration.shape
    stream = lax.axis_size("stream")
    wall = lax.axis_size("wall")
    stream_total = width * stream
    wall_total = depth * wall
    rates_x = (4.0 * width * width, float(stream_total * stream_total // 25))
    rates_z = (4.0 * depth * depth, float(wall_total * wall_total // 16))
    decays_x = [line_factors(rate)[0] for rate in rates_x]
    decays_z = [line_factors(rate)[0] for rate in rates_z]
    steps_x = [decay**width for decay in decays_x]
    collect_z, solve_z = wall_tables(rates_x, rates_z, width, depth)
    collect = collect_table(rates_x, rates_z, width, depth)
    near, home = home_tables(rates_x, rates_z, width, depth)

    (edge,) = call(
        border_kernel,
        [(4, depth, span)],
        (concentration, velocity, potential),
        [pltpu.SemaphoreType.DMA((4,))],
        source=pltpu.HBM,
        room=53 * 1024 + 848,
    )
    left_halo = lax.ppermute(edge, "stream", [(i, (i + 1) % stream) for i in range(stream)])

    members = TEAM * wall
    teams = stream // TEAM
    holders = [[t * TEAM + (m + t // (teams // 2) * (TEAM // 2)) % TEAM for m in range(TEAM)] for t in range(teams)]
    listed = [[b * stream + place for place in team for b in range(wall)] for team in holders]
    plane = [[team[k * SPREAD % members] for k in range(members)] for team in listed]
    ranks = [[team[m] for team in holders] for m in range(TEAM)]
    swap = functools.partial(lax.all_to_all, split_axis=0, concat_axis=0, tiled=True)
    table = functools.partial(jnp.array, dtype=jnp.float32)
    places = span // members
    tile = (members, places, LANES)
    flat = (2 * width * depth, span)
    near, rows = call(
        predict_kernel,
        [flat, (LANES, span)],
        (concentration, velocity, potential, table(np.concatenate([near, collect]))),
        [pltpu.VMEM(flat, jnp.float32)],
    )
    shares, gains, rows = call(
        functools.partial(enter_kernel, decays_x, decays_z),
        [tile, (2 * depth, span), (LANES, span)],
        (rows, left_halo, concentration, velocity, potential),
        aliases={0: 2},
    )
    parts = swap(shares, ("wall", "stream"), axis_index_groups=plane)
    pack = LANES // (4 * depth)
    ends, sums = call(
        functools.partial(wall_kernel, decays_z, steps_x, wall, width, depth),
        [tile, (teams, wall // pack, places, LANES)],
        (parts, table(collect_z), table(solve_z)),
        [pltpu.VMEM(tile, jnp.float32), pltpu.VMEM(tile, jnp.float32)],
    )
    sums = swap(sums, "stream", axis_index_groups=ranks)
    (links,) = call(
        functools.partial(stream_kernel, steps_x, wall, depth),
        [(members, places // HALVES, LANES)],
        (ends, sums),
    )
    links = swap(links, ("wall", "stream"), axis_index_groups=plane)
    (out,) = call(
        home_kernel,
        [concentration.shape],
        (near, gains, links, table(home)),
        [
            pltpu.VMEM((LANES, LANES), jnp.float32),
            pltpu.VMEM((span // LANES, 2, width, depth, LANES), jnp.float32),
            pltpu.SemaphoreType.DMA((span // LANES,)),
        ],
        target=pltpu.HBM,
    )
    return out


def solution(mesh):
    return jax.shard_map(
        per_device,
        mesh=mesh,
        in_specs=(
            P(None, "stream", "wall", None),
            P(None, "stream", "wall", None),
            P("stream", "wall", None),
        ),
        out_specs=P(None, "stream", "wall", None),
        check_vma=False,
    )
```

```python
import functools

import jax
import jax.numpy as jnp
import numpy as np
from jax import lax
from jax.experimental import pallas as pl
from jax.experimental.pallas import tpu as pltpu
from jax.sharding import PartitionSpec as P

ADVECT_STEP = 0.2
DRIFT_RATES = (1.0, -0.5)
FLUX_SCALE = 0.25 * ADVECT_STEP
TEAM = 4
HALVES = 2
LANES = 128
SPREAD = 39


def line_factors(rate):
    base = 1.0 + 2.0 * rate
    root = np.sqrt(1.0 + 4.0 * rate)
    return float(2.0 * rate / (base + root)), float(1.0 / root)


def block_tables(decay, gain, cells):
    place = np.arange(cells)
    local = gain * decay ** np.abs(place[:, None] - place[None, :])
    collect = np.stack([decay ** (cells - 1 - place), decay**place], axis=1)
    spread = gain * np.stack([decay ** (place + 1), decay ** (cells - place)])
    return local, collect, spread


def collect_table(rates_x, rates_z, width, depth):
    table = np.zeros((4 * depth + 4 * width, 2, width, depth))
    stream_sums = table[: 4 * depth].reshape(2, 2, depth, 2, width, depth)
    wall_sums = table[4 * depth :].reshape(2, 2, width, 2, width, depth)
    for s in range(2):
        _, gather_x, _ = block_tables(*line_factors(rates_x[s]), width)
        _, gather_z, _ = block_tables(*line_factors(rates_z[s]), depth)
        for z in range(depth):
            stream_sums[:, s, z, s, :, z] = gather_x.T
        for x in range(width):
            wall_sums[:, s, x, s, x, :] = gather_z.T
    return table.reshape(-1, 2 * width * depth)


def wall_tables(rates_x, rates_z, width, depth):
    unit = LANES // 4
    sums = 4 * (depth + width)
    collect = np.zeros((LANES, 2, 2, unit))
    solve = np.zeros((2, LANES, LANES))
    sums_in = collect[: 4 * depth].reshape(2, 2, depth, 2, 2, unit)
    ends_in = collect[4 * depth : sums].reshape(2, 2, width, 2, 2, unit)
    flux_in = collect[sums : sums + 4 * width].reshape(2, 2, width, 2, 2, unit)
    near = solve[0, : 4 * depth, : 4 * depth].reshape(2, 2, depth, 2, 2, depth)
    spread = solve[1, :, : 4 * depth].reshape(2, 2, unit, 2, 2, depth)
    moved = solve[1, :, 4 * depth : sums].reshape(2, 2, unit, 2, 2, width)
    flux_near = solve[0, sums : sums + 4 * width, : 4 * depth].reshape(2, 2, width, 2, 2, depth)
    flux_moved = solve[0, sums : sums + 4 * width, 4 * depth : sums].reshape(2, 2, width, 2, 2, width)
    for s in range(2):
        _, gather_x, _ = block_tables(*line_factors(rates_x[s]), width)
        local, gather_z, hand = block_tables(*line_factors(rates_z[s]), depth)
        decay = line_factors(rates_z[s])[0]
        for side in range(2):
            sums_in[side, s, :, :, s, width + side] = gather_z
            near[side, s, :, side, s, :] = local
            spread[:, s, width + side, side, s, :] = hand
            for x in range(width):
                ends_in[side, s, x, side, s, x] = 1.0
                moved[side, s, x, side, s, x] = 1.0
        for end, cell, size in ((0, depth - 1, -FLUX_SCALE), (1, 0, FLUX_SCALE)):
            for x in range(width):
                flux_in[end, s, x, :, s, x] = size * gather_z[cell]
                flux_moved[end, s, x, 1 - end, s, x] = size / decay
                for side in range(2):
                    flux_in[end, s, x, :, s, width + side] = size * gather_x[x, side] * gather_z[cell]
                    flux_near[end, s, x, side, s, :] = size * gather_x[x, side] * local[cell]
    return collect.reshape(LANES, LANES), solve.reshape(2 * LANES, LANES)


def home_tables(rates_x, rates_z, width, depth):
    cells = 2 * width * depth
    near = np.zeros((2, width, depth, 2, width, depth))
    stream_spread = np.zeros((2, width, depth, 2, 2, depth))
    wall_spread = np.zeros((2, width, depth, 2, 2, width))
    for s in range(2):
        local_x, _, hand_x = block_tables(*line_factors(rates_x[s]), width)
        local_z, _, hand_z = block_tables(*line_factors(rates_z[s]), depth)
        near[s, :, :, s, :, :] = np.einsum("xa,zb->xzab", local_x, local_z)
        stream_spread[s, :, :, :, s, :] = np.einsum("ex,zb->xzeb", hand_x, np.eye(depth))
        wall_spread[s, :, :, :, s, :] = np.einsum("xa,ez->xzea", local_x, hand_z)
    parts = (near[:, :, :, :, 0], stream_spread, wall_spread)
    return near.reshape(cells, cells), np.concatenate([part.reshape(cells, -1) for part in parts], axis=1)


def call(kernel, outs, ins, scratch=(), aliases=None, source=pltpu.VMEM, target=pltpu.VMEM, room=32 * 1024):
    return pl.pallas_call(
        kernel,
        out_shape=[jax.ShapeDtypeStruct(shape, jnp.float32) for shape in outs],
        in_specs=[pl.BlockSpec(memory_space=source)] * len(ins),
        out_specs=[pl.BlockSpec(memory_space=target)] * len(outs),
        scratch_shapes=list(scratch),
        input_output_aliases=aliases or {},
        compiler_params=pltpu.CompilerParams(vmem_limit_bytes=room * 1024),
    )(*ins)


def drift(volt, species):
    return (2.0 * DRIFT_RATES[species]) * volt


def face(conc_low, conc_high, speed_low, speed_high, volt_low, volt_high, species):
    return (conc_low + conc_high) * (speed_low + speed_high - drift(volt_high - volt_low, species))


def border_kernel(conc, vel, volt, edge, arrived):
    last = volt.shape[0] - 1
    copies = [
        pltpu.make_async_copy(source, edge.at[place], arrived.at[place])
        for place, source in enumerate((conc.at[0, last], conc.at[1, last], vel.at[0, last], volt.at[last]))
    ]
    for copy in copies:
        copy.start()
    for copy in copies:
        copy.wait()


def split(values):
    high = values.astype(jnp.bfloat16)
    return high, (values - high.astype(jnp.float32)).astype(jnp.bfloat16)


def product(values, table):
    high, low = split(values)
    table_high, table_low = split(table)
    dot = functools.partial(jnp.dot, preferred_element_type=jnp.float32)
    wide = table.shape[1]
    beside = jnp.concatenate([table_high, table_low], axis=1)
    if values.shape[1] <= LANES:
        under = jnp.concatenate([table_high, jnp.zeros_like(table_low)], axis=1)
        both = dot(jnp.concatenate([high, low], axis=1), jnp.concatenate([beside, under], axis=0))
        return both[:, :wide] + both[:, wide:]
    both = dot(high, beside)
    return both[:, :wide] + (both[:, wide:] + dot(low, table_high))


def left_product(table, values):
    high, low = split(values)
    table_high, table_low = split(table)
    dot = functools.partial(jnp.dot, preferred_element_type=jnp.float32)
    tall = table.shape[0]
    above = jnp.concatenate([table_high, table_low], axis=0)
    under = jnp.concatenate([table_high, jnp.zeros_like(table_low)], axis=0)
    both = dot(jnp.concatenate([above, under], axis=1), jnp.concatenate([high, low], axis=0))
    return both[:tall] + both[tall:]


def predict_kernel(conc, vel, volt, table, near, rows, cells):
    width, depth, span = volt.shape
    row = lax.broadcasted_iota(jnp.int32, (depth, span), 0)
    left = [None, None]
    sums = 4 * (width + depth)
    for x in range(width):
        here = volt[x]
        rise = vel[1, x]
        volt_up = pltpu.roll(here, depth - 1, 0)
        volt_next = pltpu.roll(here, span - 1, 1)
        speed_up = pltpu.roll(rise, depth - 1, 0)
        speed_next = pltpu.roll(vel[2, x], span - 1, 1)
        for s in range(2):
            value = conc[s, x]
            wall = face(value, pltpu.roll(value, depth - 1, 0), rise, speed_up, here, volt_up, s)
            wall = jnp.where(row == depth - 1, 0.0, wall)
            side = face(value, pltpu.roll(value, span - 1, 1), vel[2, x], speed_next, here, volt_next, s)
            total = (wall - pltpu.roll(wall, 1, 0)) + (side - pltpu.roll(side, 1, 1))
            if x:
                total = total - left[s]
            if x + 1 < width:
                left[s] = face(value, conc[s, x + 1], vel[0, x], vel[0, x + 1], here, volt[x + 1], s)
                total = total + left[s]
            place = s * width + x
            cells[place * depth : (place + 1) * depth] = value - FLUX_SCALE * total
            moved = drift(here, s)
            top = slice(depth - 1, depth)
            for part, edge in enumerate(
                (value[top], rise[top] + moved[top], value[0:1], rise[0:1] - moved[0:1])
            ):
                line = sums + part * 2 * width + place
                rows[line : line + 1] = edge
    solved = left_product(table[...], cells[...])
    near[...] = solved[: cells.shape[0]]
    rows[:sums] = solved[cells.shape[0] :]


def enter_kernel(decays_x, decays_z, rows_in, left_halo, conc, vel, volt, shares, gains, rows):
    width, depth, span = volt.shape
    row = lax.broadcasted_iota(jnp.int32, (depth, span), 0)
    for s in range(2):
        decay = decays_x[s]
        flux = face(left_halo[s], conc[s, 0], left_halo[2], vel[0, 0], left_halo[3], volt[0], s)
        taken = -FLUX_SCALE * flux
        gained = (decay - 1.0) * taken
        gains[s * depth : (s + 1) * depth] = gained
        for side, scale in enumerate((decay ** (width - 1) * (decay - 1.0), 1.0 / decay - 1.0)):
            start = (side * 2 + s) * depth
            rows[start : start + depth] = rows_in[start : start + depth] + scale * taken
            weight = jnp.zeros((depth, span), jnp.float32)
            for z in range(depth):
                weight = jnp.where(row == z, decays_z[s] ** (z if side else depth - 1 - z), weight)
            line = 4 * depth + (side * 2 + s) * width
            rows[line : line + 1] = rows_in[line : line + 1] + jnp.sum(weight * gained, axis=0, keepdims=True)
    part = shares.shape[1] // HALVES
    tiles = LANES // part
    for chunk in range(span // LANES):
        turned = rows[:, chunk * LANES : (chunk + 1) * LANES].T
        half, start = divmod(chunk * tiles, shares.shape[0])
        for k in range(tiles):
            shares[start + k, half * part : (half + 1) * part] = turned[k * part : (k + 1) * part]


def member_shift(team, teams):
    return lax.div(team, teams // 2) * (TEAM // 2)


def list_place(member, block, blocks):
    total = TEAM * blocks
    return (member * blocks + block) * pow(SPREAD, -1, total) % total


def shifted_place(member, block, blocks, shift):
    return lax.rem(list_place(member, block, blocks) + shift * blocks, TEAM * blocks)


def by_lane(values, lane, unit):
    return jnp.where(lax.bitwise_and(lane, unit) == 0, values[0], values[1])


def wall_kernel(decays, stream_steps, blocks, width, depth, parts, collect, solve, ends, sums):
    members, places, _ = parts.shape
    lane = lax.broadcasted_iota(jnp.int32, (places, LANES), 1)
    faces = 2 * width
    first = LANES // 2
    lines = [None] * members
    for m in range(TEAM):
        below = pltpu.roll(parts[list_place(m, 0, blocks)], LANES - 2 * faces, 1)
        below = below * pltpu.roll(below, LANES - faces, 1)
        for b in range(blocks):
            own = parts[list_place(m, b, blocks)]
            meet = own
            if b + 1 < blocks:
                meet = meet + pltpu.roll(parts[list_place(m, b + 1, blocks)], LANES - 2 * faces, 1)
            above = meet * pltpu.roll(meet, LANES - faces, 1)
            both = jnp.where(lane < first + faces, above, pltpu.roll(below, faces, 1))
            lines[list_place(m, b, blocks)] = jnp.where(lane < first, own, both)
            below = above
    value = jnp.concatenate(lines, axis=0)
    gathered = product(value, collect[...])
    carry = [gathered[k * places : (k + 1) * places] for k in range(members)]
    side = LANES // 2
    unit = LANES // 4
    entering = lane < side
    step = by_lane([decay**depth for decay in decays], lane, unit)
    mirrors = [decay ** (depth * blocks + 1) for decay in decays]
    mirror = by_lane(mirrors, lane, unit)
    scale = by_lane([-d / (1.0 - m * m) for d, m in zip(decays, mirrors)], lane, unit)
    weights = [
        jnp.where(
            entering,
            by_lane([decay ** (depth * b) for decay in decays], lane, unit),
            by_lane([decay ** (depth * (blocks - 1 - b)) for decay in decays], lane, unit),
        )
        for b in range(blocks)
    ]
    for m in range(TEAM):
        before = jnp.zeros((places, LANES), jnp.float32)
        after = jnp.zeros((places, LANES), jnp.float32)
        befores = []
        afters = [None] * blocks
        for b in range(blocks):
            befores.append(before)
            before = step * before + carry[list_place(m, b, blocks)]
        for b in range(blocks - 1, -1, -1):
            afters[b] = after
            after = step * after + carry[list_place(m, b, blocks)]
        total = jnp.where(entering, before, after)
        mirrored = scale * (pltpu.roll(total, side, 1) - mirror * total)
        for b in range(blocks):
            carry[list_place(m, b, blocks)] = jnp.where(entering, befores[b], afters[b]) + weights[b] * mirrored
    full = jnp.concatenate([value, jnp.concatenate(carry, axis=0)], axis=1)
    result = product(full, solve[...])
    ends[...] = result.reshape(members, places, LANES)
    step = by_lane(stream_steps, lane, depth)
    entering = lane < 2 * depth
    pack = LANES // (4 * depth)
    shift = member_shift(lax.div(lax.axis_index("stream"), TEAM), sums.shape[0])
    weights = []
    for m in range(TEAM):
        options = [by_lane([value**k for value in stream_steps], lane, depth) for k in range(TEAM)]
        plain = jnp.where(entering, options[TEAM - 1 - m], options[m])
        turned = (m + TEAM // 2) % TEAM
        weights.append(jnp.where(shift == 0, plain, jnp.where(entering, options[TEAM - 1 - turned], options[turned])))
    for group in range(blocks // pack):
        packed = None
        for part in range(pack):
            b = group * pack + part
            both = None
            for m in range(TEAM):
                place = list_place(m, b, blocks) * places
                term = weights[m] * result[place : place + places]
                both = term if both is None else both + term
            both = jnp.where(lane < 4 * depth, both, 0.0)
            packed = packed + pltpu.roll(both, part * 4 * depth, 1) if part else both
        for team in range(sums.shape[0]):
            sums[team, group] = packed


def stream_kernel(steps, blocks, depth, ends, sums, links):
    places = ends.shape[1]
    teams, groups = sums.shape[0], sums.shape[1]
    pack = blocks // groups
    part = links.shape[1]
    team = lax.div(lax.axis_index("stream"), TEAM)
    shift = member_shift(team, teams)
    lane = lax.broadcasted_iota(jnp.int32, (places, LANES), 1)
    entering = lax.bitwise_and(lane, 2 * depth) == 0
    step = by_lane(steps, lane, depth)
    leap = by_lane([value**TEAM for value in steps], lane, depth)
    closing = by_lane([1.0 / (1.0 - value ** (TEAM * teams)) for value in steps], lane, depth)
    for group in range(groups):
        before = sums[team, group]
        after = before
        for k in range(1, teams):
            before = leap * before + sums[lax.rem(team + k, teams), group]
            after = leap * after + sums[lax.rem(team + teams - k, teams), group]
        both = closing * jnp.where(entering, before, after)
        for slot in range(pack):
            b = group * pack + slot
            before = pltpu.roll(both, LANES - slot * 4 * depth, 1) if slot else both
            after = before
            afters = [None] * TEAM
            for m in range(TEAM - 1, -1, -1):
                afters[m] = after
                after = step * after + ends[shifted_place(m, b, blocks, shift)]
            for m in range(TEAM):
                own = ends[shifted_place(m, b, blocks, shift)]
                carry = jnp.where(lane < 4 * depth, jnp.where(entering, before, afters[m]), own)
                before = step * before + own
                halved = carry + pltpu.roll(pltpu.roll(carry, LANES // HALVES, 1), part, 0)
                links[shifted_place(m, b, blocks, shift)] = halved[:part]


def home_kernel(near, gains, links, table, out, rows, solved, sent):
    _, width, depth, span = out.shape
    part = links.shape[1]
    lanes = LANES // HALVES
    tiles = LANES // part
    copies = []
    for chunk in range(links.shape[0] // tiles):
        for k in range(tiles):
            rows[k * part : (k + 1) * part] = links[chunk * tiles + k]
        turned = rows[...].T
        cuts = [slice(half * (span // HALVES) + chunk * LANES, half * (span // HALVES) + (chunk + 1) * LANES) for half in range(HALVES)]
        carry = jnp.concatenate([turned[half * lanes : (half + 1) * lanes] for half in range(HALVES)], axis=1)
        gained = jnp.concatenate([gains[:, cut] for cut in cuts], axis=1)
        added = left_product(table[...], jnp.concatenate([gained, carry], axis=0))
        for half, cut in enumerate(cuts):
            place = chunk * HALVES + half
            total = near[:, cut] + added[:, half * LANES : (half + 1) * LANES]
            for s in range(2):
                for x in range(width):
                    start = (s * width + x) * depth
                    solved[place, s, x] = total[start : start + depth]
            copies.append(pltpu.make_async_copy(solved.at[place], out.at[:, :, :, cut], sent.at[place]))
            copies[-1].start()
    for copy in copies:
        copy.wait()


def per_device(concentration, velocity, potential):
    _, width, depth, span = concentration.shape
    stream = lax.axis_size("stream")
    wall = lax.axis_size("wall")
    stream_total = width * stream
    wall_total = depth * wall
    rates_x = (4.0 * width * width, float(stream_total * stream_total // 25))
    rates_z = (4.0 * depth * depth, float(wall_total * wall_total // 16))
    decays_x = [line_factors(rate)[0] for rate in rates_x]
    decays_z = [line_factors(rate)[0] for rate in rates_z]
    steps_x = [decay**width for decay in decays_x]
    collect_z, solve_z = wall_tables(rates_x, rates_z, width, depth)
    collect = collect_table(rates_x, rates_z, width, depth)
    near, home = home_tables(rates_x, rates_z, width, depth)

    (edge,) = call(
        border_kernel,
        [(4, depth, span)],
        (concentration, velocity, potential),
        [pltpu.SemaphoreType.DMA((4,))],
        source=pltpu.HBM,
        room=53 * 1024 + 848,
    )
    left_halo = lax.ppermute(edge, "stream", [(i, (i + 1) % stream) for i in range(stream)])

    members = TEAM * wall
    teams = stream // TEAM
    holders = [[t * TEAM + (m + t // (teams // 2) * (TEAM // 2)) % TEAM for m in range(TEAM)] for t in range(teams)]
    listed = [[b * stream + place for place in team for b in range(wall)] for team in holders]
    plane = [[team[k * SPREAD % members] for k in range(members)] for team in listed]
    ranks = [[team[m] for team in holders] for m in range(TEAM)]
    swap = functools.partial(lax.all_to_all, split_axis=0, concat_axis=0, tiled=True)
    table = functools.partial(jnp.array, dtype=jnp.float32)
    places = span // members
    tile = (members, places, LANES)
    flat = (2 * width * depth, span)
    near, rows = call(
        predict_kernel,
        [flat, (LANES, span)],
        (concentration, velocity, potential, table(np.concatenate([near, collect]))),
        [pltpu.VMEM(flat, jnp.float32)],
    )
    shares, gains, rows = call(
        functools.partial(enter_kernel, decays_x, decays_z),
        [tile, (2 * depth, span), (LANES, span)],
        (rows, left_halo, concentration, velocity, potential),
        aliases={0: 2},
    )
    parts = swap(shares, ("wall", "stream"), axis_index_groups=plane)
    pack = LANES // (4 * depth)
    ends, sums = call(
        functools.partial(wall_kernel, decays_z, steps_x, wall, width, depth),
        [tile, (teams, wall // pack, places, LANES)],
        (parts, table(collect_z), table(solve_z)),
    )
    sums = swap(sums, "stream", axis_index_groups=ranks)
    (links,) = call(
        functools.partial(stream_kernel, steps_x, wall, depth),
        [(members, places // HALVES, LANES)],
        (ends, sums),
    )
    links = swap(links, ("wall", "stream"), axis_index_groups=plane)
    (out,) = call(
        home_kernel,
        [concentration.shape],
        (near, gains, links, table(home)),
        [
            pltpu.VMEM((LANES, LANES), jnp.float32),
            pltpu.VMEM((span // LANES, 2, width, depth, LANES), jnp.float32),
            pltpu.SemaphoreType.DMA((span // LANES,)),
        ],
        target=pltpu.HBM,
    )
    return out


def solution(mesh):
    return jax.shard_map(
        per_device,
        mesh=mesh,
        in_specs=(
            P(None, "stream", "wall", None),
            P(None, "stream", "wall", None),
            P("stream", "wall", None),
        ),
        out_specs=P(None, "stream", "wall", None),
        check_vma=False,
    )
```

```python
import functools

import jax
import jax.numpy as jnp
import numpy as np
from jax import lax
from jax.experimental import pallas as pl
from jax.experimental.pallas import tpu as pltpu
from jax.sharding import PartitionSpec as P

ADVECT_STEP = 0.2
DRIFT_RATES = (1.0, -0.5)
FLUX_SCALE = 0.25 * ADVECT_STEP
TEAM = 4
HALVES = 2
LANES = 128
SPREAD = 39


def line_factors(rate):
    base = 1.0 + 2.0 * rate
    root = np.sqrt(1.0 + 4.0 * rate)
    return float(2.0 * rate / (base + root)), float(1.0 / root)


def block_tables(decay, gain, cells):
    place = np.arange(cells)
    local = gain * decay ** np.abs(place[:, None] - place[None, :])
    collect = np.stack([decay ** (cells - 1 - place), decay**place], axis=1)
    spread = gain * np.stack([decay ** (place + 1), decay ** (cells - place)])
    return local, collect, spread


def collect_table(rates_x, rates_z, width, depth):
    table = np.zeros((4 * depth + 4 * width, 2, width, depth))
    stream_sums = table[: 4 * depth].reshape(2, 2, depth, 2, width, depth)
    wall_sums = table[4 * depth :].reshape(2, 2, width, 2, width, depth)
    for s in range(2):
        _, gather_x, _ = block_tables(*line_factors(rates_x[s]), width)
        _, gather_z, _ = block_tables(*line_factors(rates_z[s]), depth)
        for z in range(depth):
            stream_sums[:, s, z, s, :, z] = gather_x.T
        for x in range(width):
            wall_sums[:, s, x, s, x, :] = gather_z.T
    return table.reshape(-1, 2 * width * depth)


def wall_tables(rates_x, rates_z, width, depth):
    unit = LANES // 4
    sums = 4 * (depth + width)
    collect = np.zeros((LANES, 2, 2, unit))
    solve = np.zeros((2, LANES, LANES))
    sums_in = collect[: 4 * depth].reshape(2, 2, depth, 2, 2, unit)
    ends_in = collect[4 * depth : sums].reshape(2, 2, width, 2, 2, unit)
    flux_in = collect[sums : sums + 4 * width].reshape(2, 2, width, 2, 2, unit)
    near = solve[0, : 4 * depth, : 4 * depth].reshape(2, 2, depth, 2, 2, depth)
    spread = solve[1, :, : 4 * depth].reshape(2, 2, unit, 2, 2, depth)
    moved = solve[1, :, 4 * depth : sums].reshape(2, 2, unit, 2, 2, width)
    flux_near = solve[0, sums : sums + 4 * width, : 4 * depth].reshape(2, 2, width, 2, 2, depth)
    flux_moved = solve[0, sums : sums + 4 * width, 4 * depth : sums].reshape(2, 2, width, 2, 2, width)
    for s in range(2):
        _, gather_x, _ = block_tables(*line_factors(rates_x[s]), width)
        local, gather_z, hand = block_tables(*line_factors(rates_z[s]), depth)
        decay = line_factors(rates_z[s])[0]
        for side in range(2):
            sums_in[side, s, :, :, s, width + side] = gather_z
            near[side, s, :, side, s, :] = local
            spread[:, s, width + side, side, s, :] = hand
            for x in range(width):
                ends_in[side, s, x, side, s, x] = 1.0
                moved[side, s, x, side, s, x] = 1.0
        for end, cell, size in ((0, depth - 1, -FLUX_SCALE), (1, 0, FLUX_SCALE)):
            for x in range(width):
                flux_in[end, s, x, :, s, x] = size * gather_z[cell]
                flux_moved[end, s, x, 1 - end, s, x] = size / decay
                for side in range(2):
                    flux_in[end, s, x, :, s, width + side] = size * gather_x[x, side] * gather_z[cell]
                    flux_near[end, s, x, side, s, :] = size * gather_x[x, side] * local[cell]
    return collect.reshape(LANES, LANES), solve.reshape(2 * LANES, LANES)


def home_tables(rates_x, rates_z, width, depth):
    cells = 2 * width * depth
    near = np.zeros((2, width, depth, 2, width, depth))
    stream_spread = np.zeros((2, width, depth, 2, 2, depth))
    wall_spread = np.zeros((2, width, depth, 2, 2, width))
    for s in range(2):
        local_x, _, hand_x = block_tables(*line_factors(rates_x[s]), width)
        local_z, _, hand_z = block_tables(*line_factors(rates_z[s]), depth)
        near[s, :, :, s, :, :] = np.einsum("xa,zb->xzab", local_x, local_z)
        stream_spread[s, :, :, :, s, :] = np.einsum("ex,zb->xzeb", hand_x, np.eye(depth))
        wall_spread[s, :, :, :, s, :] = np.einsum("xa,ez->xzea", local_x, hand_z)
    parts = (near[:, :, :, :, 0], stream_spread, wall_spread)
    return near.reshape(cells, cells), np.concatenate([part.reshape(cells, -1) for part in parts], axis=1)


def call(kernel, outs, ins, scratch=(), aliases=None, source=pltpu.VMEM, target=pltpu.VMEM, room=32 * 1024):
    return pl.pallas_call(
        kernel,
        out_shape=[jax.ShapeDtypeStruct(shape, jnp.float32) for shape in outs],
        in_specs=[pl.BlockSpec(memory_space=source)] * len(ins),
        out_specs=[pl.BlockSpec(memory_space=target)] * len(outs),
        scratch_shapes=list(scratch),
        input_output_aliases=aliases or {},
        compiler_params=pltpu.CompilerParams(vmem_limit_bytes=room * 1024),
    )(*ins)


def drift(volt, species):
    return (2.0 * DRIFT_RATES[species]) * volt


def face(conc_low, conc_high, speed_low, speed_high, volt_low, volt_high, species):
    return (conc_low + conc_high) * (speed_low + speed_high - drift(volt_high - volt_low, species))


def border_kernel(conc, vel, volt, edge, arrived):
    last = volt.shape[0] - 1
    copies = [
        pltpu.make_async_copy(source, edge.at[place], arrived.at[place])
        for place, source in enumerate((conc.at[0, last], conc.at[1, last], vel.at[0, last], volt.at[last]))
    ]
    for copy in copies:
        copy.start()
    for copy in copies:
        copy.wait()


def split(values):
    high = values.astype(jnp.bfloat16)
    return high, (values - high.astype(jnp.float32)).astype(jnp.bfloat16)


def product(values, table):
    high, low = split(values)
    table_high, table_low = split(table)
    dot = functools.partial(jnp.dot, preferred_element_type=jnp.float32)
    wide = table.shape[1]
    beside = jnp.concatenate([table_high, table_low], axis=1)
    if values.shape[1] <= LANES:
        under = jnp.concatenate([table_high, jnp.zeros_like(table_low)], axis=1)
        both = dot(jnp.concatenate([high, low], axis=1), jnp.concatenate([beside, under], axis=0))
        return both[:, :wide] + both[:, wide:]
    both = dot(high, beside)
    return both[:, :wide] + (both[:, wide:] + dot(low, table_high))


def left_product(table, values):
    high, low = split(values)
    table_high, table_low = split(table)
    dot = functools.partial(jnp.dot, preferred_element_type=jnp.float32)
    tall = table.shape[0]
    above = jnp.concatenate([table_high, table_low], axis=0)
    under = jnp.concatenate([table_high, jnp.zeros_like(table_low)], axis=0)
    both = dot(jnp.concatenate([above, under], axis=1), jnp.concatenate([high, low], axis=0))
    return both[:tall] + both[tall:]


def predict_kernel(conc, vel, volt, table, near, rows, cells):
    width, depth, span = volt.shape
    row = lax.broadcasted_iota(jnp.int32, (depth, span), 0)
    left = [None, None]
    sums = 4 * (width + depth)
    for x in range(width):
        here = volt[x]
        rise = vel[1, x]
        volt_up = pltpu.roll(here, depth - 1, 0)
        volt_next = pltpu.roll(here, span - 1, 1)
        speed_up = pltpu.roll(rise, depth - 1, 0)
        speed_next = pltpu.roll(vel[2, x], span - 1, 1)
        for s in range(2):
            value = conc[s, x]
            wall = face(value, pltpu.roll(value, depth - 1, 0), rise, speed_up, here, volt_up, s)
            wall = jnp.where(row == depth - 1, 0.0, wall)
            side = face(value, pltpu.roll(value, span - 1, 1), vel[2, x], speed_next, here, volt_next, s)
            total = (wall - pltpu.roll(wall, 1, 0)) + (side - pltpu.roll(side, 1, 1))
            if x:
                total = total - left[s]
            if x + 1 < width:
                left[s] = face(value, conc[s, x + 1], vel[0, x], vel[0, x + 1], here, volt[x + 1], s)
                total = total + left[s]
            place = s * width + x
            cells[place * depth : (place + 1) * depth] = value - FLUX_SCALE * total
            moved = drift(here, s)
            top = slice(depth - 1, depth)
            for part, edge in enumerate(
                (value[top], rise[top] + moved[top], value[0:1], rise[0:1] - moved[0:1])
            ):
                line = sums + part * 2 * width + place
                rows[line : line + 1] = edge
    solved = left_product(table[...], cells[...])
    near[...] = solved[: cells.shape[0]]
    rows[:sums] = solved[cells.shape[0] :]


def enter_kernel(decays_x, decays_z, rows_in, left_halo, conc, vel, volt, shares, gains, rows):
    width, depth, span = volt.shape
    row = lax.broadcasted_iota(jnp.int32, (depth, span), 0)
    for s in range(2):
        decay = decays_x[s]
        flux = face(left_halo[s], conc[s, 0], left_halo[2], vel[0, 0], left_halo[3], volt[0], s)
        taken = -FLUX_SCALE * flux
        gained = (decay - 1.0) * taken
        gains[s * depth : (s + 1) * depth] = gained
        for side, scale in enumerate((decay ** (width - 1) * (decay - 1.0), 1.0 / decay - 1.0)):
            start = (side * 2 + s) * depth
            rows[start : start + depth] = rows_in[start : start + depth] + scale * taken
            weight = jnp.zeros((depth, span), jnp.float32)
            for z in range(depth):
                weight = jnp.where(row == z, decays_z[s] ** (z if side else depth - 1 - z), weight)
            line = 4 * depth + (side * 2 + s) * width
            rows[line : line + 1] = rows_in[line : line + 1] + jnp.sum(weight * gained, axis=0, keepdims=True)
    part = shares.shape[1] // HALVES
    tiles = LANES // part
    for chunk in range(span // LANES):
        turned = rows[:, chunk * LANES : (chunk + 1) * LANES].T
        half, start = divmod(chunk * tiles, shares.shape[0])
        for k in range(tiles):
            shares[start + k, half * part : (half + 1) * part] = turned[k * part : (k + 1) * part]


def member_shift(team, teams):
    return lax.div(team, teams // 2) * (TEAM // 2)


def list_place(member, block, blocks):
    total = TEAM * blocks
    return (member * blocks + block) * pow(SPREAD, -1, total) % total


def shifted_place(member, block, blocks, shift):
    return lax.rem(list_place(member, block, blocks) + shift * blocks, TEAM * blocks)


def by_lane(values, lane, unit):
    return jnp.where(lax.bitwise_and(lane, unit) == 0, values[0], values[1])


def wall_kernel(decays, stream_steps, blocks, width, depth, parts, collect, solve, ends, sums, carry, lines):
    members, places, _ = parts.shape
    flat = members * places
    lane = lax.broadcasted_iota(jnp.int32, (places, LANES), 1)
    faces = 2 * width
    first = LANES // 2
    for m in range(TEAM):
        below = pltpu.roll(parts[list_place(m, 0, blocks)], LANES - 2 * faces, 1)
        below = below * pltpu.roll(below, LANES - faces, 1)
        for b in range(blocks):
            own = parts[list_place(m, b, blocks)]
            meet = own
            if b + 1 < blocks:
                meet = meet + pltpu.roll(parts[list_place(m, b + 1, blocks)], LANES - 2 * faces, 1)
            above = meet * pltpu.roll(meet, LANES - faces, 1)
            both = jnp.where(lane < first + faces, above, pltpu.roll(below, faces, 1))
            lines[list_place(m, b, blocks)] = jnp.where(lane < first, own, both)
            below = above
    value = lines[...].reshape(flat, LANES)
    carry[...] = product(value, collect[...]).reshape(members, places, LANES)
    side = LANES // 2
    unit = LANES // 4
    entering = lane < side
    step = by_lane([decay**depth for decay in decays], lane, unit)
    mirrors = [decay ** (depth * blocks + 1) for decay in decays]
    mirror = by_lane(mirrors, lane, unit)
    scale = by_lane([-d / (1.0 - m * m) for d, m in zip(decays, mirrors)], lane, unit)
    weights = [
        jnp.where(
            entering,
            by_lane([decay ** (depth * b) for decay in decays], lane, unit),
            by_lane([decay ** (depth * (blocks - 1 - b)) for decay in decays], lane, unit),
        )
        for b in range(blocks)
    ]
    for m in range(TEAM):
        before = jnp.zeros((places, LANES), jnp.float32)
        after = jnp.zeros((places, LANES), jnp.float32)
        befores = []
        afters = [None] * blocks
        for b in range(blocks):
            befores.append(before)
            before = step * before + carry[list_place(m, b, blocks)]
        for b in range(blocks - 1, -1, -1):
            afters[b] = after
            after = step * after + carry[list_place(m, b, blocks)]
        total = jnp.where(entering, before, after)
        mirrored = scale * (pltpu.roll(total, side, 1) - mirror * total)
        for b in range(blocks):
            carry[list_place(m, b, blocks)] = jnp.where(entering, befores[b], afters[b]) + weights[b] * mirrored
    full = jnp.concatenate([value, carry[...].reshape(flat, LANES)], axis=1)
    result = product(full, solve[...])
    ends[...] = result.reshape(members, places, LANES)
    step = by_lane(stream_steps, lane, depth)
    entering = lane < 2 * depth
    pack = LANES // (4 * depth)
    shift = member_shift(lax.div(lax.axis_index("stream"), TEAM), sums.shape[0])
    weights = []
    for m in range(TEAM):
        options = [by_lane([value**k for value in stream_steps], lane, depth) for k in range(TEAM)]
        plain = jnp.where(entering, options[TEAM - 1 - m], options[m])
        turned = (m + TEAM // 2) % TEAM
        weights.append(jnp.where(shift == 0, plain, jnp.where(entering, options[TEAM - 1 - turned], options[turned])))
    for group in range(blocks // pack):
        packed = None
        for part in range(pack):
            b = group * pack + part
            both = None
            for m in range(TEAM):
                place = list_place(m, b, blocks) * places
                term = weights[m] * result[place : place + places]
                both = term if both is None else both + term
            both = jnp.where(lane < 4 * depth, both, 0.0)
            packed = packed + pltpu.roll(both, part * 4 * depth, 1) if part else both
        for team in range(sums.shape[0]):
            sums[team, group] = packed


def stream_kernel(steps, blocks, depth, ends, sums, links):
    places = ends.shape[1]
    teams, groups = sums.shape[0], sums.shape[1]
    pack = blocks // groups
    part = links.shape[1]
    team = lax.div(lax.axis_index("stream"), TEAM)
    shift = member_shift(team, teams)
    lane = lax.broadcasted_iota(jnp.int32, (places, LANES), 1)
    entering = lax.bitwise_and(lane, 2 * depth) == 0
    step = by_lane(steps, lane, depth)
    leap = by_lane([value**TEAM for value in steps], lane, depth)
    closing = by_lane([1.0 / (1.0 - value ** (TEAM * teams)) for value in steps], lane, depth)
    for group in range(groups):
        before = sums[team, group]
        after = before
        for k in range(1, teams):
            before = leap * before + sums[lax.rem(team + k, teams), group]
            after = leap * after + sums[lax.rem(team + teams - k, teams), group]
        both = closing * jnp.where(entering, before, after)
        for slot in range(pack):
            b = group * pack + slot
            before = pltpu.roll(both, LANES - slot * 4 * depth, 1) if slot else both
            after = before
            afters = [None] * TEAM
            for m in range(TEAM - 1, -1, -1):
                afters[m] = after
                after = step * after + ends[shifted_place(m, b, blocks, shift)]
            for m in range(TEAM):
                own = ends[shifted_place(m, b, blocks, shift)]
                carry = jnp.where(lane < 4 * depth, jnp.where(entering, before, afters[m]), own)
                before = step * before + own
                halved = carry + pltpu.roll(pltpu.roll(carry, LANES // HALVES, 1), part, 0)
                links[shifted_place(m, b, blocks, shift)] = halved[:part]


def home_kernel(near, gains, links, table, out, solved, sent):
    _, width, depth, span = out.shape
    lanes = LANES // HALVES
    copies = []
    for chunk in range(links.shape[0] // LANES):
        turned = links[chunk * LANES : (chunk + 1) * LANES].T
        cuts = [slice(half * (span // HALVES) + chunk * LANES, half * (span // HALVES) + (chunk + 1) * LANES) for half in range(HALVES)]
        carry = jnp.concatenate([turned[half * lanes : (half + 1) * lanes] for half in range(HALVES)], axis=1)
        gained = jnp.concatenate([gains[:, cut] for cut in cuts], axis=1)
        added = left_product(table[...], jnp.concatenate([gained, carry], axis=0))
        for half, cut in enumerate(cuts):
            place = chunk * HALVES + half
            total = near[:, cut] + added[:, half * LANES : (half + 1) * LANES]
            for s in range(2):
                for x in range(width):
                    start = (s * width + x) * depth
                    solved[place, s, x] = total[start : start + depth]
            copies.append(pltpu.make_async_copy(solved.at[place], out.at[:, :, :, cut], sent.at[place]))
            copies[-1].start()
    for copy in copies:
        copy.wait()


def per_device(concentration, velocity, potential):
    _, width, depth, span = concentration.shape
    stream = lax.axis_size("stream")
    wall = lax.axis_size("wall")
    stream_total = width * stream
    wall_total = depth * wall
    rates_x = (4.0 * width * width, float(stream_total * stream_total // 25))
    rates_z = (4.0 * depth * depth, float(wall_total * wall_total // 16))
    decays_x = [line_factors(rate)[0] for rate in rates_x]
    decays_z = [line_factors(rate)[0] for rate in rates_z]
    steps_x = [decay**width for decay in decays_x]
    collect_z, solve_z = wall_tables(rates_x, rates_z, width, depth)
    collect = collect_table(rates_x, rates_z, width, depth)
    near, home = home_tables(rates_x, rates_z, width, depth)

    (edge,) = call(
        border_kernel,
        [(4, depth, span)],
        (concentration, velocity, potential),
        [pltpu.SemaphoreType.DMA((4,))],
        source=pltpu.HBM,
        room=53 * 1024 + 848,
    )
    left_halo = lax.ppermute(edge, "stream", [(i, (i + 1) % stream) for i in range(stream)])

    members = TEAM * wall
    teams = stream // TEAM
    holders = [[t * TEAM + (m + t // (teams // 2) * (TEAM // 2)) % TEAM for m in range(TEAM)] for t in range(teams)]
    listed = [[b * stream + place for place in team for b in range(wall)] for team in holders]
    plane = [[team[k * SPREAD % members] for k in range(members)] for team in listed]
    ranks = [[team[m] for team in holders] for m in range(TEAM)]
    swap = functools.partial(lax.all_to_all, split_axis=0, concat_axis=0, tiled=True)
    table = functools.partial(jnp.array, dtype=jnp.float32)
    places = span // members
    tile = (members, places, LANES)
    flat = (2 * width * depth, span)
    near, rows = call(
        predict_kernel,
        [flat, (LANES, span)],
        (concentration, velocity, potential, table(np.concatenate([near, collect]))),
        [pltpu.VMEM(flat, jnp.float32)],
    )
    shares, gains, rows = call(
        functools.partial(enter_kernel, decays_x, decays_z),
        [tile, (2 * depth, span), (LANES, span)],
        (rows, left_halo, concentration, velocity, potential),
        aliases={0: 2},
    )
    parts = swap(shares, ("wall", "stream"), axis_index_groups=plane)
    pack = LANES // (4 * depth)
    ends, sums = call(
        functools.partial(wall_kernel, decays_z, steps_x, wall, width, depth),
        [tile, (teams, wall // pack, places, LANES)],
        (parts, table(collect_z), table(solve_z)),
        [pltpu.VMEM(tile, jnp.float32), pltpu.VMEM(tile, jnp.float32)],
    )
    sums = swap(sums, "stream", axis_index_groups=ranks)
    (links,) = call(
        functools.partial(stream_kernel, steps_x, wall, depth),
        [(members, places // HALVES, LANES)],
        (ends, sums),
    )
    links = swap(links, ("wall", "stream"), axis_index_groups=plane)
    (out,) = call(
        home_kernel,
        [concentration.shape],
        (near, gains, links.reshape(-1, LANES), table(home)),
        [
            pltpu.VMEM((span // LANES, 2, width, depth, LANES), jnp.float32),
            pltpu.SemaphoreType.DMA((span // LANES,)),
        ],
        target=pltpu.HBM,
    )
    return out


def solution(mesh):
    return jax.shard_map(
        per_device,
        mesh=mesh,
        in_specs=(
            P(None, "stream", "wall", None),
            P(None, "stream", "wall", None),
            P("stream", "wall", None),
        ),
        out_specs=P(None, "stream", "wall", None),
        check_vma=False,
    )
```

```python
import functools

import jax
import jax.numpy as jnp
import numpy as np
from jax import lax
from jax.experimental import pallas as pl
from jax.experimental.pallas import tpu as pltpu
from jax.sharding import PartitionSpec as P

ADVECT_STEP = 0.2
DRIFT_RATES = (1.0, -0.5)
FLUX_SCALE = 0.25 * ADVECT_STEP
TEAM = 4
HALVES = 2
LANES = 128
SPREAD = 39


def line_factors(rate):
    base = 1.0 + 2.0 * rate
    root = np.sqrt(1.0 + 4.0 * rate)
    return float(2.0 * rate / (base + root)), float(1.0 / root)


def block_tables(decay, gain, cells):
    place = np.arange(cells)
    local = gain * decay ** np.abs(place[:, None] - place[None, :])
    collect = np.stack([decay ** (cells - 1 - place), decay**place], axis=1)
    spread = gain * np.stack([decay ** (place + 1), decay ** (cells - place)])
    return local, collect, spread


def collect_table(rates_x, rates_z, width, depth):
    table = np.zeros((4 * depth + 4 * width, 2, width, depth))
    stream_sums = table[: 4 * depth].reshape(2, 2, depth, 2, width, depth)
    wall_sums = table[4 * depth :].reshape(2, 2, width, 2, width, depth)
    for s in range(2):
        _, gather_x, _ = block_tables(*line_factors(rates_x[s]), width)
        _, gather_z, _ = block_tables(*line_factors(rates_z[s]), depth)
        for z in range(depth):
            stream_sums[:, s, z, s, :, z] = gather_x.T
        for x in range(width):
            wall_sums[:, s, x, s, x, :] = gather_z.T
    return table.reshape(-1, 2 * width * depth)


def wall_tables(rates_x, rates_z, width, depth):
    unit = LANES // 4
    sums = 4 * (depth + width)
    collect = np.zeros((LANES, 2, 2, unit))
    solve = np.zeros((2, LANES, LANES))
    sums_in = collect[: 4 * depth].reshape(2, 2, depth, 2, 2, unit)
    ends_in = collect[4 * depth : sums].reshape(2, 2, width, 2, 2, unit)
    flux_in = collect[sums : sums + 4 * width].reshape(2, 2, width, 2, 2, unit)
    near = solve[0, : 4 * depth, : 4 * depth].reshape(2, 2, depth, 2, 2, depth)
    spread = solve[1, :, : 4 * depth].reshape(2, 2, unit, 2, 2, depth)
    moved = solve[1, :, 4 * depth : sums].reshape(2, 2, unit, 2, 2, width)
    flux_near = solve[0, sums : sums + 4 * width, : 4 * depth].reshape(2, 2, width, 2, 2, depth)
    flux_moved = solve[0, sums : sums + 4 * width, 4 * depth : sums].reshape(2, 2, width, 2, 2, width)
    for s in range(2):
        _, gather_x, _ = block_tables(*line_factors(rates_x[s]), width)
        local, gather_z, hand = block_tables(*line_factors(rates_z[s]), depth)
        decay = line_factors(rates_z[s])[0]
        for side in range(2):
            sums_in[side, s, :, :, s, width + side] = gather_z
            near[side, s, :, side, s, :] = local
            spread[:, s, width + side, side, s, :] = hand
            for x in range(width):
                ends_in[side, s, x, side, s, x] = 1.0
                moved[side, s, x, side, s, x] = 1.0
        for end, cell, size in ((0, depth - 1, -FLUX_SCALE), (1, 0, FLUX_SCALE)):
            for x in range(width):
                flux_in[end, s, x, :, s, x] = size * gather_z[cell]
                flux_moved[end, s, x, 1 - end, s, x] = size / decay
                for side in range(2):
                    flux_in[end, s, x, :, s, width + side] = size * gather_x[x, side] * gather_z[cell]
                    flux_near[end, s, x, side, s, :] = size * gather_x[x, side] * local[cell]
    return collect.reshape(LANES, LANES), solve.reshape(2 * LANES, LANES)


def home_tables(rates_x, rates_z, width, depth):
    cells = 2 * width * depth
    near = np.zeros((2, width, depth, 2, width, depth))
    stream_spread = np.zeros((2, width, depth, 2, 2, depth))
    wall_spread = np.zeros((2, width, depth, 2, 2, width))
    for s in range(2):
        local_x, _, hand_x = block_tables(*line_factors(rates_x[s]), width)
        local_z, _, hand_z = block_tables(*line_factors(rates_z[s]), depth)
        near[s, :, :, s, :, :] = np.einsum("xa,zb->xzab", local_x, local_z)
        stream_spread[s, :, :, :, s, :] = np.einsum("ex,zb->xzeb", hand_x, np.eye(depth))
        wall_spread[s, :, :, :, s, :] = np.einsum("xa,ez->xzea", local_x, hand_z)
    parts = (near[:, :, :, :, 0], stream_spread, wall_spread)
    return near.reshape(cells, cells), np.concatenate([part.reshape(cells, -1) for part in parts], axis=1)


def call(kernel, outs, ins, scratch=(), aliases=None, source=pltpu.VMEM, target=pltpu.VMEM, room=32 * 1024):
    return pl.pallas_call(
        kernel,
        out_shape=[jax.ShapeDtypeStruct(shape, jnp.float32) for shape in outs],
        in_specs=[pl.BlockSpec(memory_space=source)] * len(ins),
        out_specs=[pl.BlockSpec(memory_space=target)] * len(outs),
        scratch_shapes=list(scratch),
        input_output_aliases=aliases or {},
        compiler_params=pltpu.CompilerParams(vmem_limit_bytes=room * 1024),
    )(*ins)


def drift(volt, species):
    return (2.0 * DRIFT_RATES[species]) * volt


def face(conc_low, conc_high, speed_low, speed_high, volt_low, volt_high, species):
    return (conc_low + conc_high) * (speed_low + speed_high - drift(volt_high - volt_low, species))


def border_kernel(conc, vel, volt, edge, arrived):
    last = volt.shape[0] - 1
    copies = [
        pltpu.make_async_copy(source, edge.at[place], arrived.at[place])
        for place, source in enumerate((conc.at[0, last], conc.at[1, last], vel.at[0, last], volt.at[last]))
    ]
    for copy in copies:
        copy.start()
    for copy in copies:
        copy.wait()


def split(values):
    high = values.astype(jnp.bfloat16)
    return high, (values - high.astype(jnp.float32)).astype(jnp.bfloat16)


def product(values, table):
    high, low = split(values)
    table_high, table_low = split(table)
    dot = functools.partial(jnp.dot, preferred_element_type=jnp.float32)
    wide = table.shape[1]
    beside = jnp.concatenate([table_high, table_low], axis=1)
    if values.shape[1] <= LANES:
        under = jnp.concatenate([table_high, jnp.zeros_like(table_low)], axis=1)
        both = dot(jnp.concatenate([high, low], axis=1), jnp.concatenate([beside, under], axis=0))
        return both[:, :wide] + both[:, wide:]
    both = dot(high, beside)
    return both[:, :wide] + (both[:, wide:] + dot(low, table_high))


def left_product(table, values):
    high, low = split(values)
    table_high, table_low = split(table)
    dot = functools.partial(jnp.dot, preferred_element_type=jnp.float32)
    tall = table.shape[0]
    above = jnp.concatenate([table_high, table_low], axis=0)
    under = jnp.concatenate([table_high, jnp.zeros_like(table_low)], axis=0)
    both = dot(jnp.concatenate([above, under], axis=1), jnp.concatenate([high, low], axis=0))
    return both[:tall] + both[tall:]


def predict_kernel(conc, vel, volt, table, near, rows, cells):
    width, depth, span = volt.shape
    row = lax.broadcasted_iota(jnp.int32, (depth, span), 0)
    left = [None, None]
    sums = 4 * (width + depth)
    for x in range(width):
        here = volt[x]
        rise = vel[1, x]
        volt_up = pltpu.roll(here, depth - 1, 0)
        volt_next = pltpu.roll(here, span - 1, 1)
        speed_up = pltpu.roll(rise, depth - 1, 0)
        speed_next = pltpu.roll(vel[2, x], span - 1, 1)
        for s in range(2):
            value = conc[s, x]
            wall = face(value, pltpu.roll(value, depth - 1, 0), rise, speed_up, here, volt_up, s)
            wall = jnp.where(row == depth - 1, 0.0, wall)
            side = face(value, pltpu.roll(value, span - 1, 1), vel[2, x], speed_next, here, volt_next, s)
            total = (wall - pltpu.roll(wall, 1, 0)) + (side - pltpu.roll(side, 1, 1))
            if x:
                total = total - left[s]
            if x + 1 < width:
                left[s] = face(value, conc[s, x + 1], vel[0, x], vel[0, x + 1], here, volt[x + 1], s)
                total = total + left[s]
            place = s * width + x
            cells[place * depth : (place + 1) * depth] = value - FLUX_SCALE * total
            moved = drift(here, s)
            top = slice(depth - 1, depth)
            for part, edge in enumerate(
                (value[top], rise[top] + moved[top], value[0:1], rise[0:1] - moved[0:1])
            ):
                line = sums + part * 2 * width + place
                rows[line : line + 1] = edge
    solved = left_product(table[...], cells[...])
    near[...] = solved[: cells.shape[0]]
    rows[:sums] = solved[cells.shape[0] :]


def enter_kernel(decays_x, decays_z, rows_in, left_halo, conc, vel, volt, shares, gains, rows):
    width, depth, span = volt.shape
    row = lax.broadcasted_iota(jnp.int32, (depth, span), 0)
    for s in range(2):
        decay = decays_x[s]
        flux = face(left_halo[s], conc[s, 0], left_halo[2], vel[0, 0], left_halo[3], volt[0], s)
        taken = -FLUX_SCALE * flux
        gained = (decay - 1.0) * taken
        gains[s * depth : (s + 1) * depth] = gained
        for side, scale in enumerate((decay ** (width - 1) * (decay - 1.0), 1.0 / decay - 1.0)):
            start = (side * 2 + s) * depth
            rows[start : start + depth] = rows_in[start : start + depth] + scale * taken
            weight = jnp.zeros((depth, span), jnp.float32)
            for z in range(depth):
                weight = jnp.where(row == z, decays_z[s] ** (z if side else depth - 1 - z), weight)
            line = 4 * depth + (side * 2 + s) * width
            rows[line : line + 1] = rows_in[line : line + 1] + jnp.sum(weight * gained, axis=0, keepdims=True)
    part = shares.shape[1] // HALVES
    tiles = LANES // part
    for chunk in range(span // LANES):
        turned = rows[:, chunk * LANES : (chunk + 1) * LANES].T
        half, start = divmod(chunk * tiles, shares.shape[0])
        for k in range(tiles):
            shares[start + k, half * part : (half + 1) * part] = turned[k * part : (k + 1) * part]


def member_shift(team, teams):
    return lax.div(team, teams // 2) * (TEAM // 2)


def list_place(member, block, blocks):
    total = TEAM * blocks
    return (member * blocks + block) * pow(SPREAD, -1, total) % total


def shifted_place(member, block, blocks, shift):
    return lax.bitwise_and(list_place(member, block, blocks) + shift * blocks, TEAM * blocks - 1)


def by_lane(values, lane, unit):
    return jnp.where(lax.bitwise_and(lane, unit) == 0, values[0], values[1])


def wall_kernel(decays, stream_steps, blocks, width, depth, parts, collect, solve, ends, sums, carry, lines):
    members, places, _ = parts.shape
    flat = members * places
    lane = lax.broadcasted_iota(jnp.int32, (places, LANES), 1)
    faces = 2 * width
    first = LANES // 2
    for m in range(TEAM):
        below = pltpu.roll(parts[list_place(m, 0, blocks)], LANES - 2 * faces, 1)
        below = below * pltpu.roll(below, LANES - faces, 1)
        for b in range(blocks):
            own = parts[list_place(m, b, blocks)]
            meet = own
            if b + 1 < blocks:
                meet = meet + pltpu.roll(parts[list_place(m, b + 1, blocks)], LANES - 2 * faces, 1)
            above = meet * pltpu.roll(meet, LANES - faces, 1)
            both = jnp.where(lane < first + faces, above, pltpu.roll(below, faces, 1))
            lines[list_place(m, b, blocks)] = jnp.where(lane < first, own, both)
            below = above
    value = lines[...].reshape(flat, LANES)
    carry[...] = product(value, collect[...]).reshape(members, places, LANES)
    side = LANES // 2
    unit = LANES // 4
    entering = lane < side
    step = by_lane([decay**depth for decay in decays], lane, unit)
    mirrors = [decay ** (depth * blocks + 1) for decay in decays]
    mirror = by_lane(mirrors, lane, unit)
    scale = by_lane([-d / (1.0 - m * m) for d, m in zip(decays, mirrors)], lane, unit)
    weights = [
        jnp.where(
            entering,
            by_lane([decay ** (depth * b) for decay in decays], lane, unit),
            by_lane([decay ** (depth * (blocks - 1 - b)) for decay in decays], lane, unit),
        )
        for b in range(blocks)
    ]
    for m in range(TEAM):
        before = jnp.zeros((places, LANES), jnp.float32)
        after = jnp.zeros((places, LANES), jnp.float32)
        befores = []
        afters = [None] * blocks
        for b in range(blocks):
            befores.append(before)
            before = step * before + carry[list_place(m, b, blocks)]
        for b in range(blocks - 1, -1, -1):
            afters[b] = after
            after = step * after + carry[list_place(m, b, blocks)]
        total = jnp.where(entering, before, after)
        mirrored = scale * (pltpu.roll(total, side, 1) - mirror * total)
        for b in range(blocks):
            carry[list_place(m, b, blocks)] = jnp.where(entering, befores[b], afters[b]) + weights[b] * mirrored
    full = jnp.concatenate([value, carry[...].reshape(flat, LANES)], axis=1)
    result = product(full, solve[...])
    ends[...] = result.reshape(members, places, LANES)
    step = by_lane(stream_steps, lane, depth)
    entering = lane < 2 * depth
    pack = LANES // (4 * depth)
    shift = member_shift(lax.div(lax.axis_index("stream"), TEAM), sums.shape[0])
    weights = []
    for m in range(TEAM):
        options = [by_lane([value**k for value in stream_steps], lane, depth) for k in range(TEAM)]
        plain = jnp.where(entering, options[TEAM - 1 - m], options[m])
        turned = (m + TEAM // 2) % TEAM
        weights.append(jnp.where(shift == 0, plain, jnp.where(entering, options[TEAM - 1 - turned], options[turned])))
    for group in range(blocks // pack):
        packed = None
        for part in range(pack):
            b = group * pack + part
            both = None
            for m in range(TEAM):
                place = list_place(m, b, blocks) * places
                term = weights[m] * result[place : place + places]
                both = term if both is None else both + term
            both = jnp.where(lane < 4 * depth, both, 0.0)
            packed = packed + pltpu.roll(both, part * 4 * depth, 1) if part else both
        for team in range(sums.shape[0]):
            sums[team, group] = packed


def stream_kernel(steps, blocks, depth, ends, sums, links):
    places = ends.shape[1]
    teams, groups = sums.shape[0], sums.shape[1]
    pack = blocks // groups
    part = links.shape[1]
    team = lax.div(lax.axis_index("stream"), TEAM)
    shift = member_shift(team, teams)
    lane = lax.broadcasted_iota(jnp.int32, (places, LANES), 1)
    entering = lax.bitwise_and(lane, 2 * depth) == 0
    step = by_lane(steps, lane, depth)
    leap = by_lane([value**TEAM for value in steps], lane, depth)
    closing = by_lane([1.0 / (1.0 - value ** (TEAM * teams)) for value in steps], lane, depth)
    for group in range(groups):
        before = sums[team, group]
        after = before
        for k in range(1, teams):
            before = leap * before + sums[lax.rem(team + k, teams), group]
            after = leap * after + sums[lax.rem(team + teams - k, teams), group]
        both = closing * jnp.where(entering, before, after)
        for slot in range(pack):
            b = group * pack + slot
            before = pltpu.roll(both, LANES - slot * 4 * depth, 1) if slot else both
            after = before
            afters = [None] * TEAM
            for m in range(TEAM - 1, -1, -1):
                afters[m] = after
                after = step * after + ends[shifted_place(m, b, blocks, shift)]
            for m in range(TEAM):
                own = ends[shifted_place(m, b, blocks, shift)]
                carry = jnp.where(lane < 4 * depth, jnp.where(entering, before, afters[m]), own)
                before = step * before + own
                halved = carry + pltpu.roll(pltpu.roll(carry, LANES // HALVES, 1), part, 0)
                links[shifted_place(m, b, blocks, shift)] = halved[:part]


def home_kernel(near, gains, links, table, out, solved, sent):
    _, width, depth, span = out.shape
    lanes = LANES // HALVES
    copies = []
    for chunk in range(links.shape[0] // LANES):
        turned = links[chunk * LANES : (chunk + 1) * LANES].T
        cuts = [slice(half * (span // HALVES) + chunk * LANES, half * (span // HALVES) + (chunk + 1) * LANES) for half in range(HALVES)]
        carry = jnp.concatenate([turned[half * lanes : (half + 1) * lanes] for half in range(HALVES)], axis=1)
        gained = jnp.concatenate([gains[:, cut] for cut in cuts], axis=1)
        added = left_product(table[...], jnp.concatenate([gained, carry], axis=0))
        for half, cut in enumerate(cuts):
            place = chunk * HALVES + half
            total = near[:, cut] + added[:, half * LANES : (half + 1) * LANES]
            for s in range(2):
                for x in range(width):
                    start = (s * width + x) * depth
                    solved[place, s, x] = total[start : start + depth]
            copies.append(pltpu.make_async_copy(solved.at[place], out.at[:, :, :, cut], sent.at[place]))
            copies[-1].start()
    for copy in copies:
        copy.wait()


def per_device(concentration, velocity, potential):
    _, width, depth, span = concentration.shape
    stream = lax.axis_size("stream")
    wall = lax.axis_size("wall")
    stream_total = width * stream
    wall_total = depth * wall
    rates_x = (4.0 * width * width, float(stream_total * stream_total // 25))
    rates_z = (4.0 * depth * depth, float(wall_total * wall_total // 16))
    decays_x = [line_factors(rate)[0] for rate in rates_x]
    decays_z = [line_factors(rate)[0] for rate in rates_z]
    steps_x = [decay**width for decay in decays_x]
    collect_z, solve_z = wall_tables(rates_x, rates_z, width, depth)
    collect = collect_table(rates_x, rates_z, width, depth)
    near, home = home_tables(rates_x, rates_z, width, depth)

    (edge,) = call(
        border_kernel,
        [(4, depth, span)],
        (concentration, velocity, potential),
        [pltpu.SemaphoreType.DMA((4,))],
        source=pltpu.HBM,
        room=53 * 1024 + 848,
    )
    left_halo = lax.ppermute(edge, "stream", [(i, (i + 1) % stream) for i in range(stream)])

    members = TEAM * wall
    teams = stream // TEAM
    holders = [[t * TEAM + (m + t // (teams // 2) * (TEAM // 2)) % TEAM for m in range(TEAM)] for t in range(teams)]
    listed = [[b * stream + place for place in team for b in range(wall)] for team in holders]
    plane = [[team[k * SPREAD % members] for k in range(members)] for team in listed]
    ranks = [[team[m] for team in holders] for m in range(TEAM)]
    swap = functools.partial(lax.all_to_all, split_axis=0, concat_axis=0, tiled=True)
    table = functools.partial(jnp.array, dtype=jnp.float32)
    places = span // members
    tile = (members, places, LANES)
    flat = (2 * width * depth, span)
    near, rows = call(
        predict_kernel,
        [flat, (LANES, span)],
        (concentration, velocity, potential, table(np.concatenate([near, collect]))),
        [pltpu.VMEM(flat, jnp.float32)],
    )
    shares, gains, rows = call(
        functools.partial(enter_kernel, decays_x, decays_z),
        [tile, (2 * depth, span), (LANES, span)],
        (rows, left_halo, concentration, velocity, potential),
        aliases={0: 2},
    )
    parts = swap(shares, ("wall", "stream"), axis_index_groups=plane)
    pack = LANES // (4 * depth)
    ends, sums = call(
        functools.partial(wall_kernel, decays_z, steps_x, wall, width, depth),
        [tile, (teams, wall // pack, places, LANES)],
        (parts, table(collect_z), table(solve_z)),
        [pltpu.VMEM(tile, jnp.float32), pltpu.VMEM(tile, jnp.float32)],
    )
    sums = swap(sums, "stream", axis_index_groups=ranks)
    (links,) = call(
        functools.partial(stream_kernel, steps_x, wall, depth),
        [(members, places // HALVES, LANES)],
        (ends, sums),
    )
    links = swap(links, ("wall", "stream"), axis_index_groups=plane)
    (out,) = call(
        home_kernel,
        [concentration.shape],
        (near, gains, links.reshape(-1, LANES), table(home)),
        [
            pltpu.VMEM((span // LANES, 2, width, depth, LANES), jnp.float32),
            pltpu.SemaphoreType.DMA((span // LANES,)),
        ],
        target=pltpu.HBM,
    )
    return out


def solution(mesh):
    return jax.shard_map(
        per_device,
        mesh=mesh,
        in_specs=(
            P(None, "stream", "wall", None),
            P(None, "stream", "wall", None),
            P("stream", "wall", None),
        ),
        out_specs=P(None, "stream", "wall", None),
        check_vma=False,
    )
```
